128 devices in a mesh: dp: 8 (over z, y_hi), expert: 16 (over x, y_lo, core).
Axes of the slice: x: 4, y: 4 (y_hi: 2, y_lo: 2; y = y_hi * 2 + y_lo), z: 4, core: 2. Of those that a mesh axis runs over, the one named last changes fastest.
Arguments:
- tokens: bfloat16 [16384, 3072], P(('dp', 'expert')), may hold values from -64 to 64
- attn_param: bfloat16 [18432, 128], P('dp'), may hold values from -0.75 to 0.75
- expert_ids: int32 [16384, 1], P(('dp', 'expert')), may hold values from 0 to 15; in each aligned block of 128 rows (0 to 127, 128 to 255, ...) at most 10 rows name the same one
- gate_score: float32 [16384, 1], P(('dp', 'expert')), may hold values from 0.25 to 1
- w_in: bfloat16 [16, 3072, 2, 5376], P('expert', None, None, 'dp'), may hold values from -0.109375 to 0.109375
- w_out: bfloat16 [16, 5376, 3072], P('expert', 'dp'), may hold values from -0.078125 to 0.078125
- cotangent: bfloat16 [16384, 3072], P(('dp', 'expert')), may hold values from -24 to 24
Outputs:
- grad_tokens: bfloat16 [16384, 3072], P(('dp', 'expert'))
- attn_grad: float32 [18432, 128], P(('dp', 'expert'))
The draws below stay inside these ranges and needn't reach their ends.
Inputs may be any that keep to these rules, and one draw needn't show every extreme that they name: `expert_ids`: each row names 1 different experts. In the rows of one device no expert is named more than 10 times, and in every draw some device's rows name some expert exactly 10 times.
All inputs are finite; a program needn't handle non-finite values.
Results may differ from the reference program's by a relative error of at most 0.02.
Values may be sent and summed in bfloat16 or wider, within the bound.
No kernel may reach another device: no remote copies, remote signals or barrier semaphores. Data moves between devices by JAX's collectives and lax.ppermute only.
A program may use at most 128 MiB of HBM per device.

```python
import math
from functools import partial
import jax
import jax.numpy as jnp
import numpy as np
from jax import lax

D = 3072
HD = 128
QH = 2
FF = 5376
TOPK = 1
TOK_DEV = 128
EXPERTS = 16
CAP = 10
TOKENS = 16384
N_DP = 8
N_EXPERT = 16


def draw_tokens(key, part):
    key = jax.random.fold_in(key, 5)
    base_key, column_key = jax.random.split(key, 2)
    base = jnp.clip(jax.random.normal(base_key, (TOKENS, D), jnp.float32), -4.0, 4.0)
    columns = jnp.exp(jax.random.uniform(column_key, (1, D), jnp.float32, math.log(0.5), math.log(5.0)))
    values = base * columns
    return values.astype(jnp.bfloat16)


def draw_attn_param(key, part):
    key = jax.random.fold_in(key, 9)
    base_key = jax.random.fold_in(key, 0)
    rows = jnp.arange((2 * QH + 2) * D)
    base = jnp.clip(jax.random.normal(base_key, ((2 * QH + 2) * D, HD), jnp.float32), -4.0, 4.0)
    scale = jnp.where(rows < (QH + 2) * D, D ** (-0.5), (QH * HD) ** (-0.5)).astype(jnp.float32)[:, None]
    values = base * scale
    return values.astype(jnp.bfloat16)


def spiked(result, rng, source, target, parts, factor):
    owner, partner = [(jnp.arange(result.shape[axis_at]) // (result.shape[axis_at] // parts)).reshape([-1 if axis == axis_at else 1 for axis in range(result.ndim)]) for axis_at in (source, target)]
    chosen = jax.random.permutation(rng, parts)[partner]
    strong = (owner == chosen) | (owner == (partner + parts // 2) % parts)
    return jnp.where(strong, factor * result, result)


def levels(rng, dims, cuts, smallest, top_value):
    factor_of = 1.0
    for dim, parts in cuts:
        draws = jax.random.uniform(jax.random.fold_in(jax.random.fold_in(rng, 6), dim), (parts,), jnp.float32, smallest / len(cuts), top_value / len(cuts))
        factor_of = factor_of * jnp.repeat(jnp.exp(draws), dims[dim] // parts).reshape((-1,) + (1,) * (len(dims) - 1 - dim))
    return factor_of


def shared_out(rng, own, number, rows, amount, top, bound, skew):
    order = jax.random.permutation(rng, amount)
    heavy_load, ordinary = shares(amount, rows * top, bound, skew, True), shares(amount, rows * top, bound, skew, False)
    places = jnp.arange(amount)

    def named(tallies, rotation):
        used = int((tallies > 0).sum())
        fixed = max(1, used // 4)
        moved = fixed + (places - fixed + rotation * (used - fixed)) % max(1, amount - fixed)
        return jnp.zeros((amount,), jnp.int32).at[order[jnp.where(places < fixed, places, moved)]].set(jnp.asarray(tallies, jnp.int32))

    tallies = jnp.where(number % 4 == 0, named(heavy_load, number // 4), named(ordinary, number - number // 4 - 1))
    mixed = jax.random.permutation(jax.random.fold_in(own, 3), amount)
    giver, taker = mixed[0:amount // 2 * 2:2], mixed[1:amount // 2 * 2:2]
    margin = jnp.minimum(tallies[giver] - 1, bound - tallies[taker]) // 2
    margin = jnp.where((giver == order[0]) | (taker == order[0]) | (tallies[taker] == 0), 0, jnp.maximum(margin, 0))
    moved = jax.random.randint(jax.random.fold_in(own, 4), (amount // 2,), 0, 1 << 20) % (margin + 1)
    tallies = tallies.at[giver].add(-moved).at[taker].add(moved)
    members = jnp.searchsorted(jnp.cumsum(tallies), jnp.arange(rows * top), side="right").astype(jnp.int32)
    table = members.reshape(top, rows).T
    table = table[jax.random.permutation(jax.random.fold_in(own, 1), rows)]
    rotation = jax.random.randint(jax.random.fold_in(own, 2), (rows, 1), 0, top)
    return jnp.take_along_axis(table, (jnp.arange(top)[None, :] + rotation) % top, axis=1)


def shares(amount, total, most, skew, full):
    weights = [(1 << 20) // math.isqrt(grade ** skew) + 1 for grade in range(1, amount + 1)]
    largest = most if full else min(most, max(-(-total // amount), total * weights[0] // sum(weights)))
    least = 1 if total - largest >= amount - 1 else 0
    holding, surplus = [largest] + [least] * (amount - 1), total - largest - least * (amount - 1)
    while surplus > 0:
        free = [i for i in range(1, amount) if holding[i] < largest] or [i for i in range(1, amount) if holding[i] < most]
        whole, remaining = sum([weights[i] for i in free]), surplus
        for i in free:
            more = min(most - holding[i], max(1, remaining * weights[i] // whole), surplus)
            holding[i] = holding[i] + more
            surplus = surplus - more
    return np.array(holding)


def gaussian(own_key, extent, deviation, most, cuts=(), kind=jnp.bfloat16):
    gain = levels(own_key, extent, cuts, -0.22, 0.18) if cuts else 1.0
    values = jax.random.normal(own_key, extent, jnp.float32) * deviation * gain
    return jnp.minimum(jnp.maximum(values, -most), most).astype(kind)


def heavy_noise(rng, dims, deviation, limit, shards, heavy, held_as=jnp.bfloat16):
    values = deviation * jax.random.normal(rng, dims, jnp.float32)
    if shards:
        values = values * levels(rng, dims, shards, -0.22, 0.18)
    return jnp.clip(spiked(values, jax.random.fold_in(rng, 3), *heavy), -limit, limit).astype(held_as)


def setup_inputs(seed: int = 0) -> dict:
    splits = jax.random.split(jax.random.key(seed), 8)
    tokens = draw_tokens(jax.random.fold_in(splits[7], 71), 0)
    attn_param = draw_attn_param(jax.random.fold_in(splits[7], 71), 0)
    expert_ids_keys = jax.random.split(jax.random.fold_in(splits[2], 1), TOKENS // TOK_DEV)
    expert_ids_turns = jax.random.permutation(jax.random.fold_in(splits[2], 3), TOKENS // TOK_DEV)
    expert_ids = jax.vmap(lambda own, number: shared_out(jax.random.fold_in(splits[2], 2), own, number, TOK_DEV, EXPERTS, TOPK, CAP, 0))(expert_ids_keys, expert_ids_turns).reshape((TOKENS, TOPK))
    gate_score = jnp.clip(0.25 + 0.75 * jax.random.uniform(splits[3], (TOKENS, TOPK), jnp.float32) ** levels(splits[3], (TOKENS, TOPK), ((0, 128),), -0.2, 0.2), 0.25, 1.0)
    w_in = gaussian(splits[4], (EXPERTS, D, 2, FF), D ** -0.5, 0.109375, ((0, 16), (3, 8)))
    w_out = gaussian(splits[5], (EXPERTS, FF, D), FF ** -0.5, 0.078125, ((0, 16), (1, 8)))
    cotangent = heavy_noise(splits[6], (TOKENS, D), 1.0, 24.0, ((0, 128),), (0, 1, 128, 5.5))
    return dict(tokens=tokens, attn_param=attn_param, expert_ids=expert_ids, gate_score=gate_score, w_in=w_in, w_out=w_out, cotangent=cotangent)


EPSILON = 1e-05
MASKED = -1e+30
PRECISE = lax.Precision.HIGHEST

def layer_norm(values):
    widened = values.astype(jnp.float32)
    center = widened - lax.optimization_barrier(jnp.mean(widened, axis=-1, keepdims=True))
    inverse = lax.rsqrt(lax.optimization_barrier(jnp.mean(center * center, axis=-1, keepdims=True)) + EPSILON)
    return (center * inverse, inverse)

def norm_back(normed, inverse, upstream):
    mean_grad = lax.optimization_barrier(jnp.mean(upstream, axis=-1, keepdims=True))
    mean_proj = lax.optimization_barrier(jnp.mean(upstream * normed, axis=-1, keepdims=True))
    return inverse * (upstream - mean_grad - normed * mean_proj)

def slot_table(expert_ids, experts, capacity):
    flat_ids = expert_ids.reshape(-1).astype(jnp.int32)
    one_hot = (flat_ids[:, None] == jnp.arange(experts, dtype=jnp.int32)[None, :]).astype(jnp.int32)
    earlier = (jnp.cumsum(one_hot, axis=0) - one_hot).astype(jnp.int32)
    position = lax.optimization_barrier(jnp.sum(earlier * one_hot, axis=1)).astype(jnp.int32)
    target = (flat_ids * capacity + position).astype(jnp.int32)
    entries = flat_ids.shape[0]
    owners = jnp.zeros((experts * capacity,), jnp.int32).at[target].set(jnp.arange(entries, dtype=jnp.int32))
    filled = jnp.zeros((experts * capacity,), jnp.int32).at[target].set(jnp.ones((entries,), jnp.int32))
    return (owners, filled, target)

def reference(tokens, attn_param, expert_ids, gate_score, w_in, w_out, cotangent):
    sequences = N_DP * N_EXPERT
    score_scale = HD ** (-0.5)
    block_units = FF // N_DP
    blocks = QH + 2
    normed_one, inverse_one = layer_norm(tokens)
    normed_one_b = normed_one.astype(jnp.bfloat16)
    project = jnp.transpose(attn_param[:blocks * D].reshape(blocks, D, HD), (1, 0, 2)).reshape(D, blocks * HD)
    out_map = jnp.transpose(attn_param[blocks * D:].reshape(QH, D, HD), (1, 0, 2)).reshape(D, QH * HD)
    projected = jnp.dot(normed_one_b, project, preferred_element_type=jnp.float32).astype(jnp.bfloat16)
    projected = projected.reshape(sequences, TOK_DEV, blocks, HD)
    queries = projected[:, :, :QH].astype(jnp.float32)
    key_rows = projected[:, :, QH].astype(jnp.float32)
    value_rows = projected[:, :, QH + 1].astype(jnp.float32)
    scores = jnp.einsum('sqhc,skc->shqk', queries, key_rows, precision=PRECISE) * score_scale
    causal = jnp.arange(TOK_DEV)[:, None] >= jnp.arange(TOK_DEV)[None, :]
    scores = jnp.where(causal[None, None], scores, MASKED)
    row_max = lax.optimization_barrier(jnp.max(scores, axis=3, keepdims=True))
    raised = jnp.exp(scores - row_max)
    attention = raised / lax.optimization_barrier(jnp.sum(raised, axis=3, keepdims=True))
    attention_b = attention.astype(jnp.bfloat16)
    attention_f = attention_b.astype(jnp.float32)
    context = jnp.einsum('shqk,skc->sqhc', attention_f, value_rows, precision=PRECISE).astype(jnp.bfloat16)
    context = context.reshape(sequences * TOK_DEV, QH * HD)
    attn_out = jnp.dot(context, out_map.T, preferred_element_type=jnp.float32)
    residual = (tokens.astype(jnp.float32) + attn_out).astype(jnp.bfloat16)
    normed_two, inverse_two = layer_norm(residual)
    normed_two_b = normed_two.astype(jnp.bfloat16)
    weights = gate_score.astype(jnp.float32)
    owners, filled, target = jax.vmap(partial(slot_table, experts=EXPERTS, capacity=CAP))(expert_ids.reshape(sequences, TOK_DEV, TOPK))
    offsets = (jnp.arange(sequences, dtype=jnp.int32) * TOK_DEV)[:, None]
    slot_token = (offsets + owners // TOPK).astype(jnp.int32).reshape(sequences, EXPERTS, CAP)
    slot_pick = (offsets * TOPK + owners).astype(jnp.int32).reshape(sequences, EXPERTS, CAP)
    live_all = filled.reshape(sequences, EXPERTS, CAP)
    flat_weights = weights.reshape(-1)

    def one_expert(running, expert_no):
        rows_at = jnp.take(slot_token, expert_no, axis=1).reshape(-1)
        live_at = (jnp.take(live_all, expert_no, axis=1).reshape(-1) == 1)[:, None]
        weight_at = jnp.take(flat_weights, jnp.take(slot_pick, expert_no, axis=1).reshape(-1), axis=0)
        inputs = jnp.where(live_at, jnp.take(normed_two_b, rows_at, axis=0), jnp.zeros((), jnp.bfloat16))
        cot_rows = jnp.where(live_at, jnp.take(cotangent, rows_at, axis=0), jnp.zeros((), jnp.bfloat16))
        inner_weight = jnp.take(w_in, expert_no, axis=0)
        outer_weight = jnp.take(w_out, expert_no, axis=0)
        mixed_rows = jnp.dot(inputs, inner_weight.reshape(D, 2 * FF), preferred_element_type=jnp.float32)
        gate_part = mixed_rows[:, :FF]
        up_part = mixed_rows[:, FF:]
        squash = jax.nn.sigmoid(gate_part)
        grad_act = jnp.dot(cot_rows, outer_weight.T, preferred_element_type=jnp.float32)
        grad_mixed = jnp.concatenate([grad_act * up_part * squash * (1.0 + gate_part * (1.0 - squash)), grad_act * gate_part * squash], axis=1).astype(jnp.bfloat16)
        row_count = grad_mixed.shape[0]
        split_grad = grad_mixed.astype(jnp.float32).reshape(row_count, 2, N_DP, block_units)
        split_weight = inner_weight.astype(jnp.float32).reshape(D, 2, N_DP, block_units)
        pieces = jnp.einsum('rjbu,djbu->brd', split_grad, split_weight, precision=PRECISE)
        pieces = pieces.astype(jnp.bfloat16).astype(jnp.float32)
        returned = lax.optimization_barrier(jnp.sum(pieces, axis=0)).astype(jnp.bfloat16)
        contrib = jnp.where(live_at, weight_at[:, None] * returned.astype(jnp.float32), 0.0)
        return (running.at[rows_at].add(contrib), None)
    moe_grad, _ = lax.scan(one_expert, jnp.zeros((sequences * TOK_DEV, D), jnp.float32), jnp.arange(EXPERTS, dtype=jnp.int32))
    grad_hidden = cotangent.astype(jnp.float32) + norm_back(normed_two, inverse_two, moe_grad)
    grad_hidden_b = grad_hidden.astype(jnp.bfloat16)
    grad_context = jnp.dot(grad_hidden_b, out_map, preferred_element_type=jnp.float32)
    grad_context = grad_context.reshape(sequences, TOK_DEV, QH, HD)
    grad_attention = jnp.einsum('sqhc,skc->shqk', grad_context, value_rows, precision=PRECISE)
    grad_value = jnp.einsum('shqk,sqhc->skc', attention_f, grad_context, precision=PRECISE)
    grad_scores = attention * (grad_attention - lax.optimization_barrier(jnp.sum(grad_attention * attention, axis=3, keepdims=True))) * score_scale
    grad_query = jnp.einsum('shqk,skc->sqhc', grad_scores, key_rows, precision=PRECISE)
    grad_key = jnp.einsum('shqk,sqhc->skc', grad_scores, queries, precision=PRECISE)
    grad_qkv = jnp.concatenate([grad_query, grad_key[:, :, None], grad_value[:, :, None]], axis=2)
    grad_qkv = grad_qkv.astype(jnp.bfloat16).reshape(sequences * TOK_DEV, blocks * HD)
    grad_normed = jnp.dot(grad_qkv, project.T, preferred_element_type=jnp.float32)
    grad_tokens = (grad_hidden + norm_back(normed_one, inverse_one, grad_normed)).astype(jnp.bfloat16)
    grad_project = jnp.dot(normed_one_b.T, grad_qkv, preferred_element_type=jnp.float32)
    grad_project = jnp.transpose(grad_project.reshape(D, blocks, HD), (1, 0, 2)).reshape(blocks * D, HD)
    grad_out = jnp.dot(grad_hidden_b.T, context, preferred_element_type=jnp.float32)
    grad_out = jnp.transpose(grad_out.reshape(D, QH, HD), (1, 0, 2)).reshape(QH * D, HD)
    attn_grad = jnp.concatenate([grad_project, grad_out], axis=0) * TOKENS ** (-0.5)
    return (grad_tokens, attn_grad)
```

```python
import jax
import jax.numpy as jnp
from jax import lax
from jax.sharding import Mesh, PartitionSpec as P

EPSILON = 1e-05
MASKED = -1e30
AXES = ("z", "yh", "x", "yl", "c")
DP = ("z", "yh")
EX = ("x", "yl", "c")
SIZES = (4, 2, 4, 2, 2)
EXPERTS = 16
N_DP = 8
CAP = 10
HEADS = 2
F32 = jnp.float32
BF16 = jnp.bfloat16


def layer_norm(values):
    widened = values.astype(F32)
    center = widened - jnp.mean(widened, axis=-1, keepdims=True)
    inverse = lax.rsqrt(jnp.mean(center * center, axis=-1, keepdims=True) + EPSILON)
    return (center * inverse, inverse)


def norm_back(normed, inverse, upstream):
    mean_grad = jnp.mean(upstream, axis=-1, keepdims=True)
    mean_proj = jnp.mean(upstream * normed, axis=-1, keepdims=True)
    return inverse * (upstream - mean_grad - normed * mean_proj)


def contract(first_op, second_op, first_dim, second_dim):
    return lax.dot_general(
        first_op,
        second_op,
        (((first_dim,), (second_dim,)), ((), ())),
        preferred_element_type=F32,
    )


def swap(values, axis):
    return lax.ppermute(values, axis, [(0, 1), (1, 0)])


def slot_matrix(expert_ids, seq_len):
    flat = expert_ids.reshape(-1)
    one_hot = (flat[:, None] == jnp.arange(EXPERTS, dtype=jnp.int32)[None, :]).astype(F32)
    rows = jnp.arange(seq_len)
    earlier = (rows[:, None] > rows[None, :]).astype(F32)
    before = jnp.dot(earlier, one_hot, preferred_element_type=F32)
    position = jnp.sum(before * one_hot, axis=1).astype(jnp.int32)
    target = flat * CAP + position
    return (jnp.arange(EXPERTS * CAP, dtype=jnp.int32)[:, None] == target[None, :]).astype(BF16)


def gather_params(attn_param):
    rows, head_dim = attn_param.shape
    half = rows // 2
    core = lax.axis_index("c")
    own = lax.dynamic_slice_in_dim(attn_param, core * half, half, 0)
    own = lax.all_to_all(
        jnp.broadcast_to(own[None], (N_DP, half, head_dim)), DP, split_axis=0, concat_axis=0, tiled=True
    )
    other = swap(own, "c")
    first = jnp.where(core == 0, own, other)
    second = jnp.where(core == 0, other, own)
    return jnp.stack([first, second], axis=1).reshape(N_DP * rows, head_dim)


def to_experts(buffer):
    features = buffer.shape[1]
    moved = lax.all_to_all(
        buffer.reshape(EXPERTS, CAP, features), EX, split_axis=0, concat_axis=0, tiled=True
    )
    return moved.reshape(EXPERTS * CAP, features)


def add_round(first, second):
    return (first.astype(F32) + second.astype(F32)).astype(BF16)


def scatter_grads(terms):
    head_dim = terms.shape[1]
    core = lax.axis_index("c")
    split = terms.astype(BF16).reshape(*SIZES, -1, head_dim)
    split = jnp.transpose(split, (4, 2, 3, 0, 1, 5, 6))
    split = split.reshape(2, 4, 2, N_DP, -1, head_dim)
    mine = lax.dynamic_index_in_dim(split, core, 0, keepdims=False)
    theirs = lax.dynamic_index_in_dim(split, 1 - core, 0, keepdims=False)
    summed = add_round(mine, swap(theirs, "c"))
    summed = summed.reshape(8, -1, head_dim)
    parts = lax.all_to_all(summed, ("x", "yl"), split_axis=0, concat_axis=0, tiled=True)
    summed = jnp.sum(parts.astype(F32), axis=0).astype(BF16).reshape(N_DP, -1, head_dim)
    parts = lax.all_to_all(summed, DP, split_axis=0, concat_axis=0, tiled=True)
    return jnp.sum(parts.astype(F32), axis=0)


def per_device(tokens, attn_param, expert_ids, gate_score, w_in, w_out, cotangent):
    seq_len, features = tokens.shape
    head_dim = attn_param.shape[1]
    hidden = w_out.shape[1]
    score_scale = head_dim ** (-0.5)
    devices = N_DP * EXPERTS
    slots = slot_matrix(expert_ids, seq_len)
    inner = jnp.transpose(w_in[0], (1, 2, 0))
    gate_map, up_map = inner[0], inner[1]
    outer = w_out[0]

    packed = gather_params(attn_param)
    cot_rows = to_experts(contract(slots, cotangent, 1, 0).astype(BF16))
    all_cot = lax.all_gather(cot_rows, DP, axis=0, tiled=True)

    normed_one, inverse_one = layer_norm(tokens)
    normed_one_b = normed_one.astype(BF16)
    blocks = packed.reshape(2 * HEADS + 2, features, head_dim)
    project = blocks[: HEADS + 2]
    out_blocks = blocks[HEADS + 2 :]
    projected = jnp.einsum(
        "td,jdc->tjc", normed_one_b, project, preferred_element_type=F32
    ).astype(BF16)
    queries = projected[:, :HEADS]
    key_rows = projected[:, HEADS]
    value_rows = projected[:, HEADS + 1]
    scores = jnp.einsum("qhc,kc->hqk", queries, key_rows, preferred_element_type=F32) * score_scale
    causal = lax.broadcasted_iota(jnp.int32, (seq_len, seq_len), 0) >= lax.broadcasted_iota(
        jnp.int32, (seq_len, seq_len), 1
    )
    scores = jnp.where(causal[None], scores, MASKED)
    row_max = jnp.max(scores, axis=2, keepdims=True)
    raised = jnp.exp(scores - row_max)
    attention = raised / jnp.sum(raised, axis=2, keepdims=True)
    attention_b = attention.astype(BF16)
    context = jnp.einsum(
        "hqk,kc->qhc", attention_b, value_rows, preferred_element_type=F32
    ).astype(BF16)
    attn_out = jnp.einsum("thc,hdc->td", context, out_blocks, preferred_element_type=F32)
    residual = (tokens.astype(F32) + attn_out).astype(BF16)
    normed_two, inverse_two = layer_norm(residual)
    normed_rows = to_experts(contract(slots, normed_two.astype(BF16), 1, 0).astype(BF16))
    all_normed = lax.all_gather(normed_rows, DP, axis=0, tiled=True)

    grad_act = contract(all_cot, outer, 1, 1)
    gate_part = contract(all_normed, gate_map, 1, 1)
    up_part = contract(all_normed, up_map, 1, 1)
    squash = jax.nn.sigmoid(gate_part)
    grad_gate = (grad_act * up_part * squash * (1.0 + gate_part * (1.0 - squash))).astype(BF16)
    grad_up = (grad_act * gate_part * squash).astype(BF16)
    partial_rows = (contract(grad_gate, gate_map, 1, 0) + contract(grad_up, up_map, 1, 0)).astype(BF16)
    summed = lax.psum_scatter(partial_rows, DP, scatter_dimension=0, tiled=True)
    arrived = to_experts(summed)
    back_rows = contract(slots, arrived, 0, 0)
    moe_grad = gate_score * back_rows
    grad_hidden = cotangent.astype(F32) + norm_back(normed_two, inverse_two, moe_grad)
    grad_hidden_b = grad_hidden.astype(BF16)
    grad_context = jnp.einsum(
        "td,hdc->thc", grad_hidden_b, out_blocks, preferred_element_type=F32
    )
    grad_context_b = grad_context.astype(BF16)
    grad_attention = jnp.einsum(
        "qhc,kc->hqk", grad_context_b, value_rows, preferred_element_type=F32
    )
    grad_value = jnp.einsum("hqk,qhc->kc", attention_b, grad_context_b, preferred_element_type=F32)
    grad_scores = (
        attention
        * (grad_attention - jnp.sum(grad_attention * attention, axis=2, keepdims=True))
        * score_scale
    )
    grad_scores_b = grad_scores.astype(BF16)
    grad_query = jnp.einsum("hqk,kc->qhc", grad_scores_b, key_rows, preferred_element_type=F32)
    grad_key = jnp.einsum("hqk,qhc->kc", grad_scores_b, queries, preferred_element_type=F32)
    grad_qkv = jnp.concatenate([grad_query, grad_key[:, None], grad_value[:, None]], axis=1).astype(BF16)
    grad_project = jnp.einsum("td,tjc->jdc", normed_one_b, grad_qkv, preferred_element_type=F32)
    grad_out = jnp.einsum("td,thc->hdc", grad_hidden_b, context, preferred_element_type=F32)
    grad_term = jnp.concatenate(
        [grad_project.reshape(-1, head_dim), grad_out.reshape(-1, head_dim)], axis=0
    )
    attn_grad = scatter_grads(grad_term * (seq_len * devices) ** (-0.5))
    grad_normed = jnp.einsum("tjc,jdc->td", grad_qkv, project, preferred_element_type=F32)
    grad_tokens = (grad_hidden + norm_back(normed_one, inverse_one, grad_normed)).astype(BF16)
    return (grad_tokens, attn_grad)


def solution(mesh):
    fine = Mesh(mesh.devices.reshape(SIZES), AXES)
    rows = P(AXES, None)
    in_specs = (
        rows,
        P(DP, None),
        rows,
        rows,
        P(EX, None, None, DP),
        P(EX, DP, None),
        rows,
    )
    return jax.shard_map(
        per_device, mesh=fine, in_specs=in_specs, out_specs=(rows, rows), check_vma=False
    )
```

```python
import jax
import jax.numpy as jnp
from jax import lax
from jax.experimental import pallas as pl
from jax.experimental.pallas import tpu as pltpu
from jax.sharding import Mesh, PartitionSpec as P

EPSILON = 1e-05
MASKED = -1e30
AXES = ("z", "yh", "x", "yl", "c")
DP = ("z", "yh")
EX = ("x", "yl", "c")
CHIPS = ("z", "yh", "x", "yl")
SIZES = (4, 2, 4, 2, 2)
EXPERTS = 16
N_DP = 8
CAP = 10
MAIN = 8
HEADS = 2
HALF = 80
PADDED = 768
F32 = jnp.float32
BF16 = jnp.bfloat16


def layer_norm(values):
    widened = values.astype(F32)
    center = widened - jnp.mean(widened, axis=-1, keepdims=True)
    inverse = lax.rsqrt(jnp.mean(center * center, axis=-1, keepdims=True) + EPSILON)
    return (center * inverse, inverse)


def norm_back(normed, inverse, upstream):
    mean_grad = jnp.mean(upstream, axis=-1, keepdims=True)
    mean_proj = jnp.mean(upstream * normed, axis=-1, keepdims=True)
    return inverse * (upstream - mean_grad - normed * mean_proj)


def contract(first_op, second_op, first_dim, second_dim):
    return lax.dot_general(
        first_op,
        second_op,
        (((first_dim,), (second_dim,)), ((), ())),
        preferred_element_type=F32,
    )


def swap(values, axis):
    return lax.ppermute(values, axis, [(0, 1), (1, 0)])


def along_z(values, shift):
    return lax.ppermute(values, "z", [(i, (i + shift) % 4) for i in range(4)])


def exchange(blocks, axes):
    return lax.all_to_all(blocks, axes, split_axis=0, concat_axis=0, tiled=True)


def after(value, *earlier):
    return lax.optimization_barrier((value,) + earlier)[0]


def add_round(first, *others):
    total = first.astype(F32)
    for other in others:
        total = total + other.astype(F32)
    return total.astype(BF16)


def slot_matrix(expert_ids, seq_len):
    flat = expert_ids.reshape(-1)
    one_hot = (flat[:, None] == jnp.arange(EXPERTS, dtype=jnp.int32)[None, :]).astype(F32)
    rows = jnp.arange(seq_len)
    earlier = (rows[:, None] > rows[None, :]).astype(F32)
    before = jnp.dot(earlier, one_hot, preferred_element_type=F32)
    position = jnp.sum(before * one_hot, axis=1).astype(jnp.int32)
    rest = CAP - MAIN
    target = jnp.where(
        position < MAIN, flat * MAIN + position, EXPERTS * MAIN + flat * rest + position - MAIN
    )
    return (jnp.arange(EXPERTS * CAP, dtype=jnp.int32)[:, None] == target[None, :]).astype(BF16)


def gather_params(attn_param):
    rows, head_dim = attn_param.shape
    half = rows // 2
    core = lax.axis_index("c")
    own = lax.dynamic_slice_in_dim(attn_param, core * half, half, 0)
    own = exchange(jnp.broadcast_to(own[None], (N_DP, half, head_dim)), DP)
    other = swap(own, "c")
    first = jnp.where(core == 0, own, other)
    second = jnp.where(core == 0, other, own)
    return jnp.stack([first, second], axis=1).reshape(N_DP * rows, head_dim)


def between_experts(rows):
    features = rows.shape[1]
    cut = EXPERTS * MAIN
    extra = rows[cut:].reshape(cut, -1)
    packed = jnp.concatenate([rows[:cut], extra], axis=1)
    width = packed.shape[1]
    packed = exchange(packed.reshape(EXPERTS, MAIN, width), EX).reshape(cut, width)
    extra = packed[:, features:].reshape(-1, features)
    return packed[:, :features], extra


def spread(main, extra):
    one = main[:HALF]
    two = jnp.concatenate([main[HALF:], extra], axis=0)
    one_z = {0: one, 1: along_z(one, 1), 3: along_z(one, -1), 2: along_z(one, 2)}
    two_y = swap(two, "yh")
    one_y = {0: swap(one, "yh")}
    for s in (1, 3, 2):
        one_y[s] = swap(one_z[s], "yh")
    late, late_y = after(two, one_z[1], one_z[3]), after(two_y, one_z[1], one_z[3])
    two_z, two_yz = {0: two}, {0: two_y}
    for s in (1, 3, 2):
        two_z[s] = along_z(late, s)
    for s in (1, 3, 2):
        two_yz[s] = along_z(late_y, s)
    return (one_z, one_y), (two_z, two_yz)


def collect(first, second):
    early = [along_z(first[0][s], -s) for s in (1, 3, 2)]
    early_y = swap(second[1][0], "yh")
    late = [along_z(first[1][s], -s) for s in (1, 3, 2)]
    swapped = {s: swap(second[1][s], "yh") for s in (1, 3, 2)}
    far = add_round(first[1][0], *late)
    far = swap(far, "yh")
    back = [along_z(add_round(second[0][s], swapped[s]), -s) for s in (1, 3, 2)]
    one = add_round(first[0][0], far, *early)
    two = add_round(second[0][0], early_y, *back)
    return one, two


def expert_kernel(count, rows, tall, *refs):
    normed_refs, cot_refs = refs[:count], refs[count : 2 * count]
    inner_ref, outer_ref = refs[2 * count : 2 * count + 2]
    out_refs = refs[2 * count + 2 : 3 * count + 2]
    (normed, cot, gate_map, up_map, outer_map, grad_gate, grad_up, result, row_sem, map_sem, out_sem) = refs[
        3 * count + 2 :
    ]
    hidden, features = outer_ref.shape

    def load(source, target, sem):
        copy = pltpu.make_async_copy(source, target, sem)
        copy.start()
        return copy

    pieces = [(0, 256), (256, 256), (512, hidden - 512)]
    rows_in = [load(ref, normed.at[pl.ds(i * rows, rows)], row_sem.at[0, i]) for i, ref in enumerate(normed_refs)]
    maps_in = []
    for i, (start, size) in enumerate(pieces):
        at = pl.ds(start, size)
        maps_in.append(
            [
                load(inner_ref.at[0, at], gate_map.at[at], map_sem.at[0, i]),
                load(inner_ref.at[1, at], up_map.at[at], map_sem.at[1, i]),
                load(outer_ref.at[at], outer_map.at[at], map_sem.at[2, i]),
            ]
        )
        if i == 0:
            rows_in += [
                load(ref, cot.at[pl.ds(j * rows, rows)], row_sem.at[1, j]) for j, ref in enumerate(cot_refs)
            ]
    blank = jnp.zeros((PADDED - hidden, features), BF16)
    for ref in (gate_map, up_map, outer_map):
        ref[pl.ds(hidden, PADDED - hidden)] = blank
    for copy in rows_in:
        copy.wait()
    steps = count * rows // tall

    for i in range(len(pieces)):
        for copy in maps_in[i]:
            copy.wait()
        at = pl.ds(i * 256, 256)

        @pl.loop(0, steps)
        def _(step):
            here = pl.ds(pl.multiple_of(step * tall, 16), tall)
            gate_part = contract(normed[here], gate_map[at], 1, 1)
            up_part = contract(normed[here], up_map[at], 1, 1)
            grad_act = contract(cot[here], outer_map[at], 1, 1)
            squash = 1.0 / (1.0 + jnp.exp(-gate_part))
            scaled = grad_act * squash
            grad_gate[here, at] = (scaled * up_part * (1.0 + gate_part * (1.0 - squash))).astype(BF16)
            grad_up[here, at] = (scaled * gate_part).astype(BF16)

    wide = 512
    copies = []
    for n in range(features // wide):
        lanes = pl.ds(n * wide, wide)

        @pl.loop(0, steps)
        def _(step):
            here = pl.ds(pl.multiple_of(step * tall, 16), tall)
            result[here, lanes] = (
                contract(grad_gate[here], gate_map[:, lanes], 1, 0)
                + contract(grad_up[here], up_map[:, lanes], 1, 0)
            ).astype(BF16)

        copies += [
            load(result.at[pl.ds(i * rows, rows), lanes], ref.at[:, lanes], out_sem.at[n, i])
            for i, ref in enumerate(out_refs)
        ]
    for copy in copies:
        copy.wait()


def experts(normed_blocks, cot_blocks, inner, outer, tall):
    count = len(normed_blocks)
    rows, features = normed_blocks[0].shape
    hidden = outer.shape[0]
    total = count * rows
    anywhere = pl.BlockSpec(memory_space=pl.ANY)
    return pl.pallas_call(
        lambda *refs: expert_kernel(count, rows, tall, *refs),
        out_shape=[jax.ShapeDtypeStruct((rows, features), BF16)] * count,
        in_specs=[anywhere] * (2 * count + 2),
        out_specs=[anywhere] * count,
        scratch_shapes=[
            pltpu.VMEM((total, features), BF16),
            pltpu.VMEM((total, features), BF16),
            pltpu.VMEM((PADDED, features), BF16),
            pltpu.VMEM((PADDED, features), BF16),
            pltpu.VMEM((PADDED, features), BF16),
            pltpu.VMEM((total, PADDED), BF16),
            pltpu.VMEM((total, PADDED), BF16),
            pltpu.VMEM((total, features), BF16),
            pltpu.SemaphoreType.DMA((2, count)),
            pltpu.SemaphoreType.DMA((3, 3)),
            pltpu.SemaphoreType.DMA((features // 512, count)),
        ],
        compiler_params=pltpu.CompilerParams(vmem_limit_bytes=48 * 1024 * 1024),
        cost_estimate=pl.CostEstimate(
            flops=10 * total * features * hidden,
            bytes_accessed=6 * total * features + 6 * hidden * features,
            transcendentals=total * hidden,
        ),
    )(*normed_blocks, *cot_blocks, inner, outer)


def param_kernel(scale, head_dim, core_ref, normed_ref, hidden_ref, grads_ref, context_ref, out_ref, terms):
    features = normed_ref.shape[1]
    tile = 1024
    for block in range(6):
        left_ref = normed_ref if block < 4 else hidden_ref
        right = (grads_ref[:, block * head_dim : (block + 1) * head_dim] if block < 4
                 else context_ref[:, (block - 4) * head_dim : (block - 3) * head_dim])
        for start in range(0, features, tile):
            part = contract(left_ref[:, start : start + tile], right, 0, 0) * scale
            terms[pl.ds(block * features + start, tile)] = part.astype(BF16)
    core = core_ref[0]

    @pl.loop(0, out_ref.shape[0])
    def _(group):
        size = out_ref.shape[1]
        out_ref[group] = terms[pl.ds(pl.multiple_of((2 * group + core) * size, 16), size)]


def param_terms(core, normed, hidden, grads, context, scale, head_dim):
    features = normed.shape[1]
    rows = 6 * features
    whole = pl.BlockSpec(memory_space=pltpu.VMEM)
    return pl.pallas_call(
        lambda *refs: param_kernel(scale, head_dim, *refs),
        out_shape=jax.ShapeDtypeStruct((64, rows // 128, head_dim), BF16),
        in_specs=[pl.BlockSpec(memory_space=pltpu.SMEM)] + [whole] * 4,
        out_specs=whole,
        scratch_shapes=[pltpu.VMEM((rows, head_dim), BF16)],
        compiler_params=pltpu.CompilerParams(vmem_limit_bytes=40 * 1024 * 1024),
        cost_estimate=pl.CostEstimate(
            flops=2 * rows * head_dim * normed.shape[0], bytes_accessed=8 * 1024 * 1024, transcendentals=0
        ),
    )(core, normed, hidden, grads, context)


def per_device(tokens, attn_param, expert_ids, gate_score, w_in, w_out, cotangent):
    seq_len, features = tokens.shape
    head_dim = attn_param.shape[1]
    score_scale = head_dim ** (-0.5)
    devices = N_DP * EXPERTS
    slots = slot_matrix(expert_ids, seq_len)
    inner = jnp.transpose(w_in[0], (1, 2, 0))
    outer = w_out[0]

    packed = gather_params(attn_param)
    cot_main, cot_extra = between_experts(contract(slots, cotangent, 1, 0).astype(BF16))
    cot_one, cot_two = spread(cot_main, cot_extra)

    normed_one, inverse_one = layer_norm(tokens)
    normed_one_b = normed_one.astype(BF16)
    normed_both = jnp.concatenate([normed_one_b, swap(normed_one_b, "c")], axis=0)
    blocks = packed.reshape(2 * HEADS + 2, features, head_dim)
    project = blocks[: HEADS + 2]
    out_blocks = blocks[HEADS + 2 :]
    projected = jnp.einsum(
        "td,jdc->tjc", normed_one_b, project, preferred_element_type=F32
    ).astype(BF16)
    queries = projected[:, :HEADS]
    key_rows = projected[:, HEADS]
    value_rows = projected[:, HEADS + 1]
    scores = jnp.einsum("qhc,kc->hqk", queries, key_rows, preferred_element_type=F32) * score_scale
    causal = lax.broadcasted_iota(jnp.int32, (seq_len, seq_len), 0) >= lax.broadcasted_iota(
        jnp.int32, (seq_len, seq_len), 1
    )
    scores = jnp.where(causal[None], scores, MASKED)
    row_max = jnp.max(scores, axis=2, keepdims=True)
    raised = jnp.exp(scores - row_max)
    attention = raised / jnp.sum(raised, axis=2, keepdims=True)
    attention_b = attention.astype(BF16)
    context = jnp.einsum(
        "hqk,kc->qhc", attention_b, value_rows, preferred_element_type=F32
    ).astype(BF16)
    context_flat = context.reshape(seq_len, HEADS * head_dim)
    context_both = jnp.concatenate([context_flat, swap(context_flat, "c")], axis=0)
    attn_out = jnp.einsum("thc,hdc->td", context, out_blocks, preferred_element_type=F32)
    residual = (tokens.astype(F32) + attn_out).astype(BF16)
    normed_two, inverse_two = layer_norm(residual)
    main, extra = between_experts(contract(slots, normed_two.astype(BF16), 1, 0).astype(BF16))
    one, two = spread(main, extra)

    def near(first, second):
        return [first[0][s] for s in range(4)] + [second[0][0], second[1][0]]

    def far(first, second):
        return (
            [first[1][s] for s in range(4)]
            + [second[0][s] for s in (1, 2, 3)]
            + [second[1][s] for s in (1, 2, 3)]
        )

    near_rows = experts(near(one, two), near(cot_one, cot_two), inner, outer, 240)
    far_rows = experts(far(one, two), far(cot_one, cot_two), inner, outer, 400)
    back_one = (dict(enumerate(near_rows[:4])), dict(enumerate(far_rows[:4])))
    back_two = (
        {0: near_rows[4], 1: far_rows[4], 2: far_rows[5], 3: far_rows[6]},
        {0: near_rows[5], 1: far_rows[7], 2: far_rows[8], 3: far_rows[9]},
    )
    sum_one, sum_two = collect(back_one, back_two)
    back_main, back_extra = between_experts(jnp.concatenate([sum_one, sum_two], axis=0))
    cut = EXPERTS * MAIN
    back_rows = contract(slots[:cut], back_main, 0, 0) + contract(slots[cut:], back_extra, 0, 0)
    moe_grad = gate_score * back_rows
    grad_hidden = cotangent.astype(F32) + norm_back(normed_two, inverse_two, moe_grad)
    grad_hidden_b = grad_hidden.astype(BF16)
    hidden_both = jnp.concatenate([grad_hidden_b, swap(grad_hidden_b, "c")], axis=0)
    grad_context = jnp.einsum(
        "td,hdc->thc", grad_hidden_b, out_blocks, preferred_element_type=F32
    )
    grad_context_b = grad_context.astype(BF16)
    grad_attention = jnp.einsum(
        "qhc,kc->hqk", grad_context_b, value_rows, preferred_element_type=F32
    )
    grad_value = jnp.einsum("hqk,qhc->kc", attention_b, grad_context_b, preferred_element_type=F32)
    grad_scores = (
        attention
        * (grad_attention - jnp.sum(grad_attention * attention, axis=2, keepdims=True))
        * score_scale
    )
    grad_scores_b = grad_scores.astype(BF16)
    grad_query = jnp.einsum("hqk,kc->qhc", grad_scores_b, key_rows, preferred_element_type=F32)
    grad_key = jnp.einsum("hqk,qhc->kc", grad_scores_b, queries, preferred_element_type=F32)
    grad_qkv = jnp.concatenate([grad_query, grad_key[:, None], grad_value[:, None]], axis=1).astype(BF16)
    grads_flat = grad_qkv.reshape(seq_len, (HEADS + 2) * head_dim)
    grads_both = jnp.concatenate([grads_flat, swap(grads_flat, "c")], axis=0)
    core = lax.axis_index("c").astype(jnp.int32).reshape(1)
    terms = param_terms(
        core, normed_both, hidden_both, grads_both, context_both, (seq_len * devices) ** (-0.5), head_dim
    )
    attn_grad = jnp.sum(exchange(terms, CHIPS).astype(F32), axis=0)
    grad_normed = jnp.einsum("tjc,jdc->td", grad_qkv, project, preferred_element_type=F32)
    grad_tokens = (grad_hidden + norm_back(normed_one, inverse_one, grad_normed)).astype(BF16)
    return (grad_tokens, attn_grad)


def solution(mesh):
    fine = Mesh(mesh.devices.reshape(SIZES), AXES)
    rows = P(AXES, None)
    in_specs = (
        rows,
        P(DP, None),
        rows,
        rows,
        P(EX, None, None, DP),
        P(EX, DP, None),
        rows,
    )
    return jax.shard_map(
        per_device, mesh=fine, in_specs=in_specs, out_specs=(rows, rows), check_vma=False
    )
```

```python
import jax
import jax.numpy as jnp
from jax import lax
from jax.experimental import pallas as pl
from jax.experimental.pallas import tpu as pltpu
from jax.sharding import Mesh, PartitionSpec as P

EPSILON = 1e-05
MASKED = -1e30
AXES = ("z", "yh", "x", "yl", "c")
DP = ("z", "yh")
EX = ("x", "yl", "c")
CHIPS = ("z", "yh", "x", "yl")
SIZES = (4, 2, 4, 2, 2)
EXPERTS = 16
N_DP = 8
CAP = 10
MAIN = 8
HEADS = 2
HALF = 80
PADDED = 768
F32 = jnp.float32
BF16 = jnp.bfloat16


def layer_norm(values):
    widened = values.astype(F32)
    center = widened - jnp.mean(widened, axis=-1, keepdims=True)
    inverse = lax.rsqrt(jnp.mean(center * center, axis=-1, keepdims=True) + EPSILON)
    return (center * inverse, inverse)


def norm_back(normed, inverse, upstream):
    mean_grad = jnp.mean(upstream, axis=-1, keepdims=True)
    mean_proj = jnp.mean(upstream * normed, axis=-1, keepdims=True)
    return inverse * (upstream - mean_grad - normed * mean_proj)


def contract(first_op, second_op, first_dim, second_dim):
    return lax.dot_general(
        first_op,
        second_op,
        (((first_dim,), (second_dim,)), ((), ())),
        preferred_element_type=F32,
    )


def swap(values, axis):
    return lax.ppermute(values, axis, [(0, 1), (1, 0)])


def along_z(values, shift):
    return lax.ppermute(values, "z", [(i, (i + shift) % 4) for i in range(4)])


def exchange(blocks, axes):
    return lax.all_to_all(blocks, axes, split_axis=0, concat_axis=0, tiled=True)


def after(value, *earlier):
    return lax.optimization_barrier((value,) + earlier)[0]


def add_round(first, *others):
    total = first.astype(F32)
    for other in others:
        total = total + other.astype(F32)
    return total.astype(BF16)


def slot_matrix(expert_ids, seq_len):
    flat = expert_ids.reshape(-1)
    one_hot = (flat[:, None] == jnp.arange(EXPERTS, dtype=jnp.int32)[None, :]).astype(F32)
    rows = jnp.arange(seq_len)
    earlier = (rows[:, None] > rows[None, :]).astype(F32)
    before = jnp.dot(earlier, one_hot, preferred_element_type=F32)
    position = jnp.sum(before * one_hot, axis=1).astype(jnp.int32)
    rest = CAP - MAIN
    target = jnp.where(
        position < MAIN, flat * MAIN + position, EXPERTS * MAIN + flat * rest + position - MAIN
    )
    return (jnp.arange(EXPERTS * CAP, dtype=jnp.int32)[:, None] == target[None, :]).astype(BF16)


def place_kernel(places, piece, at_ref, *refs):
    block_refs, out_ref, sems = refs[: len(places)], refs[-2], refs[-1]
    copies = []
    number = 0
    for ref, parts in zip(block_refs, places):
        for i, (s, r, half) in enumerate(parts):
            z = lax.rem(at_ref[0] - s + 4, 4)
            yh = lax.rem(at_ref[1] + r, 2)
            copy = pltpu.make_async_copy(
                ref.at[pl.ds(i * piece, piece)], out_ref.at[z * 2 + yh, pl.ds(half * piece, piece)], sems.at[number]
            )
            copy.start()
            copies.append(copy)
            number += 1
    for copy in copies:
        copy.wait()


def gather_params(attn_param, earlier):
    rows, head_dim = attn_param.shape
    half = rows // 2
    piece = half // 2
    core = lax.axis_index("c")
    own = lax.dynamic_slice_in_dim(attn_param, core * half, half, 0)
    first, second = own[:piece], own[piece:]
    around = [along_z(first, s) for s in (1, 3, 2)]
    own_y = swap(own, "yh")
    pair = after(jnp.concatenate([second, own_y[piece:]], axis=0), around[0], around[1])
    around_y = [swap(block, "yh") for block in around]
    pairs = [along_z(pair, s) for s in (1, 3, 2)]
    blocks = [own, own_y] + around + around_y + pairs
    places = (
        [[(0, 0, 0), (0, 0, 1)], [(0, 1, 0), (0, 1, 1)]]
        + [[(s, 0, 0)] for s in (1, 3, 2)]
        + [[(s, 1, 0)] for s in (1, 3, 2)]
        + [[(s, 0, 1), (s, 1, 1)] for s in (1, 3, 2)]
    )
    at = after(jnp.stack([lax.axis_index("z"), lax.axis_index("yh")]).astype(jnp.int32), earlier)
    anywhere = pl.BlockSpec(memory_space=pl.ANY)
    own = pl.pallas_call(
        lambda *refs: place_kernel(places, piece, *refs),
        out_shape=jax.ShapeDtypeStruct((N_DP, half, head_dim), BF16),
        in_specs=[pl.BlockSpec(memory_space=pltpu.SMEM)] + [anywhere] * len(blocks),
        out_specs=anywhere,
        scratch_shapes=[pltpu.SemaphoreType.DMA((16,))],
    )(at, *blocks)
    other = swap(own, "c")
    first = jnp.where(core == 0, own, other)
    second = jnp.where(core == 0, other, own)
    return jnp.stack([first, second], axis=1).reshape(N_DP * rows, head_dim)


def between_experts(rows):
    features = rows.shape[1]
    cut = EXPERTS * MAIN
    extra = rows[cut:].reshape(cut, -1)
    packed = jnp.concatenate([rows[:cut], extra], axis=1)
    width = packed.shape[1]
    packed = exchange(packed.reshape(EXPERTS, MAIN, width), EX).reshape(cut, width)
    extra = packed[:, features:].reshape(-1, features)
    return packed[:, :features], extra


def spread_near(own):
    one = own[:HALF]
    own_y = swap(own, "yh")
    return [own, own_y] + [along_z(one, s) for s in (1, 3, 2)]


def spread_far(near, between):
    own, own_y, near_z, far_z, across = near
    pair = after(jnp.concatenate([own[HALF:], own_y[HALF:]], axis=0), near_z, far_z)
    first = [swap(near_z, "yh"), swap(far_z, "yh")]
    second = [along_z(pair, 1), along_z(pair, 3)]
    return first + [swap(after(across, *between), "yh")] + second + [along_z(pair, 2)]


def collect(near, far):
    kept, one_y, two_y, *one_z = near
    early = [along_z(block, -s) for block, s in zip(one_z, (1, 3, 2))]
    early_y = swap(two_y, "yh")
    *one_yz, two_z, two_yz = far
    (*one_yz, two_yz), early, early_y = lax.optimization_barrier(([*one_yz, two_yz], early, early_y))
    late = [along_z(block, -s) for block, s in zip(one_yz, (1, 3, 2))]
    swapped = swap(two_yz, "yh")
    across = swap(add_round(one_y, *late), "yh")
    pairs = add_round(two_z, swapped)
    back = [along_z(pairs[i * HALF : (i + 1) * HALF], -s) for i, s in enumerate((1, 3, 2))]
    one = add_round(kept[:HALF], across, *early)
    two = add_round(kept[HALF:], early_y, *back)
    return jnp.concatenate([one, two], axis=0)


def expert_kernel(counts, pieces_out, tall, *refs):
    count = len(counts)
    outs = len(pieces_out)
    normed_refs, cot_refs = refs[:count], refs[count : 2 * count]
    inner_ref, outer_ref = refs[2 * count : 2 * count + 2]
    out_refs = refs[2 * count + 2 : 2 * count + 2 + outs]
    (normed, cot, gate_map, up_map, outer_map, grad_gate, grad_up, result, row_sem, map_sem, out_sem) = refs[
        2 * count + 2 + outs :
    ]
    hidden, features = outer_ref.shape
    starts = [sum(counts[:i]) for i in range(count)]

    def load(source, target, sem):
        copy = pltpu.make_async_copy(source, target, sem)
        copy.start()
        return copy

    def load_rows(block_refs, target, side):
        return [
            load(ref, target.at[pl.ds(starts[i], counts[i])], row_sem.at[side, i])
            for i, ref in enumerate(block_refs)
        ]

    pieces = [(0, 256), (256, 256), (512, hidden - 512)]
    rows_in = load_rows(normed_refs, normed, 0)
    maps_in = []
    for i, (start, size) in enumerate(pieces):
        at = pl.ds(start, size)
        maps_in.append(
            [
                load(inner_ref.at[0, at], gate_map.at[at], map_sem.at[0, i]),
                load(inner_ref.at[1, at], up_map.at[at], map_sem.at[1, i]),
                load(outer_ref.at[at], outer_map.at[at], map_sem.at[2, i]),
            ]
        )
        if i == 0:
            rows_in += load_rows(cot_refs, cot, 1)
    blank = jnp.zeros((PADDED - hidden, features), BF16)
    for ref in (gate_map, up_map, outer_map):
        ref[pl.ds(hidden, PADDED - hidden)] = blank
    for copy in rows_in:
        copy.wait()
    steps = sum(counts) // tall

    for i in range(len(pieces)):
        for copy in maps_in[i]:
            copy.wait()
        at = pl.ds(i * 256, 256)

        @pl.loop(0, steps)
        def _(step):
            here = pl.ds(pl.multiple_of(step * tall, 16), tall)
            gate_part = contract(normed[here], gate_map[at], 1, 1)
            up_part = contract(normed[here], up_map[at], 1, 1)
            grad_act = contract(cot[here], outer_map[at], 1, 1)
            squash = 1.0 / (1.0 + jnp.exp(-gate_part))
            scaled = grad_act * squash
            grad_gate[here, at] = (scaled * up_part * (1.0 + gate_part * (1.0 - squash))).astype(BF16)
            grad_up[here, at] = (scaled * gate_part).astype(BF16)

    wide = 512
    copies = []
    for n in range(features // wide):
        lanes = pl.ds(n * wide, wide)

        @pl.loop(0, steps)
        def _(step):
            here = pl.ds(pl.multiple_of(step * tall, 16), tall)
            result[here, lanes] = (
                contract(grad_gate[here], gate_map[:, lanes], 1, 0)
                + contract(grad_up[here], up_map[:, lanes], 1, 0)
            ).astype(BF16)

        number = 0
        for ref, parts in zip(out_refs, pieces_out):
            at = 0
            for start, size in parts:
                copies.append(
                    load(
                        result.at[pl.ds(start, size), lanes],
                        ref.at[pl.ds(at, size), lanes],
                        out_sem.at[n, number],
                    )
                )
                at += size
                number += 1
    for copy in copies:
        copy.wait()


def experts(normed_blocks, cot_blocks, inner, outer, pieces_out, tall):
    counts = [block.shape[0] for block in normed_blocks]
    features = normed_blocks[0].shape[1]
    hidden = outer.shape[0]
    total = sum(counts)
    anywhere = pl.BlockSpec(memory_space=pl.ANY)
    return pl.pallas_call(
        lambda *refs: expert_kernel(counts, pieces_out, tall, *refs),
        out_shape=[
            jax.ShapeDtypeStruct((sum(size for _, size in parts), features), BF16) for parts in pieces_out
        ],
        in_specs=[anywhere] * (2 * len(counts) + 2),
        out_specs=[anywhere] * len(pieces_out),
        scratch_shapes=[
            pltpu.VMEM((total, features), BF16),
            pltpu.VMEM((total, features), BF16),
            pltpu.VMEM((PADDED, features), BF16),
            pltpu.VMEM((PADDED, features), BF16),
            pltpu.VMEM((PADDED, features), BF16),
            pltpu.VMEM((total, PADDED), BF16),
            pltpu.VMEM((total, PADDED), BF16),
            pltpu.VMEM((total, features), BF16),
            pltpu.SemaphoreType.DMA((2, len(counts))),
            pltpu.SemaphoreType.DMA((3, 3)),
            pltpu.SemaphoreType.DMA((features // 512, sum(len(parts) for parts in pieces_out))),
        ],
        compiler_params=pltpu.CompilerParams(vmem_limit_bytes=48 * 1024 * 1024),
        cost_estimate=pl.CostEstimate(
            flops=10 * total * features * hidden,
            bytes_accessed=6 * total * features + 6 * hidden * features,
            transcendentals=total * hidden,
        ),
    )(*normed_blocks, *cot_blocks, inner, outer)


def param_kernel(scale, head_dim, core_ref, normed_ref, hidden_ref, grads_ref, context_ref, out_ref, terms):
    features = normed_ref.shape[1]
    tile = 1024
    for block in range(6):
        left_ref = normed_ref if block < 4 else hidden_ref
        right = (grads_ref[:, block * head_dim : (block + 1) * head_dim] if block < 4
                 else context_ref[:, (block - 4) * head_dim : (block - 3) * head_dim])
        for start in range(0, features, tile):
            part = contract(left_ref[:, start : start + tile], right, 0, 0) * scale
            terms[pl.ds(block * features + start, tile)] = part.astype(BF16)
    core = core_ref[0]

    @pl.loop(0, out_ref.shape[0])
    def _(group):
        size = out_ref.shape[1]
        out_ref[group] = terms[pl.ds(pl.multiple_of((2 * group + core) * size, 16), size)]


def param_terms(core, normed, hidden, grads, context, scale, head_dim):
    features = normed.shape[1]
    rows = 6 * features
    whole = pl.BlockSpec(memory_space=pltpu.VMEM)
    return pl.pallas_call(
        lambda *refs: param_kernel(scale, head_dim, *refs),
        out_shape=jax.ShapeDtypeStruct((64, rows // 128, head_dim), BF16),
        in_specs=[pl.BlockSpec(memory_space=pltpu.SMEM)] + [whole] * 4,
        out_specs=whole,
        scratch_shapes=[pltpu.VMEM((rows, head_dim), BF16)],
        compiler_params=pltpu.CompilerParams(vmem_limit_bytes=40 * 1024 * 1024),
        cost_estimate=pl.CostEstimate(
            flops=2 * rows * head_dim * normed.shape[0], bytes_accessed=8 * 1024 * 1024, transcendentals=0
        ),
    )(core, normed, hidden, grads, context)


def per_device(tokens, attn_param, expert_ids, gate_score, w_in, w_out, cotangent):
    seq_len, features = tokens.shape
    head_dim = attn_param.shape[1]
    score_scale = head_dim ** (-0.5)
    devices = N_DP * EXPERTS
    slots = slot_matrix(expert_ids, seq_len)
    inner = jnp.transpose(w_in[0], (1, 2, 0))
    outer = w_out[0]

    cot_main, cot_extra = between_experts(contract(slots, cotangent, 1, 0).astype(BF16))
    packed = gather_params(attn_param, cot_main)
    cot_near = spread_near(jnp.concatenate([cot_main, cot_extra], axis=0))
    cot_far = spread_far(cot_near, ())

    normed_one, inverse_one = layer_norm(tokens)
    normed_one_b = normed_one.astype(BF16)
    normed_both = jnp.concatenate([normed_one_b, swap(normed_one_b, "c")], axis=0)
    blocks = packed.reshape(2 * HEADS + 2, features, head_dim)
    project = blocks[: HEADS + 2]
    out_blocks = blocks[HEADS + 2 :]
    projected = jnp.einsum(
        "td,jdc->tjc", normed_one_b, project, preferred_element_type=F32
    ).astype(BF16)
    queries = projected[:, :HEADS]
    key_rows = projected[:, HEADS]
    value_rows = projected[:, HEADS + 1]
    scores = jnp.einsum("qhc,kc->hqk", queries, key_rows, preferred_element_type=F32) * score_scale
    causal = lax.broadcasted_iota(jnp.int32, (seq_len, seq_len), 0) >= lax.broadcasted_iota(
        jnp.int32, (seq_len, seq_len), 1
    )
    scores = jnp.where(causal[None], scores, MASKED)
    row_max = jnp.max(scores, axis=2, keepdims=True)
    raised = jnp.exp(scores - row_max)
    attention = raised / jnp.sum(raised, axis=2, keepdims=True)
    attention_b = attention.astype(BF16)
    context = jnp.einsum(
        "hqk,kc->qhc", attention_b, value_rows, preferred_element_type=F32
    ).astype(BF16)
    context_flat = context.reshape(seq_len, HEADS * head_dim)
    context_both = jnp.concatenate([context_flat, swap(context_flat, "c")], axis=0)
    attn_out = jnp.einsum("thc,hdc->td", context, out_blocks, preferred_element_type=F32)
    residual = (tokens.astype(F32) + attn_out).astype(BF16)
    normed_two, inverse_two = layer_norm(residual)
    main, extra = between_experts(contract(slots, normed_two.astype(BF16), 1, 0).astype(BF16))
    near = spread_near(after(jnp.concatenate([main, extra], axis=0), *cot_far))
    near[4], normed_both, context_both = lax.optimization_barrier((near[4], normed_both, context_both))
    h = HALF
    near_rows = experts(
        near,
        cot_near,
        inner,
        outer,
        [[(0, 2 * h)], [(2 * h, h)], [(3 * h, h)], [(4 * h, h)], [(5 * h, h)], [(6 * h, h)]],
        7 * h,
    )
    far = spread_far(near, (near_rows[0],))
    far_rows = experts(
        far,
        cot_far,
        inner,
        outer,
        [
            [(0, h)],
            [(h, h)],
            [(2 * h, h)],
            [(3 * h, h), (5 * h, h), (7 * h, h)],
            [(4 * h, h), (6 * h, h), (8 * h, h)],
        ],
        3 * h,
    )
    back_main, back_extra = between_experts(collect(near_rows, far_rows))
    cut = EXPERTS * MAIN
    back_rows = contract(slots[:cut], back_main, 0, 0) + contract(slots[cut:], back_extra, 0, 0)
    moe_grad = gate_score * back_rows
    grad_hidden = cotangent.astype(F32) + norm_back(normed_two, inverse_two, moe_grad)
    grad_hidden_b = grad_hidden.astype(BF16)
    hidden_both = jnp.concatenate([grad_hidden_b, swap(grad_hidden_b, "c")], axis=0)
    grad_context = jnp.einsum(
        "td,hdc->thc", grad_hidden_b, out_blocks, preferred_element_type=F32
    )
    grad_context_b = grad_context.astype(BF16)
    grad_attention = jnp.einsum(
        "qhc,kc->hqk", grad_context_b, value_rows, preferred_element_type=F32
    )
    grad_value = jnp.einsum("hqk,qhc->kc", attention_b, grad_context_b, preferred_element_type=F32)
    grad_scores = (
        attention
        * (grad_attention - jnp.sum(grad_attention * attention, axis=2, keepdims=True))
        * score_scale
    )
    grad_scores_b = grad_scores.astype(BF16)
    grad_query = jnp.einsum("hqk,kc->qhc", grad_scores_b, key_rows, preferred_element_type=F32)
    grad_key = jnp.einsum("hqk,qhc->kc", grad_scores_b, queries, preferred_element_type=F32)
    grad_qkv = jnp.concatenate([grad_query, grad_key[:, None], grad_value[:, None]], axis=1).astype(BF16)
    grads_flat = grad_qkv.reshape(seq_len, (HEADS + 2) * head_dim)
    grads_both = jnp.concatenate([grads_flat, swap(grads_flat, "c")], axis=0)
    core = lax.axis_index("c").astype(jnp.int32).reshape(1)
    terms = param_terms(
        core, normed_both, hidden_both, grads_both, context_both, (seq_len * devices) ** (-0.5), head_dim
    )
    attn_grad = jnp.sum(exchange(terms, CHIPS).astype(F32), axis=0)
    grad_normed = jnp.einsum("tjc,jdc->td", grad_qkv, project, preferred_element_type=F32)
    grad_tokens = (grad_hidden + norm_back(normed_one, inverse_one, grad_normed)).astype(BF16)
    return (grad_tokens, attn_grad)


def solution(mesh):
    fine = Mesh(mesh.devices.reshape(SIZES), AXES)
    rows = P(AXES, None)
    in_specs = (
        rows,
        P(DP, None),
        rows,
        rows,
        P(EX, None, None, DP),
        P(EX, DP, None),
        rows,
    )
    return jax.shard_map(
        per_device, mesh=fine, in_specs=in_specs, out_specs=(rows, rows), check_vma=False
    )
```

```python
import jax
import jax.numpy as jnp
from jax import lax
from jax.experimental import pallas as pl
from jax.experimental.pallas import tpu as pltpu
from jax.sharding import Mesh, PartitionSpec as P

EPSILON = 1e-05
MASKED = -1e30
AXES = ("z", "yh", "x", "yl", "c")
DP = ("z", "yh")
EX = ("x", "yl", "c")
CHIPS = ("z", "yh", "x", "yl")
SIZES = (4, 2, 4, 2, 2)
EXPERTS = 16
N_DP = 8
CAP = 10
MAIN = 8
HEADS = 2
HALF = 80
PADDED = 768
F32 = jnp.float32
BF16 = jnp.bfloat16


def layer_norm(values):
    widened = values.astype(F32)
    center = widened - jnp.mean(widened, axis=-1, keepdims=True)
    inverse = lax.rsqrt(jnp.mean(center * center, axis=-1, keepdims=True) + EPSILON)
    return (center * inverse, inverse)


def norm_back(normed, inverse, upstream):
    mean_grad = jnp.mean(upstream, axis=-1, keepdims=True)
    mean_proj = jnp.mean(upstream * normed, axis=-1, keepdims=True)
    return inverse * (upstream - mean_grad - normed * mean_proj)


def contract(first_op, second_op, first_dim, second_dim):
    return lax.dot_general(
        first_op,
        second_op,
        (((first_dim,), (second_dim,)), ((), ())),
        preferred_element_type=F32,
    )


def swap(values, axis):
    return lax.ppermute(values, axis, [(0, 1), (1, 0)])


def along_z(values, shift):
    return lax.ppermute(values, "z", [(i, (i + shift) % 4) for i in range(4)])


def exchange(blocks, axes):
    return lax.all_to_all(blocks, axes, split_axis=0, concat_axis=0, tiled=True)


def after(value, *earlier):
    return lax.optimization_barrier((value,) + earlier)[0]


def add_round(first, *others):
    total = first.astype(F32)
    for other in others:
        total = total + other.astype(F32)
    return total.astype(BF16)


def slot_matrix(expert_ids, seq_len):
    flat = expert_ids.reshape(-1)
    one_hot = (flat[:, None] == jnp.arange(EXPERTS, dtype=jnp.int32)[None, :]).astype(F32)
    rows = jnp.arange(seq_len)
    earlier = (rows[:, None] > rows[None, :]).astype(F32)
    before = jnp.dot(earlier, one_hot, preferred_element_type=F32)
    position = jnp.sum(before * one_hot, axis=1).astype(jnp.int32)
    rest = CAP - MAIN
    target = jnp.where(
        position < MAIN, flat * MAIN + position, EXPERTS * MAIN + flat * rest + position - MAIN
    )
    return (jnp.arange(EXPERTS * CAP, dtype=jnp.int32)[:, None] == target[None, :]).astype(BF16)


def place_kernel(places, piece, at_ref, *refs):
    block_refs, out_ref, sems = refs[: len(places)], refs[-2], refs[-1]
    copies = []
    number = 0
    for ref, parts in zip(block_refs, places):
        for i, (s, r, half) in enumerate(parts):
            z = lax.rem(at_ref[0] - s + 4, 4)
            yh = lax.rem(at_ref[1] + r, 2)
            copy = pltpu.make_async_copy(
                ref.at[pl.ds(i * piece, piece)], out_ref.at[z * 2 + yh, pl.ds(half * piece, piece)], sems.at[number]
            )
            copy.start()
            copies.append(copy)
            number += 1
    for copy in copies:
        copy.wait()


def gather_params(attn_param, earlier):
    rows, head_dim = attn_param.shape
    half = rows // 2
    piece = half // 2
    core = lax.axis_index("c")
    own = lax.dynamic_slice_in_dim(attn_param, core * half, half, 0)
    first, second = own[:piece], own[piece:]
    around = [along_z(first, s) for s in (1, 3, 2)]
    own_y = swap(own, "yh")
    pair = after(jnp.concatenate([second, own_y[piece:]], axis=0), around[0], around[1])
    around_y = [swap(block, "yh") for block in around]
    pairs = [along_z(pair, s) for s in (1, 3, 2)]
    blocks = [own, own_y] + around + around_y + pairs
    places = (
        [[(0, 0, 0), (0, 0, 1)], [(0, 1, 0), (0, 1, 1)]]
        + [[(s, 0, 0)] for s in (1, 3, 2)]
        + [[(s, 1, 0)] for s in (1, 3, 2)]
        + [[(s, 0, 1), (s, 1, 1)] for s in (1, 3, 2)]
    )
    at = after(jnp.stack([lax.axis_index("z"), lax.axis_index("yh")]).astype(jnp.int32), earlier)
    anywhere = pl.BlockSpec(memory_space=pl.ANY)
    own = pl.pallas_call(
        lambda *refs: place_kernel(places, piece, *refs),
        out_shape=jax.ShapeDtypeStruct((N_DP, half, head_dim), BF16),
        in_specs=[pl.BlockSpec(memory_space=pltpu.SMEM)] + [anywhere] * len(blocks),
        out_specs=pl.BlockSpec(memory_space=pltpu.VMEM),
        scratch_shapes=[pltpu.SemaphoreType.DMA((16,))],
        compiler_params=pltpu.CompilerParams(vmem_limit_bytes=16 * 1024 * 1024),
    )(at, *blocks)
    other = swap(own, "c")
    first = jnp.where(core == 0, own, other)
    second = jnp.where(core == 0, other, own)
    return jnp.stack([first, second], axis=1).reshape(N_DP * rows, head_dim)


def between_experts(rows):
    features = rows.shape[1]
    cut = EXPERTS * MAIN
    extra = rows[cut:].reshape(cut, -1)
    packed = jnp.concatenate([rows[:cut], extra], axis=1)
    width = packed.shape[1]
    packed = exchange(packed.reshape(EXPERTS, MAIN, width), EX).reshape(cut, width)
    extra = packed[:, features:].reshape(-1, features)
    return packed[:, :features], extra


def spread_near(own):
    one = own[:HALF]
    own_y = swap(own, "yh")
    return [own, own_y] + [along_z(one, s) for s in (1, 3, 2)]


def spread_far(near, between):
    own, own_y, near_z, far_z, across = near
    pair = after(jnp.concatenate([own[HALF:], own_y[HALF:]], axis=0), near_z, far_z)
    first = [swap(near_z, "yh"), swap(far_z, "yh")]
    second = [along_z(pair, 1), along_z(pair, 3)]
    return first + [swap(after(across, *between), "yh")] + second + [along_z(pair, 2)]


def collect(near, far):
    kept, one_y, two_y, *one_z = near
    early = [along_z(block, -s) for block, s in zip(one_z, (1, 3, 2))]
    early_y = swap(two_y, "yh")
    *one_yz, two_z, two_yz = far
    (*one_yz, two_yz), early, early_y = lax.optimization_barrier(([*one_yz, two_yz], early, early_y))
    late = [along_z(block, -s) for block, s in zip(one_yz, (1, 3, 2))]
    swapped = swap(two_yz, "yh")
    across = swap(add_round(one_y, *late), "yh")
    pairs = add_round(two_z, swapped)
    back = [along_z(pairs[i * HALF : (i + 1) * HALF], -s) for i, s in enumerate((1, 3, 2))]
    one = add_round(kept[:HALF], across, *early)
    two = add_round(kept[HALF:], early_y, *back)
    return jnp.concatenate([one, two], axis=0)


def expert_kernel(counts, pieces_out, tall, *refs):
    count = len(counts)
    outs = len(pieces_out)
    normed_refs, cot_refs = refs[:count], refs[count : 2 * count]
    inner_ref, outer_ref = refs[2 * count : 2 * count + 2]
    out_refs = refs[2 * count + 2 : 2 * count + 2 + outs]
    (normed, cot, gate_map, up_map, outer_map, grad_gate, grad_up, result, row_sem, map_sem, out_sem) = refs[
        2 * count + 2 + outs :
    ]
    hidden, features = outer_ref.shape
    starts = [sum(counts[:i]) for i in range(count)]

    def load(source, target, sem):
        copy = pltpu.make_async_copy(source, target, sem)
        copy.start()
        return copy

    def load_rows(block_refs, target, side):
        return [
            load(ref, target.at[pl.ds(starts[i], counts[i])], row_sem.at[side, i])
            for i, ref in enumerate(block_refs)
        ]

    pieces = [(0, 256), (256, 256), (512, hidden - 512)]
    rows_in = load_rows(normed_refs, normed, 0)
    maps_in = []
    for i, (start, size) in enumerate(pieces):
        at = pl.ds(start, size)
        maps_in.append(
            [
                load(inner_ref.at[0, at], gate_map.at[at], map_sem.at[0, i]),
                load(inner_ref.at[1, at], up_map.at[at], map_sem.at[1, i]),
                load(outer_ref.at[at], outer_map.at[at], map_sem.at[2, i]),
            ]
        )
        if i == 0:
            rows_in += load_rows(cot_refs, cot, 1)
    blank = jnp.zeros((PADDED - hidden, features), BF16)
    for ref in (gate_map, up_map, outer_map):
        ref[pl.ds(hidden, PADDED - hidden)] = blank
    for copy in rows_in:
        copy.wait()
    steps = sum(counts) // tall

    for i in range(len(pieces)):
        for copy in maps_in[i]:
            copy.wait()
        at = pl.ds(i * 256, 256)

        @pl.loop(0, steps)
        def _(step):
            here = pl.ds(pl.multiple_of(step * tall, 16), tall)
            gate_part = contract(normed[here], gate_map[at], 1, 1)
            up_part = contract(normed[here], up_map[at], 1, 1)
            grad_act = contract(cot[here], outer_map[at], 1, 1)
            squash = 1.0 / (1.0 + jnp.exp(-gate_part))
            scaled = grad_act * squash
            grad_gate[here, at] = (scaled * up_part * (1.0 + gate_part * (1.0 - squash))).astype(BF16)
            grad_up[here, at] = (scaled * gate_part).astype(BF16)

    wide = 512
    copies = []
    for n in range(features // wide):
        lanes = pl.ds(n * wide, wide)

        @pl.loop(0, steps)
        def _(step):
            here = pl.ds(pl.multiple_of(step * tall, 16), tall)
            result[here, lanes] = (
                contract(grad_gate[here], gate_map[:, lanes], 1, 0)
                + contract(grad_up[here], up_map[:, lanes], 1, 0)
            ).astype(BF16)

        number = 0
        for ref, parts in zip(out_refs, pieces_out):
            at = 0
            for start, size in parts:
                copies.append(
                    load(
                        result.at[pl.ds(start, size), lanes],
                        ref.at[pl.ds(at, size), lanes],
                        out_sem.at[n, number],
                    )
                )
                at += size
                number += 1
    for copy in copies:
        copy.wait()


def experts(normed_blocks, cot_blocks, inner, outer, pieces_out, tall):
    counts = [block.shape[0] for block in normed_blocks]
    features = normed_blocks[0].shape[1]
    hidden = outer.shape[0]
    total = sum(counts)
    anywhere = pl.BlockSpec(memory_space=pl.ANY)
    return pl.pallas_call(
        lambda *refs: expert_kernel(counts, pieces_out, tall, *refs),
        out_shape=[
            jax.ShapeDtypeStruct((sum(size for _, size in parts), features), BF16) for parts in pieces_out
        ],
        in_specs=[anywhere] * (2 * len(counts) + 2),
        out_specs=[anywhere] * len(pieces_out),
        scratch_shapes=[
            pltpu.VMEM((total, features), BF16),
            pltpu.VMEM((total, features), BF16),
            pltpu.VMEM((PADDED, features), BF16),
            pltpu.VMEM((PADDED, features), BF16),
            pltpu.VMEM((PADDED, features), BF16),
            pltpu.VMEM((total, PADDED), BF16),
            pltpu.VMEM((total, PADDED), BF16),
            pltpu.VMEM((total, features), BF16),
            pltpu.SemaphoreType.DMA((2, len(counts))),
            pltpu.SemaphoreType.DMA((3, 3)),
            pltpu.SemaphoreType.DMA((features // 512, sum(len(parts) for parts in pieces_out))),
        ],
        compiler_params=pltpu.CompilerParams(vmem_limit_bytes=48 * 1024 * 1024),
        cost_estimate=pl.CostEstimate(
            flops=10 * total * features * hidden,
            bytes_accessed=6 * total * features + 6 * hidden * features,
            transcendentals=total * hidden,
        ),
    )(*normed_blocks, *cot_blocks, inner, outer)


def param_kernel(scale, head_dim, core_ref, normed_ref, hidden_ref, grads_ref, context_ref, out_ref, terms):
    features = normed_ref.shape[1]
    tile = 1024
    for block in range(6):
        left_ref = normed_ref if block < 4 else hidden_ref
        right = (grads_ref[:, block * head_dim : (block + 1) * head_dim] if block < 4
                 else context_ref[:, (block - 4) * head_dim : (block - 3) * head_dim])
        for start in range(0, features, tile):
            part = contract(left_ref[:, start : start + tile], right, 0, 0) * scale
            terms[pl.ds(block * features + start, tile)] = part.astype(BF16)
    core = core_ref[0]

    @pl.loop(0, out_ref.shape[0])
    def _(group):
        size = out_ref.shape[1]
        out_ref[group] = terms[pl.ds(pl.multiple_of((2 * group + core) * size, 16), size)]


def param_terms(core, normed, hidden, grads, context, scale, head_dim):
    features = normed.shape[1]
    rows = 6 * features
    whole = pl.BlockSpec(memory_space=pltpu.VMEM)
    return pl.pallas_call(
        lambda *refs: param_kernel(scale, head_dim, *refs),
        out_shape=jax.ShapeDtypeStruct((64, rows // 128, head_dim), BF16),
        in_specs=[pl.BlockSpec(memory_space=pltpu.SMEM)] + [whole] * 4,
        out_specs=whole,
        scratch_shapes=[pltpu.VMEM((rows, head_dim), BF16)],
        compiler_params=pltpu.CompilerParams(vmem_limit_bytes=40 * 1024 * 1024),
        cost_estimate=pl.CostEstimate(
            flops=2 * rows * head_dim * normed.shape[0], bytes_accessed=8 * 1024 * 1024, transcendentals=0
        ),
    )(core, normed, hidden, grads, context)


def per_device(tokens, attn_param, expert_ids, gate_score, w_in, w_out, cotangent):
    seq_len, features = tokens.shape
    head_dim = attn_param.shape[1]
    score_scale = head_dim ** (-0.5)
    devices = N_DP * EXPERTS
    slots = slot_matrix(expert_ids, seq_len)
    inner = jnp.transpose(w_in[0], (1, 2, 0))
    outer = w_out[0]

    cot_main, cot_extra = between_experts(contract(slots, cotangent, 1, 0).astype(BF16))
    packed = gather_params(attn_param, cot_main)
    cot_near = spread_near(jnp.concatenate([cot_main, cot_extra], axis=0))
    cot_far = spread_far(cot_near, ())

    normed_one, inverse_one = layer_norm(tokens)
    normed_one_b = normed_one.astype(BF16)
    normed_both = jnp.concatenate([normed_one_b, swap(normed_one_b, "c")], axis=0)
    blocks = packed.reshape(2 * HEADS + 2, features, head_dim)
    project = blocks[: HEADS + 2]
    out_blocks = blocks[HEADS + 2 :]
    projected = jnp.einsum(
        "td,jdc->tjc", normed_one_b, project, preferred_element_type=F32
    ).astype(BF16)
    queries = projected[:, :HEADS]
    key_rows = projected[:, HEADS]
    value_rows = projected[:, HEADS + 1]
    scores = jnp.einsum("qhc,kc->hqk", queries, key_rows, preferred_element_type=F32) * score_scale
    causal = lax.broadcasted_iota(jnp.int32, (seq_len, seq_len), 0) >= lax.broadcasted_iota(
        jnp.int32, (seq_len, seq_len), 1
    )
    scores = jnp.where(causal[None], scores, MASKED)
    row_max = jnp.max(scores, axis=2, keepdims=True)
    raised = jnp.exp(scores - row_max)
    attention = raised / jnp.sum(raised, axis=2, keepdims=True)
    attention_b = attention.astype(BF16)
    context = jnp.einsum(
        "hqk,kc->qhc", attention_b, value_rows, preferred_element_type=F32
    ).astype(BF16)
    context_flat = context.reshape(seq_len, HEADS * head_dim)
    context_both = jnp.concatenate([context_flat, swap(context_flat, "c")], axis=0)
    attn_out = jnp.einsum("thc,hdc->td", context, out_blocks, preferred_element_type=F32)
    residual = (tokens.astype(F32) + attn_out).astype(BF16)
    normed_two, inverse_two = layer_norm(residual)
    main, extra = between_experts(contract(slots, normed_two.astype(BF16), 1, 0).astype(BF16))
    near = spread_near(after(jnp.concatenate([main, extra], axis=0), *cot_far))
    near[4], normed_both, context_both = lax.optimization_barrier((near[4], normed_both, context_both))
    h = HALF
    near_rows = experts(
        near,
        cot_near,
        inner,
        outer,
        [[(0, 2 * h)], [(2 * h, h)], [(3 * h, h)], [(4 * h, h)], [(5 * h, h)], [(6 * h, h)]],
        7 * h,
    )
    far = spread_far(near, (near_rows[0],))
    far_rows = experts(
        far,
        cot_far,
        inner,
        outer,
        [
            [(0, h)],
            [(h, h)],
            [(2 * h, h)],
            [(3 * h, h), (5 * h, h), (7 * h, h)],
            [(4 * h, h), (6 * h, h), (8 * h, h)],
        ],
        3 * h,
    )
    back_main, back_extra = between_experts(collect(near_rows, far_rows))
    cut = EXPERTS * MAIN
    back_rows = contract(slots[:cut], back_main, 0, 0) + contract(slots[cut:], back_extra, 0, 0)
    moe_grad = gate_score * back_rows
    grad_hidden = cotangent.astype(F32) + norm_back(normed_two, inverse_two, moe_grad)
    grad_hidden_b = grad_hidden.astype(BF16)
    hidden_both = jnp.concatenate([grad_hidden_b, swap(grad_hidden_b, "c")], axis=0)
    grad_context = jnp.einsum(
        "td,hdc->thc", grad_hidden_b, out_blocks, preferred_element_type=F32
    )
    grad_context_b = grad_context.astype(BF16)
    grad_attention = jnp.einsum(
        "qhc,kc->hqk", grad_context_b, value_rows, preferred_element_type=F32
    )
    grad_value = jnp.einsum("hqk,qhc->kc", attention_b, grad_context_b, preferred_element_type=F32)
    grad_scores = (
        attention
        * (grad_attention - jnp.sum(grad_attention * attention, axis=2, keepdims=True))
        * score_scale
    )
    grad_scores_b = grad_scores.astype(BF16)
    grad_query = jnp.einsum("hqk,kc->qhc", grad_scores_b, key_rows, preferred_element_type=F32)
    grad_key = jnp.einsum("hqk,qhc->kc", grad_scores_b, queries, preferred_element_type=F32)
    grad_qkv = jnp.concatenate([grad_query, grad_key[:, None], grad_value[:, None]], axis=1).astype(BF16)
    grads_flat = grad_qkv.reshape(seq_len, (HEADS + 2) * head_dim)
    grads_both = jnp.concatenate([grads_flat, swap(grads_flat, "c")], axis=0)
    core = lax.axis_index("c").astype(jnp.int32).reshape(1)
    terms = param_terms(
        core, normed_both, hidden_both, grads_both, context_both, (seq_len * devices) ** (-0.5), head_dim
    )
    attn_grad = jnp.sum(exchange(terms, CHIPS).astype(F32), axis=0)
    grad_normed = jnp.einsum("tjc,jdc->td", grad_qkv, project, preferred_element_type=F32)
    grad_tokens = (grad_hidden + norm_back(normed_one, inverse_one, grad_normed)).astype(BF16)
    return (grad_tokens, attn_grad)


def solution(mesh):
    fine = Mesh(mesh.devices.reshape(SIZES), AXES)
    rows = P(AXES, None)
    in_specs = (
        rows,
        P(DP, None),
        rows,
        rows,
        P(EX, None, None, DP),
        P(EX, DP, None),
        rows,
    )
    return jax.shard_map(
        per_device, mesh=fine, in_specs=in_specs, out_specs=(rows, rows), check_vma=False
    )
```

```python
import jax
import jax.numpy as jnp
from jax import lax
from jax.experimental import pallas as pl
from jax.experimental.pallas import tpu as pltpu
from jax.sharding import Mesh, PartitionSpec as P

EPSILON = 1e-05
MASKED = -1e30
AXES = ("z", "yh", "x", "yl", "c")
DP = ("z", "yh")
EX = ("x", "yl", "c")
CHIPS = ("z", "yh", "x", "yl")
SIZES = (4, 2, 4, 2, 2)
EXPERTS = 16
N_DP = 8
CAP = 10
MAIN = 8
HEADS = 2
HALF = 80
PADDED = 768
F32 = jnp.float32
BF16 = jnp.bfloat16


def layer_norm(values):
    widened = values.astype(F32)
    center = widened - jnp.mean(widened, axis=-1, keepdims=True)
    inverse = lax.rsqrt(jnp.mean(center * center, axis=-1, keepdims=True) + EPSILON)
    return (center * inverse, inverse)


def norm_back(normed, inverse, upstream):
    mean_grad = jnp.mean(upstream, axis=-1, keepdims=True)
    mean_proj = jnp.mean(upstream * normed, axis=-1, keepdims=True)
    return inverse * (upstream - mean_grad - normed * mean_proj)


def contract(first_op, second_op, first_dim, second_dim):
    return lax.dot_general(
        first_op,
        second_op,
        (((first_dim,), (second_dim,)), ((), ())),
        preferred_element_type=F32,
    )


def swap(values, axis):
    return lax.ppermute(values, axis, [(0, 1), (1, 0)])


def along_z(values, shift):
    return lax.ppermute(values, "z", [(i, (i + shift) % 4) for i in range(4)])


def exchange(blocks, axes):
    return lax.all_to_all(blocks, axes, split_axis=0, concat_axis=0, tiled=True)


def after(value, *earlier):
    return lax.optimization_barrier((value,) + earlier)[0]


def add_round(first, *others):
    total = first.astype(F32)
    for other in others:
        total = total + other.astype(F32)
    return total.astype(BF16)


def slot_matrix(expert_ids, seq_len):
    flat = expert_ids.reshape(-1)
    one_hot = (flat[:, None] == jnp.arange(EXPERTS, dtype=jnp.int32)[None, :]).astype(F32)
    rows = jnp.arange(seq_len)
    earlier = (rows[:, None] > rows[None, :]).astype(F32)
    before = jnp.dot(earlier, one_hot, preferred_element_type=F32)
    position = jnp.sum(before * one_hot, axis=1).astype(jnp.int32)
    rest = CAP - MAIN
    target = jnp.where(
        position < MAIN, flat * MAIN + position, EXPERTS * MAIN + flat * rest + position - MAIN
    )
    return (jnp.arange(EXPERTS * CAP, dtype=jnp.int32)[:, None] == target[None, :]).astype(BF16)


def place_kernel(places, piece, at_ref, *refs):
    block_refs, out_ref, sems = refs[: len(places)], refs[-2], refs[-1]
    copies = []
    number = 0
    for ref, parts in zip(block_refs, places):
        for i, (s, r, half) in enumerate(parts):
            z = lax.rem(at_ref[0] - s + 4, 4)
            yh = lax.rem(at_ref[1] + r, 2)
            copy = pltpu.make_async_copy(
                ref.at[pl.ds(i * piece, piece)], out_ref.at[z * 2 + yh, pl.ds(half * piece, piece)], sems.at[number]
            )
            copy.start()
            copies.append(copy)
            number += 1
    for copy in copies:
        copy.wait()


def gather_params(attn_param, earlier):
    rows, head_dim = attn_param.shape
    half = rows // 2
    piece = half // 2
    core = lax.axis_index("c")
    own = lax.dynamic_slice_in_dim(attn_param, core * half, half, 0)
    first, second = own[:piece], own[piece:]
    around = [along_z(first, s) for s in (1, 3, 2)]
    own_y = swap(own, "yh")
    pair = after(jnp.concatenate([second, own_y[piece:]], axis=0), around[0], around[1])
    around_y = [swap(block, "yh") for block in around]
    pairs = [along_z(pair, s) for s in (1, 3, 2)]
    blocks = [own, own_y] + around + around_y + pairs
    places = (
        [[(0, 0, 0), (0, 0, 1)], [(0, 1, 0), (0, 1, 1)]]
        + [[(s, 0, 0)] for s in (1, 3, 2)]
        + [[(s, 1, 0)] for s in (1, 3, 2)]
        + [[(s, 0, 1), (s, 1, 1)] for s in (1, 3, 2)]
    )
    at = after(jnp.stack([lax.axis_index("z"), lax.axis_index("yh")]).astype(jnp.int32), earlier)
    anywhere = pl.BlockSpec(memory_space=pl.ANY)
    own = pl.pallas_call(
        lambda *refs: place_kernel(places, piece, *refs),
        out_shape=jax.ShapeDtypeStruct((N_DP, half, head_dim), BF16),
        in_specs=[pl.BlockSpec(memory_space=pltpu.SMEM)] + [anywhere] * len(blocks),
        out_specs=pl.BlockSpec(memory_space=pltpu.VMEM),
        scratch_shapes=[pltpu.SemaphoreType.DMA((16,))],
        compiler_params=pltpu.CompilerParams(vmem_limit_bytes=60 * 1024 * 1024),
    )(at, *blocks)
    other = swap(own, "c")
    first = jnp.where(core == 0, own, other)
    second = jnp.where(core == 0, other, own)
    return jnp.stack([first, second], axis=1).reshape(N_DP * rows, head_dim)


def between_experts(rows):
    features = rows.shape[1]
    cut = EXPERTS * MAIN
    extra = rows[cut:].reshape(cut, -1)
    packed = jnp.concatenate([rows[:cut], extra], axis=1)
    width = packed.shape[1]
    packed = exchange(packed.reshape(EXPERTS, MAIN, width), EX).reshape(cut, width)
    extra = packed[:, features:].reshape(-1, features)
    return packed[:, :features], extra


def spread_near(own):
    one = own[:HALF]
    own_y = swap(own, "yh")
    return [own, own_y] + [along_z(one, s) for s in (1, 3, 2)]


def spread_far(near, between):
    own, own_y, near_z, far_z, across = near
    pair = after(jnp.concatenate([own[HALF:], own_y[HALF:]], axis=0), near_z, far_z)
    first = [swap(near_z, "yh"), swap(far_z, "yh")]
    second = [along_z(pair, 1), along_z(pair, 3)]
    return first + [swap(after(across, *between), "yh")] + second + [along_z(pair, 2)]


def collect(near, far):
    kept, one_y, two_y, *one_z = near
    early = [along_z(block, -s) for block, s in zip(one_z, (1, 3, 2))]
    early_y = swap(two_y, "yh")
    *one_yz, two_z, two_yz = far
    (*one_yz, two_yz), early, early_y = lax.optimization_barrier(([*one_yz, two_yz], early, early_y))
    late = [along_z(block, -s) for block, s in zip(one_yz, (1, 3, 2))]
    swapped = swap(two_yz, "yh")
    across = swap(add_round(one_y, *late), "yh")
    pairs = add_round(two_z, swapped)
    back = [along_z(pairs[i * HALF : (i + 1) * HALF], -s) for i, s in enumerate((1, 3, 2))]
    one = add_round(kept[:HALF], across, *early)
    two = add_round(kept[HALF:], early_y, *back)
    return jnp.concatenate([one, two], axis=0)


def expert_kernel(counts, sources, pieces_out, tall, at_ref, cot_ref, *refs):
    count = len(counts)
    outs = len(pieces_out)
    normed_refs = refs[:count]
    inner_ref, outer_ref = refs[count : count + 2]
    out_refs = refs[count + 2 : count + 2 + outs]
    (normed, cot, gate_map, up_map, outer_map, grad_gate, grad_up, result, row_sem, cot_sem, map_sem, out_sem) = refs[
        count + 2 + outs :
    ]
    hidden, features = outer_ref.shape
    starts = [sum(counts[:i]) for i in range(count)]

    def load(source, target, sem):
        copy = pltpu.make_async_copy(source, target, sem)
        copy.start()
        return copy

    pieces = [(0, 256), (256, 256), (512, hidden - 512)]
    rows_in = [
        load(ref, normed.at[pl.ds(starts[i], counts[i])], row_sem.at[i]) for i, ref in enumerate(normed_refs)
    ]
    maps_in = []
    for i, (start, size) in enumerate(pieces):
        at = pl.ds(start, size)
        maps_in.append(
            [
                load(inner_ref.at[0, at], gate_map.at[at], map_sem.at[0, i]),
                load(inner_ref.at[1, at], up_map.at[at], map_sem.at[1, i]),
                load(outer_ref.at[at], outer_map.at[at], map_sem.at[2, i]),
            ]
        )
        if i == 0:
            at = 0
            for j, (s, r, start, size) in enumerate(sources):
                device = lax.rem(at_ref[0] - s + 4, 4) * 2 + lax.rem(at_ref[1] + r, 2)
                rows_in.append(
                    load(cot_ref.at[device, pl.ds(start, size)], cot.at[pl.ds(at, size)], cot_sem.at[j])
                )
                at += size
    blank = jnp.zeros((PADDED - hidden, features), BF16)
    for ref in (gate_map, up_map, outer_map):
        ref[pl.ds(hidden, PADDED - hidden)] = blank
    for copy in rows_in:
        copy.wait()
    steps = sum(counts) // tall

    for i in range(len(pieces)):
        for copy in maps_in[i]:
            copy.wait()
        at = pl.ds(i * 256, 256)

        @pl.loop(0, steps)
        def _(step):
            here = pl.ds(pl.multiple_of(step * tall, 16), tall)
            gate_part = contract(normed[here], gate_map[at], 1, 1)
            up_part = contract(normed[here], up_map[at], 1, 1)
            grad_act = contract(cot[here], outer_map[at], 1, 1)
            squash = 1.0 / (1.0 + jnp.exp(-gate_part))
            scaled = grad_act * squash
            grad_gate[here, at] = (scaled * up_part * (1.0 + gate_part * (1.0 - squash))).astype(BF16)
            grad_up[here, at] = (scaled * gate_part).astype(BF16)

    wide = 512
    copies = []
    for n in range(features // wide):
        lanes = pl.ds(n * wide, wide)

        @pl.loop(0, steps)
        def _(step):
            here = pl.ds(pl.multiple_of(step * tall, 16), tall)
            result[here, lanes] = (
                contract(grad_gate[here], gate_map[:, lanes], 1, 0)
                + contract(grad_up[here], up_map[:, lanes], 1, 0)
            ).astype(BF16)

        number = 0
        for ref, parts in zip(out_refs, pieces_out):
            at = 0
            for start, size in parts:
                copies.append(
                    load(
                        result.at[pl.ds(start, size), lanes],
                        ref.at[pl.ds(at, size), lanes],
                        out_sem.at[n, number],
                    )
                )
                at += size
                number += 1
    for copy in copies:
        copy.wait()


def experts(at, normed_blocks, cot, sources, inner, outer, pieces_out, tall):
    counts = [block.shape[0] for block in normed_blocks]
    features = normed_blocks[0].shape[1]
    hidden = outer.shape[0]
    total = sum(counts)
    anywhere = pl.BlockSpec(memory_space=pl.ANY)
    return pl.pallas_call(
        lambda *refs: expert_kernel(counts, sources, pieces_out, tall, *refs),
        out_shape=[
            jax.ShapeDtypeStruct((sum(size for _, size in parts), features), BF16) for parts in pieces_out
        ],
        in_specs=[pl.BlockSpec(memory_space=pltpu.SMEM)] + [anywhere] * (len(counts) + 3),
        out_specs=[anywhere] * len(pieces_out),
        scratch_shapes=[
            pltpu.VMEM((total, features), BF16),
            pltpu.VMEM((total, features), BF16),
            pltpu.VMEM((PADDED, features), BF16),
            pltpu.VMEM((PADDED, features), BF16),
            pltpu.VMEM((PADDED, features), BF16),
            pltpu.VMEM((total, PADDED), BF16),
            pltpu.VMEM((total, PADDED), BF16),
            pltpu.VMEM((total, features), BF16),
            pltpu.SemaphoreType.DMA((len(counts),)),
            pltpu.SemaphoreType.DMA((len(sources),)),
            pltpu.SemaphoreType.DMA((3, 3)),
            pltpu.SemaphoreType.DMA((features // 512, sum(len(parts) for parts in pieces_out))),
        ],
        compiler_params=pltpu.CompilerParams(vmem_limit_bytes=60 * 1024 * 1024),
        cost_estimate=pl.CostEstimate(
            flops=10 * total * features * hidden,
            bytes_accessed=6 * total * features + 6 * hidden * features,
            transcendentals=total * hidden,
        ),
    )(at, cot, *normed_blocks, inner, outer)


def param_kernel(scale, head_dim, core_ref, normed_ref, hidden_ref, grads_ref, context_ref, out_ref, terms):
    features = normed_ref.shape[1]
    tile = 1024
    for block in range(6):
        left_ref = normed_ref if block < 4 else hidden_ref
        right = (grads_ref[:, block * head_dim : (block + 1) * head_dim] if block < 4
                 else context_ref[:, (block - 4) * head_dim : (block - 3) * head_dim])
        for start in range(0, features, tile):
            part = contract(left_ref[:, start : start + tile], right, 0, 0) * scale
            terms[pl.ds(block * features + start, tile)] = part.astype(BF16)
    core = core_ref[0]

    @pl.loop(0, out_ref.shape[0])
    def _(group):
        size = out_ref.shape[1]
        out_ref[group] = terms[pl.ds(pl.multiple_of((2 * group + core) * size, 16), size)]


def param_terms(core, normed, hidden, grads, context, scale, head_dim):
    features = normed.shape[1]
    rows = 6 * features
    whole = pl.BlockSpec(memory_space=pltpu.VMEM)
    return pl.pallas_call(
        lambda *refs: param_kernel(scale, head_dim, *refs),
        out_shape=jax.ShapeDtypeStruct((64, rows // 128, head_dim), BF16),
        in_specs=[pl.BlockSpec(memory_space=pltpu.SMEM)] + [whole] * 4,
        out_specs=whole,
        scratch_shapes=[pltpu.VMEM((rows, head_dim), BF16)],
        compiler_params=pltpu.CompilerParams(vmem_limit_bytes=40 * 1024 * 1024),
        cost_estimate=pl.CostEstimate(
            flops=2 * rows * head_dim * normed.shape[0], bytes_accessed=8 * 1024 * 1024, transcendentals=0
        ),
    )(core, normed, hidden, grads, context)


def per_device(tokens, attn_param, expert_ids, gate_score, w_in, w_out, cotangent):
    seq_len, features = tokens.shape
    head_dim = attn_param.shape[1]
    score_scale = head_dim ** (-0.5)
    devices = N_DP * EXPERTS
    slots = slot_matrix(expert_ids, seq_len)
    inner = jnp.transpose(w_in[0], (1, 2, 0))
    outer = w_out[0]

    cot_main, cot_extra = between_experts(contract(slots, cotangent, 1, 0).astype(BF16))
    cot_rows = jnp.concatenate([cot_main, cot_extra], axis=0)
    packed = gather_params(attn_param, cot_rows)
    cot = lax.all_gather(cot_rows, DP, axis=0)
    at = jnp.stack([lax.axis_index("z"), lax.axis_index("yh")]).astype(jnp.int32)

    normed_one, inverse_one = layer_norm(tokens)
    normed_one_b = normed_one.astype(BF16)
    normed_both = jnp.concatenate([normed_one_b, swap(normed_one_b, "c")], axis=0)
    blocks = packed.reshape(2 * HEADS + 2, features, head_dim)
    project = blocks[: HEADS + 2]
    out_blocks = blocks[HEADS + 2 :]
    projected = jnp.einsum(
        "td,jdc->tjc", normed_one_b, project, preferred_element_type=F32
    ).astype(BF16)
    queries = projected[:, :HEADS]
    key_rows = projected[:, HEADS]
    value_rows = projected[:, HEADS + 1]
    scores = jnp.einsum("qhc,kc->hqk", queries, key_rows, preferred_element_type=F32) * score_scale
    causal = lax.broadcasted_iota(jnp.int32, (seq_len, seq_len), 0) >= lax.broadcasted_iota(
        jnp.int32, (seq_len, seq_len), 1
    )
    scores = jnp.where(causal[None], scores, MASKED)
    row_max = jnp.max(scores, axis=2, keepdims=True)
    raised = jnp.exp(scores - row_max)
    attention = raised / jnp.sum(raised, axis=2, keepdims=True)
    attention_b = attention.astype(BF16)
    context = jnp.einsum(
        "hqk,kc->qhc", attention_b, value_rows, preferred_element_type=F32
    ).astype(BF16)
    context_flat = context.reshape(seq_len, HEADS * head_dim)
    context_both = jnp.concatenate([context_flat, swap(context_flat, "c")], axis=0)
    attn_out = jnp.einsum("thc,hdc->td", context, out_blocks, preferred_element_type=F32)
    residual = (tokens.astype(F32) + attn_out).astype(BF16)
    normed_two, inverse_two = layer_norm(residual)
    main, extra = between_experts(contract(slots, normed_two.astype(BF16), 1, 0).astype(BF16))
    near = spread_near(jnp.concatenate([main, extra], axis=0))
    near[4], normed_both, context_both = lax.optimization_barrier((near[4], normed_both, context_both))
    h = HALF
    near_rows = experts(
        at,
        near,
        cot,
        [(0, 0, 0, 2 * h), (0, 1, 0, 2 * h)] + [(s, 0, 0, h) for s in (1, 3, 2)],
        inner,
        outer,
        [[(0, 2 * h)], [(2 * h, h)], [(3 * h, h)], [(4 * h, h)], [(5 * h, h)], [(6 * h, h)]],
        7 * h,
    )
    far = spread_far(near, (near_rows[0],))
    far_rows = experts(
        at,
        far,
        cot,
        [(s, 1, 0, h) for s in (1, 3, 2)] + [(s, r, h, h) for s in (1, 3, 2) for r in (0, 1)],
        inner,
        outer,
        [
            [(0, h)],
            [(h, h)],
            [(2 * h, h)],
            [(3 * h, h), (5 * h, h), (7 * h, h)],
            [(4 * h, h), (6 * h, h), (8 * h, h)],
        ],
        3 * h,
    )
    back_main, back_extra = between_experts(collect(near_rows, far_rows))
    cut = EXPERTS * MAIN
    back_rows = contract(slots[:cut], back_main, 0, 0) + contract(slots[cut:], back_extra, 0, 0)
    moe_grad = gate_score * back_rows
    grad_hidden = cotangent.astype(F32) + norm_back(normed_two, inverse_two, moe_grad)
    grad_hidden_b = grad_hidden.astype(BF16)
    hidden_both = jnp.concatenate([grad_hidden_b, swap(grad_hidden_b, "c")], axis=0)
    grad_context = jnp.einsum(
        "td,hdc->thc", grad_hidden_b, out_blocks, preferred_element_type=F32
    )
    grad_context_b = grad_context.astype(BF16)
    grad_attention = jnp.einsum(
        "qhc,kc->hqk", grad_context_b, value_rows, preferred_element_type=F32
    )
    grad_value = jnp.einsum("hqk,qhc->kc", attention_b, grad_context_b, preferred_element_type=F32)
    grad_scores = (
        attention
        * (grad_attention - jnp.sum(grad_attention * attention, axis=2, keepdims=True))
        * score_scale
    )
    grad_scores_b = grad_scores.astype(BF16)
    grad_query = jnp.einsum("hqk,kc->qhc", grad_scores_b, key_rows, preferred_element_type=F32)
    grad_key = jnp.einsum("hqk,qhc->kc", grad_scores_b, queries, preferred_element_type=F32)
    grad_qkv = jnp.concatenate([grad_query, grad_key[:, None], grad_value[:, None]], axis=1).astype(BF16)
    grads_flat = grad_qkv.reshape(seq_len, (HEADS + 2) * head_dim)
    grads_both = jnp.concatenate([grads_flat, swap(grads_flat, "c")], axis=0)
    core = lax.axis_index("c").astype(jnp.int32).reshape(1)
    terms = param_terms(
        core, normed_both, hidden_both, grads_both, context_both, (seq_len * devices) ** (-0.5), head_dim
    )
    attn_grad = jnp.sum(exchange(terms, CHIPS).astype(F32), axis=0)
    grad_normed = jnp.einsum("tjc,jdc->td", grad_qkv, project, preferred_element_type=F32)
    grad_tokens = (grad_hidden + norm_back(normed_one, inverse_one, grad_normed)).astype(BF16)
    return (grad_tokens, attn_grad)


def solution(mesh):
    fine = Mesh(mesh.devices.reshape(SIZES), AXES)
    rows = P(AXES, None)
    in_specs = (
        rows,
        P(DP, None),
        rows,
        rows,
        P(EX, None, None, DP),
        P(EX, DP, None),
        rows,
    )
    return jax.shard_map(
        per_device, mesh=fine, in_specs=in_specs, out_specs=(rows, rows), check_vma=False
    )
```

```python
import jax
import jax.numpy as jnp
from jax import lax
from jax.experimental import pallas as pl
from jax.experimental.pallas import tpu as pltpu
from jax.sharding import Mesh, PartitionSpec as P

EPSILON = 1e-05
MASKED = -1e30
AXES = ("z", "yh", "x", "yl", "c")
DP = ("z", "yh")
EX = ("x", "yl", "c")
CHIPS = ("z", "yh", "x", "yl")
SIZES = (4, 2, 4, 2, 2)
EXPERTS = 16
N_DP = 8
CAP = 10
MAIN = 8
HEADS = 2
HALF = 96
PADDED = 768
F32 = jnp.float32
BF16 = jnp.bfloat16


def layer_norm(values):
    widened = values.astype(F32)
    center = widened - jnp.mean(widened, axis=-1, keepdims=True)
    inverse = lax.rsqrt(jnp.mean(center * center, axis=-1, keepdims=True) + EPSILON)
    return (center * inverse, inverse)


def norm_back(normed, inverse, upstream):
    mean_grad = jnp.mean(upstream, axis=-1, keepdims=True)
    mean_proj = jnp.mean(upstream * normed, axis=-1, keepdims=True)
    return inverse * (upstream - mean_grad - normed * mean_proj)


def contract(first_op, second_op, first_dim, second_dim):
    return lax.dot_general(
        first_op,
        second_op,
        (((first_dim,), (second_dim,)), ((), ())),
        preferred_element_type=F32,
    )


def swap(values, axis):
    return lax.ppermute(values, axis, [(0, 1), (1, 0)])


def along_z(values, shift):
    return lax.ppermute(values, "z", [(i, (i + shift) % 4) for i in range(4)])


def exchange(blocks, axes):
    return lax.all_to_all(blocks, axes, split_axis=0, concat_axis=0, tiled=True)


def after(value, *earlier):
    return lax.optimization_barrier((value,) + earlier)[0]


def add_round(first, *others):
    total = first.astype(F32)
    for other in others:
        total = total + other.astype(F32)
    return total.astype(BF16)


def slot_matrix(expert_ids, seq_len):
    flat = expert_ids.reshape(-1)
    one_hot = (flat[:, None] == jnp.arange(EXPERTS, dtype=jnp.int32)[None, :]).astype(F32)
    rows = jnp.arange(seq_len)
    earlier = (rows[:, None] > rows[None, :]).astype(F32)
    before = jnp.dot(earlier, one_hot, preferred_element_type=F32)
    position = jnp.sum(before * one_hot, axis=1).astype(jnp.int32)
    rest = CAP - MAIN
    target = jnp.where(
        position < MAIN, flat * MAIN + position, EXPERTS * MAIN + flat * rest + position - MAIN
    )
    return (jnp.arange(EXPERTS * CAP, dtype=jnp.int32)[:, None] == target[None, :]).astype(BF16)


def place_kernel(places, piece, at_ref, *refs):
    block_refs, out_ref, sems = refs[: len(places)], refs[-2], refs[-1]
    copies = []
    number = 0
    for ref, parts in zip(block_refs, places):
        for i, (s, r, half) in enumerate(parts):
            z = lax.rem(at_ref[0] - s + 4, 4)
            yh = lax.rem(at_ref[1] + r, 2)
            copy = pltpu.make_async_copy(
                ref.at[pl.ds(i * piece, piece)], out_ref.at[z * 2 + yh, pl.ds(half * piece, piece)], sems.at[number]
            )
            copy.start()
            copies.append(copy)
            number += 1
    for copy in copies:
        copy.wait()


def gather_params(attn_param, earlier):
    rows, head_dim = attn_param.shape
    half = rows // 2
    piece = half // 2
    core = lax.axis_index("c")
    own = lax.dynamic_slice_in_dim(attn_param, core * half, half, 0)
    first, second = own[:piece], own[piece:]
    around = [along_z(first, s) for s in (1, 3, 2)]
    own_y = swap(own, "yh")
    pair = after(jnp.concatenate([second, own_y[piece:]], axis=0), around[0], around[1])
    earlier = after(earlier, own_y, *around)
    around_y = [swap(block, "yh") for block in around]
    pairs = [along_z(pair, s) for s in (1, 3, 2)]
    blocks = [own, own_y] + around + around_y + pairs
    places = (
        [[(0, 0, 0), (0, 0, 1)], [(0, 1, 0), (0, 1, 1)]]
        + [[(s, 0, 0)] for s in (1, 3, 2)]
        + [[(s, 1, 0)] for s in (1, 3, 2)]
        + [[(s, 0, 1), (s, 1, 1)] for s in (1, 3, 2)]
    )
    at = after(jnp.stack([lax.axis_index("z"), lax.axis_index("yh")]).astype(jnp.int32), earlier)
    anywhere = pl.BlockSpec(memory_space=pl.ANY)
    own = pl.pallas_call(
        lambda *refs: place_kernel(places, piece, *refs),
        out_shape=jax.ShapeDtypeStruct((N_DP, half, head_dim), BF16),
        in_specs=[pl.BlockSpec(memory_space=pltpu.SMEM)] + [anywhere] * len(blocks),
        out_specs=pl.BlockSpec(memory_space=pltpu.VMEM),
        scratch_shapes=[pltpu.SemaphoreType.DMA((16,))],
        compiler_params=pltpu.CompilerParams(vmem_limit_bytes=60 * 1024 * 1024),
    )(at, *blocks)
    other = swap(own, "c")
    first = jnp.where(core == 0, own, other)
    second = jnp.where(core == 0, other, own)
    return jnp.stack([first, second], axis=1).reshape(N_DP * rows, head_dim), earlier


def between_experts(rows):
    features = rows.shape[1]
    cut = EXPERTS * MAIN
    extra = rows[cut:].reshape(cut, -1)
    packed = jnp.concatenate([rows[:cut], extra], axis=1)
    width = packed.shape[1]
    packed = exchange(packed.reshape(EXPERTS, MAIN, width), EX).reshape(cut, width)
    extra = packed[:, features:].reshape(-1, features)
    return packed[:, :features], extra


def spread_near(own):
    one = own[:HALF]
    own_y = swap(own, "yh")
    return [own, own_y] + [along_z(one, s) for s in (1, 3, 2)]


def spread_far(near, between):
    own, own_y, near_z, far_z, across = near
    pair = after(jnp.concatenate([own[HALF:], own_y[HALF:]], axis=0), near_z, far_z)
    first = [swap(near_z, "yh"), swap(far_z, "yh")]
    second = [along_z(pair, 1), along_z(pair, 3)]
    return first + [swap(after(across, *between), "yh")] + second + [along_z(pair, 2)]


def collect(near, far):
    kept, one_y, two_y, *one_z = near
    early = [along_z(block, -s) for block, s in zip(one_z, (1, 3, 2))]
    early_y = swap(two_y, "yh")
    *one_yz, two_z, two_yz = far
    (*one_yz, two_yz), early, early_y = lax.optimization_barrier(([*one_yz, two_yz], early, early_y))
    late = [along_z(block, -s) for block, s in zip(one_yz, (1, 3, 2))]
    swapped = swap(two_yz, "yh")
    across = swap(add_round(one_y, *late), "yh")
    pairs = add_round(two_z, swapped)
    rest = kept.shape[0] - HALF
    back = [along_z(pairs[i * rest : (i + 1) * rest], -s) for i, s in enumerate((1, 3, 2))]
    one = add_round(kept[:HALF], across, *early)
    two = add_round(kept[HALF:], early_y, *back)
    return jnp.concatenate([one, two], axis=0)


def expert_kernel(counts, sources, pieces_out, at_ref, cot_ref, *refs):
    count = len(counts)
    outs = len(pieces_out)
    normed_refs = refs[:count]
    inner_ref, outer_ref = refs[count : count + 2]
    out_refs = refs[count + 2 : count + 2 + outs]
    (normed, cot, gate_map, up_map, outer_map, grad_gate, grad_up, result, row_sem, cot_sem, map_sem, out_sem) = refs[
        count + 2 + outs :
    ]
    hidden, features = outer_ref.shape
    starts = [sum(counts[:i]) for i in range(count)]

    def load(source, target, sem):
        copy = pltpu.make_async_copy(source, target, sem)
        copy.start()
        return copy

    pieces = [(0, 256), (256, 256), (512, hidden - 512)]

    def load_maps(i):
        at = pl.ds(*pieces[i])
        return [
            load(inner_ref.at[0, at], gate_map.at[at], map_sem.at[0, i]),
            load(inner_ref.at[1, at], up_map.at[at], map_sem.at[1, i]),
            load(outer_ref.at[at], outer_map.at[at], map_sem.at[2, i]),
        ]

    rows_in = [
        load(ref, normed.at[pl.ds(starts[i], counts[i])], row_sem.at[i]) for i, ref in enumerate(normed_refs)
    ]
    maps_in = load_maps(0)
    cots_in = []
    at = 0
    for j, (s, r, start, size) in enumerate(sources):
        device = lax.rem(at_ref[0] - s + 4, 4) * 2 + lax.rem(at_ref[1] + r, 2)
        cots_in.append(load(cot_ref.at[device, pl.ds(start, size)], cot.at[pl.ds(at, size)], cot_sem.at[j]))
        at += size
    blank = jnp.zeros((PADDED - hidden, features), BF16)
    for ref in (gate_map, up_map, outer_map):
        ref[pl.ds(hidden, PADDED - hidden)] = blank
    for copy in rows_in:
        copy.wait()

    for i in range(len(pieces)):
        gate_in, up_in, outer_in = maps_in
        at = pl.ds(i * 256, 256)
        gate_in.wait()
        if i + 1 < len(pieces):
            maps_in = load_maps(i + 1)
        gate_part = contract(normed[...], gate_map[at], 1, 1)
        up_in.wait()
        up_part = contract(normed[...], up_map[at], 1, 1)
        if i == 0:
            for copy in cots_in:
                copy.wait()
        outer_in.wait()
        grad_act = contract(cot[...], outer_map[at], 1, 1)
        squash = 1.0 / (1.0 + jnp.exp(-gate_part))
        scaled = grad_act * squash
        grad_gate[:, at] = (scaled * up_part * (1.0 + gate_part * (1.0 - squash))).astype(BF16)
        grad_up[:, at] = (scaled * gate_part).astype(BF16)

    wide = 512
    copies = []
    for n in range(features // wide):
        lanes = pl.ds(n * wide, wide)

        result[:, lanes] = (
            contract(grad_gate[...], gate_map[:, lanes], 1, 0) + contract(grad_up[...], up_map[:, lanes], 1, 0)
        ).astype(BF16)
        number = 0
        for ref, parts in zip(out_refs, pieces_out):
            at = 0
            for start, size in parts:
                copies.append(
                    load(
                        result.at[pl.ds(start, size), lanes],
                        ref.at[pl.ds(at, size), lanes],
                        out_sem.at[n, number],
                    )
                )
                at += size
                number += 1
    for copy in copies:
        copy.wait()


def experts(at, normed_blocks, cot, sources, inner, outer, pieces_out):
    counts = [block.shape[0] for block in normed_blocks]
    features = normed_blocks[0].shape[1]
    hidden = outer.shape[0]
    total = sum(counts)
    anywhere = pl.BlockSpec(memory_space=pl.ANY)
    return pl.pallas_call(
        lambda *refs: expert_kernel(counts, sources, pieces_out, *refs),
        out_shape=[
            jax.ShapeDtypeStruct((sum(size for _, size in parts), features), BF16) for parts in pieces_out
        ],
        in_specs=[pl.BlockSpec(memory_space=pltpu.SMEM)] + [anywhere] * (len(counts) + 3),
        out_specs=[anywhere] * len(pieces_out),
        scratch_shapes=[
            pltpu.VMEM((total, features), BF16),
            pltpu.VMEM((total, features), BF16),
            pltpu.VMEM((PADDED, features), BF16),
            pltpu.VMEM((PADDED, features), BF16),
            pltpu.VMEM((PADDED, features), BF16),
            pltpu.VMEM((total, PADDED), BF16),
            pltpu.VMEM((total, PADDED), BF16),
            pltpu.VMEM((total, features), BF16),
            pltpu.SemaphoreType.DMA((len(counts),)),
            pltpu.SemaphoreType.DMA((len(sources),)),
            pltpu.SemaphoreType.DMA((3, 3)),
            pltpu.SemaphoreType.DMA((features // 512, sum(len(parts) for parts in pieces_out))),
        ],
        compiler_params=pltpu.CompilerParams(vmem_limit_bytes=60 * 1024 * 1024),
        cost_estimate=pl.CostEstimate(
            flops=10 * total * features * hidden,
            bytes_accessed=6 * total * features + 6 * hidden * features,
            transcendentals=total * hidden,
        ),
    )(at, cot, *normed_blocks, inner, outer)


def param_kernel(scale, head_dim, core_ref, normed_ref, hidden_ref, grads_ref, context_ref, out_ref, terms):
    features = normed_ref.shape[1]
    tile = 1024
    for block in range(6):
        left_ref = normed_ref if block < 4 else hidden_ref
        right = (grads_ref[:, block * head_dim : (block + 1) * head_dim] if block < 4
                 else context_ref[:, (block - 4) * head_dim : (block - 3) * head_dim])
        for start in range(0, features, tile):
            part = contract(left_ref[:, start : start + tile], right, 0, 0) * scale
            terms[pl.ds(block * features + start, tile)] = part.astype(BF16)
    core = core_ref[0]

    @pl.loop(0, out_ref.shape[0])
    def _(group):
        size = out_ref.shape[1]
        out_ref[group] = terms[pl.ds(pl.multiple_of((2 * group + core) * size, 16), size)]


def param_terms(core, normed, hidden, grads, context, scale, head_dim):
    features = normed.shape[1]
    rows = 6 * features
    whole = pl.BlockSpec(memory_space=pltpu.VMEM)
    return pl.pallas_call(
        lambda *refs: param_kernel(scale, head_dim, *refs),
        out_shape=jax.ShapeDtypeStruct((64, rows // 128, head_dim), BF16),
        in_specs=[pl.BlockSpec(memory_space=pltpu.SMEM)] + [whole] * 4,
        out_specs=whole,
        scratch_shapes=[pltpu.VMEM((rows, head_dim), BF16)],
        compiler_params=pltpu.CompilerParams(vmem_limit_bytes=40 * 1024 * 1024),
        cost_estimate=pl.CostEstimate(
            flops=2 * rows * head_dim * normed.shape[0], bytes_accessed=8 * 1024 * 1024, transcendentals=0
        ),
    )(core, normed, hidden, grads, context)


def per_device(tokens, attn_param, expert_ids, gate_score, w_in, w_out, cotangent):
    seq_len, features = tokens.shape
    head_dim = attn_param.shape[1]
    score_scale = head_dim ** (-0.5)
    devices = N_DP * EXPERTS
    slots = slot_matrix(expert_ids, seq_len)
    inner = jnp.transpose(w_in[0], (1, 2, 0))
    outer = w_out[0]

    cot_main, cot_extra = between_experts(contract(slots, cotangent, 1, 0).astype(BF16))
    cot_rows = jnp.concatenate([cot_main, cot_extra], axis=0)
    packed, cot_rows = gather_params(attn_param, cot_rows)
    cot = lax.all_gather(cot_rows, DP, axis=0)
    at = jnp.stack([lax.axis_index("z"), lax.axis_index("yh")]).astype(jnp.int32)

    normed_one, inverse_one = layer_norm(tokens)
    normed_one_b = normed_one.astype(BF16)
    normed_both = jnp.concatenate([normed_one_b, swap(normed_one_b, "c")], axis=0)
    blocks = packed.reshape(2 * HEADS + 2, features, head_dim)
    project = blocks[: HEADS + 2]
    out_blocks = blocks[HEADS + 2 :]
    projected = jnp.einsum(
        "td,jdc->tjc", normed_one_b, project, preferred_element_type=F32
    ).astype(BF16)
    queries = projected[:, :HEADS]
    key_rows = projected[:, HEADS]
    value_rows = projected[:, HEADS + 1]
    scores = jnp.einsum("qhc,kc->hqk", queries, key_rows, preferred_element_type=F32) * score_scale
    causal = lax.broadcasted_iota(jnp.int32, (seq_len, seq_len), 0) >= lax.broadcasted_iota(
        jnp.int32, (seq_len, seq_len), 1
    )
    scores = jnp.where(causal[None], scores, MASKED)
    row_max = jnp.max(scores, axis=2, keepdims=True)
    raised = jnp.exp(scores - row_max)
    attention = raised / jnp.sum(raised, axis=2, keepdims=True)
    attention_b = attention.astype(BF16)
    context = jnp.einsum(
        "hqk,kc->qhc", attention_b, value_rows, preferred_element_type=F32
    ).astype(BF16)
    context_flat = context.reshape(seq_len, HEADS * head_dim)
    context_both = jnp.concatenate([context_flat, swap(context_flat, "c")], axis=0)
    attn_out = jnp.einsum("thc,hdc->td", context, out_blocks, preferred_element_type=F32)
    residual = (tokens.astype(F32) + attn_out).astype(BF16)
    normed_two, inverse_two = layer_norm(residual)
    main, extra = between_experts(contract(slots, normed_two.astype(BF16), 1, 0).astype(BF16))
    near = spread_near(jnp.concatenate([main, extra], axis=0))
    near[4], normed_both, context_both = lax.optimization_barrier((near[4], normed_both, context_both))
    h = HALF
    rest = EXPERTS * CAP - h
    whole = EXPERTS * CAP
    near_rows = experts(
        at,
        near,
        cot,
        [(0, 0, 0, whole), (0, 1, 0, whole)] + [(s, 0, 0, h) for s in (1, 3, 2)],
        inner,
        outer,
        [[(0, whole)], [(whole, h)], [(whole + h, rest)]] + [[(2 * whole + i * h, h)] for i in range(3)],
    )
    far = spread_far(near, (near_rows[0],))
    far_rows = experts(
        at,
        far,
        cot,
        [(s, 1, 0, h) for s in (1, 3, 2)] + [(s, r, h, rest) for s in (1, 3, 2) for r in (0, 1)],
        inner,
        outer,
        [[(i * h, h)] for i in range(3)]
        + [[(3 * h + (2 * i + r) * rest, rest) for i in range(3)] for r in (0, 1)],
    )
    back_main, back_extra = between_experts(collect(near_rows, far_rows))
    cut = EXPERTS * MAIN
    back_rows = contract(slots[:cut], back_main, 0, 0) + contract(slots[cut:], back_extra, 0, 0)
    moe_grad = gate_score * back_rows
    grad_hidden = cotangent.astype(F32) + norm_back(normed_two, inverse_two, moe_grad)
    grad_hidden_b = grad_hidden.astype(BF16)
    hidden_both = jnp.concatenate([grad_hidden_b, swap(grad_hidden_b, "c")], axis=0)
    grad_context = jnp.einsum(
        "td,hdc->thc", grad_hidden_b, out_blocks, preferred_element_type=F32
    )
    grad_context_b = grad_context.astype(BF16)
    grad_attention = jnp.einsum(
        "qhc,kc->hqk", grad_context_b, value_rows, preferred_element_type=F32
    )
    grad_value = jnp.einsum("hqk,qhc->kc", attention_b, grad_context_b, preferred_element_type=F32)
    grad_scores = (
        attention
        * (grad_attention - jnp.sum(grad_attention * attention, axis=2, keepdims=True))
        * score_scale
    )
    grad_scores_b = grad_scores.astype(BF16)
    grad_query = jnp.einsum("hqk,kc->qhc", grad_scores_b, key_rows, preferred_element_type=F32)
    grad_key = jnp.einsum("hqk,qhc->kc", grad_scores_b, queries, preferred_element_type=F32)
    grad_qkv = jnp.concatenate([grad_query, grad_key[:, None], grad_value[:, None]], axis=1).astype(BF16)
    grads_flat = grad_qkv.reshape(seq_len, (HEADS + 2) * head_dim)
    grads_both = jnp.concatenate([grads_flat, swap(grads_flat, "c")], axis=0)
    core = lax.axis_index("c").astype(jnp.int32).reshape(1)
    terms = param_terms(
        core, normed_both, hidden_both, grads_both, context_both, (seq_len * devices) ** (-0.5), head_dim
    )
    attn_grad = jnp.sum(exchange(terms, CHIPS).astype(F32), axis=0)
    grad_normed = jnp.einsum("tjc,jdc->td", grad_qkv, project, preferred_element_type=F32)
    grad_tokens = (grad_hidden + norm_back(normed_one, inverse_one, grad_normed)).astype(BF16)
    return (grad_tokens, attn_grad)


def solution(mesh):
    fine = Mesh(mesh.devices.reshape(SIZES), AXES)
    rows = P(AXES, None)
    in_specs = (
        rows,
        P(DP, None),
        rows,
        rows,
        P(EX, None, None, DP),
        P(EX, DP, None),
        rows,
    )
    return jax.shard_map(
        per_device, mesh=fine, in_specs=in_specs, out_specs=(rows, rows), check_vma=False
    )
```

```python
import jax
import jax.numpy as jnp
from jax import lax
from jax.experimental import pallas as pl
from jax.experimental.pallas import tpu as pltpu
from jax.sharding import Mesh, PartitionSpec as P

EPSILON = 1e-05
MASKED = -1e30
AXES = ("z", "yh", "x", "yl", "c")
DP = ("z", "yh")
EX = ("x", "yl", "c")
CHIPS = ("z", "yh", "x", "yl")
SIZES = (4, 2, 4, 2, 2)
EXPERTS = 16
N_DP = 8
CAP = 10
MAIN = 8
HEADS = 2
HALF = 96
PADDED = 768
F32 = jnp.float32
BF16 = jnp.bfloat16


def layer_norm(values):
    widened = values.astype(F32)
    center = widened - jnp.mean(widened, axis=-1, keepdims=True)
    inverse = lax.rsqrt(jnp.mean(center * center, axis=-1, keepdims=True) + EPSILON)
    return (center * inverse, inverse)


def norm_back(normed, inverse, upstream):
    mean_grad = jnp.mean(upstream, axis=-1, keepdims=True)
    mean_proj = jnp.mean(upstream * normed, axis=-1, keepdims=True)
    return inverse * (upstream - mean_grad - normed * mean_proj)


def contract(first_op, second_op, first_dim, second_dim):
    return lax.dot_general(
        first_op,
        second_op,
        (((first_dim,), (second_dim,)), ((), ())),
        preferred_element_type=F32,
    )


def swap(values, axis):
    return lax.ppermute(values, axis, [(0, 1), (1, 0)])


def along_z(values, shift):
    return lax.ppermute(values, "z", [(i, (i + shift) % 4) for i in range(4)])


def exchange(blocks, axes):
    return lax.all_to_all(blocks, axes, split_axis=0, concat_axis=0, tiled=True)


def after(value, *earlier):
    return lax.optimization_barrier((value,) + earlier)[0]


def add_round(first, *others):
    total = first.astype(F32)
    for other in others:
        total = total + other.astype(F32)
    return total.astype(BF16)


def slot_matrix(expert_ids, seq_len):
    flat = expert_ids.reshape(-1)
    one_hot = (flat[:, None] == jnp.arange(EXPERTS, dtype=jnp.int32)[None, :]).astype(F32)
    rows = jnp.arange(seq_len)
    earlier = (rows[:, None] > rows[None, :]).astype(F32)
    before = jnp.dot(earlier, one_hot, preferred_element_type=F32)
    position = jnp.sum(before * one_hot, axis=1).astype(jnp.int32)
    rest = CAP - MAIN
    target = jnp.where(
        position < MAIN, flat * MAIN + position, EXPERTS * MAIN + flat * rest + position - MAIN
    )
    return (jnp.arange(EXPERTS * CAP, dtype=jnp.int32)[:, None] == target[None, :]).astype(BF16)


def place_kernel(places, piece, at_ref, *refs):
    block_refs, out_ref, sems = refs[: len(places)], refs[-2], refs[-1]
    copies = []
    number = 0
    for ref, parts in zip(block_refs, places):
        for i, (s, r, half) in enumerate(parts):
            z = lax.rem(at_ref[0] - s + 4, 4)
            yh = lax.rem(at_ref[1] + r, 2)
            copy = pltpu.make_async_copy(
                ref.at[pl.ds(i * piece, piece)], out_ref.at[z * 2 + yh, pl.ds(half * piece, piece)], sems.at[number]
            )
            copy.start()
            copies.append(copy)
            number += 1
    for copy in copies:
        copy.wait()


def gather_params(attn_param, earlier):
    rows, head_dim = attn_param.shape
    half = rows // 2
    piece = half // 2
    core = lax.axis_index("c")
    own = lax.dynamic_slice_in_dim(attn_param, core * half, half, 0)
    first, second = own[:piece], own[piece:]
    around = [along_z(first, s) for s in (1, 3, 2)]
    own_y = swap(own, "yh")
    pair = after(jnp.concatenate([second, own_y[piece:]], axis=0), around[0], around[1])
    earlier = after(earlier, own_y, *around)
    around_y = [swap(block, "yh") for block in around]
    pairs = [along_z(pair, s) for s in (1, 3, 2)]
    blocks = [own, own_y] + around + around_y + pairs
    places = (
        [[(0, 0, 0), (0, 0, 1)], [(0, 1, 0), (0, 1, 1)]]
        + [[(s, 0, 0)] for s in (1, 3, 2)]
        + [[(s, 1, 0)] for s in (1, 3, 2)]
        + [[(s, 0, 1), (s, 1, 1)] for s in (1, 3, 2)]
    )
    spread = spread_near(earlier)
    at = jnp.stack([lax.axis_index("z"), lax.axis_index("yh")]).astype(jnp.int32)
    at = after(at, *spread[1:4])
    anywhere = pl.BlockSpec(memory_space=pl.ANY)
    own = pl.pallas_call(
        lambda *refs: place_kernel(places, piece, *refs),
        out_shape=jax.ShapeDtypeStruct((N_DP, half, head_dim), BF16),
        in_specs=[pl.BlockSpec(memory_space=pltpu.SMEM)] + [anywhere] * len(blocks),
        out_specs=pl.BlockSpec(memory_space=pltpu.VMEM),
        scratch_shapes=[pltpu.SemaphoreType.DMA((16,))],
        compiler_params=pltpu.CompilerParams(vmem_limit_bytes=60 * 1024 * 1024),
    )(at, *blocks)
    other = swap(own, "c")
    first = jnp.where(core == 0, own, other)
    second = jnp.where(core == 0, other, own)
    return jnp.stack([first, second], axis=1).reshape(N_DP * rows, head_dim), spread


def between_experts(rows):
    features = rows.shape[1]
    cut = EXPERTS * MAIN
    extra = rows[cut:].reshape(cut, -1)
    packed = jnp.concatenate([rows[:cut], extra], axis=1)
    width = packed.shape[1]
    packed = exchange(packed.reshape(EXPERTS, MAIN, width), EX).reshape(cut, width)
    extra = packed[:, features:].reshape(-1, features)
    return packed[:, :features], extra


def spread_near(own):
    one = own[:HALF]
    own_y = swap(own, "yh")
    return [own, own_y] + [along_z(one, s) for s in (1, 3, 2)]


def spread_far(near, between):
    own, own_y, near_z, far_z, across = near
    pair = after(jnp.concatenate([own[HALF:], own_y[HALF:]], axis=0), near_z, far_z)
    first = [swap(near_z, "yh"), swap(far_z, "yh")]
    second = [along_z(pair, 1), along_z(pair, 3)]
    return first + [swap(after(across, *between), "yh")] + second + [along_z(pair, 2)]


def collect(near, far):
    kept, one_y, two_y, *one_z = near
    early = [along_z(block, -s) for block, s in zip(one_z, (1, 3, 2))]
    early_y = swap(two_y, "yh")
    *one_yz, two_z, two_yz = far
    (*one_yz, two_yz), early, early_y = lax.optimization_barrier(([*one_yz, two_yz], early, early_y))
    late = [along_z(block, -s) for block, s in zip(one_yz, (1, 3, 2))]
    swapped = swap(two_yz, "yh")
    across = swap(add_round(one_y, *late), "yh")
    pairs = add_round(two_z, swapped)
    rest = kept.shape[0] - HALF
    back = [along_z(pairs[i * rest : (i + 1) * rest], -s) for i, s in enumerate((1, 3, 2))]
    one = add_round(kept[:HALF], across, *early)
    two = add_round(kept[HALF:], early_y, *back)
    return jnp.concatenate([one, two], axis=0)


def expert_kernel(counts, pieces_out, tall, *refs):
    count = len(counts)
    outs = len(pieces_out)
    normed_refs, cot_refs = refs[:count], refs[count : 2 * count]
    inner_ref, outer_ref = refs[2 * count : 2 * count + 2]
    out_refs = refs[2 * count + 2 : 2 * count + 2 + outs]
    (normed, cot, gate_map, up_map, outer_map, grad_gate, grad_up, result, row_sem, map_sem, out_sem) = refs[
        2 * count + 2 + outs :
    ]
    hidden, features = outer_ref.shape
    starts = [sum(counts[:i]) for i in range(count)]

    def load(source, target, sem):
        copy = pltpu.make_async_copy(source, target, sem)
        copy.start()
        return copy

    def load_rows(block_refs, target, side):
        return [
            load(ref, target.at[pl.ds(starts[i], counts[i])], row_sem.at[side, i])
            for i, ref in enumerate(block_refs)
        ]

    pieces = [(0, 256), (256, 256), (512, hidden - 512)]
    rows_in = load_rows(normed_refs, normed, 0)
    maps_in = []
    for i, (start, size) in enumerate(pieces):
        at = pl.ds(start, size)
        maps_in.append(
            [
                load(inner_ref.at[0, at], gate_map.at[at], map_sem.at[0, i]),
                load(inner_ref.at[1, at], up_map.at[at], map_sem.at[1, i]),
                load(outer_ref.at[at], outer_map.at[at], map_sem.at[2, i]),
            ]
        )
        if i == 0:
            rows_in += load_rows(cot_refs, cot, 1)
    blank = jnp.zeros((PADDED - hidden, features), BF16)
    for ref in (gate_map, up_map, outer_map):
        ref[pl.ds(hidden, PADDED - hidden)] = blank
    for copy in rows_in:
        copy.wait()
    steps = sum(counts) // tall

    for i in range(len(pieces)):
        for copy in maps_in[i]:
            copy.wait()
        at = pl.ds(i * 256, 256)

        @pl.loop(0, steps)
        def _(step):
            here = pl.ds(pl.multiple_of(step * tall, 16), tall)
            gate_part = contract(normed[here], gate_map[at], 1, 1)
            up_part = contract(normed[here], up_map[at], 1, 1)
            grad_act = contract(cot[here], outer_map[at], 1, 1)
            squash = 1.0 / (1.0 + jnp.exp(-gate_part))
            scaled = grad_act * squash
            grad_gate[here, at] = (scaled * up_part * (1.0 + gate_part * (1.0 - squash))).astype(BF16)
            grad_up[here, at] = (scaled * gate_part).astype(BF16)

    wide = 512
    copies = []
    for n in range(features // wide):
        lanes = pl.ds(n * wide, wide)

        @pl.loop(0, steps)
        def _(step):
            here = pl.ds(pl.multiple_of(step * tall, 16), tall)
            result[here, lanes] = (
                contract(grad_gate[here], gate_map[:, lanes], 1, 0)
                + contract(grad_up[here], up_map[:, lanes], 1, 0)
            ).astype(BF16)

        number = 0
        for ref, parts in zip(out_refs, pieces_out):
            at = 0
            for start, size in parts:
                copies.append(
                    load(
                        result.at[pl.ds(start, size), lanes],
                        ref.at[pl.ds(at, size), lanes],
                        out_sem.at[n, number],
                    )
                )
                at += size
                number += 1
    for copy in copies:
        copy.wait()


def experts(normed_blocks, cot_blocks, inner, outer, pieces_out, tall):
    counts = [block.shape[0] for block in normed_blocks]
    features = normed_blocks[0].shape[1]
    hidden = outer.shape[0]
    total = sum(counts)
    anywhere = pl.BlockSpec(memory_space=pl.ANY)
    return pl.pallas_call(
        lambda *refs: expert_kernel(counts, pieces_out, tall, *refs),
        out_shape=[
            jax.ShapeDtypeStruct((sum(size for _, size in parts), features), BF16) for parts in pieces_out
        ],
        in_specs=[anywhere] * (2 * len(counts) + 2),
        out_specs=[anywhere] * len(pieces_out),
        scratch_shapes=[
            pltpu.VMEM((total, features), BF16),
            pltpu.VMEM((total, features), BF16),
            pltpu.VMEM((PADDED, features), BF16),
            pltpu.VMEM((PADDED, features), BF16),
            pltpu.VMEM((PADDED, features), BF16),
            pltpu.VMEM((total, PADDED), BF16),
            pltpu.VMEM((total, PADDED), BF16),
            pltpu.VMEM((total, features), BF16),
            pltpu.SemaphoreType.DMA((2, len(counts))),
            pltpu.SemaphoreType.DMA((3, 3)),
            pltpu.SemaphoreType.DMA((features // 512, sum(len(parts) for parts in pieces_out))),
        ],
        compiler_params=pltpu.CompilerParams(vmem_limit_bytes=60 * 1024 * 1024),
        cost_estimate=pl.CostEstimate(
            flops=10 * total * features * hidden,
            bytes_accessed=6 * total * features + 6 * hidden * features,
            transcendentals=total * hidden,
        ),
    )(*normed_blocks, *cot_blocks, inner, outer)


def param_kernel(scale, head_dim, core_ref, normed_ref, hidden_ref, grads_ref, context_ref, out_ref, terms):
    features = normed_ref.shape[1]
    tile = 1024
    for block in range(6):
        left_ref = normed_ref if block < 4 else hidden_ref
        right = (grads_ref[:, block * head_dim : (block + 1) * head_dim] if block < 4
                 else context_ref[:, (block - 4) * head_dim : (block - 3) * head_dim])
        for start in range(0, features, tile):
            part = contract(left_ref[:, start : start + tile], right, 0, 0) * scale
            terms[pl.ds(block * features + start, tile)] = part.astype(BF16)
    core = core_ref[0]

    @pl.loop(0, out_ref.shape[0])
    def _(group):
        size = out_ref.shape[1]
        out_ref[group] = terms[pl.ds(pl.multiple_of((2 * group + core) * size, 16), size)]


def param_terms(core, normed, hidden, grads, context, scale, head_dim):
    features = normed.shape[1]
    rows = 6 * features
    whole = pl.BlockSpec(memory_space=pltpu.VMEM)
    return pl.pallas_call(
        lambda *refs: param_kernel(scale, head_dim, *refs),
        out_shape=jax.ShapeDtypeStruct((64, rows // 128, head_dim), BF16),
        in_specs=[pl.BlockSpec(memory_space=pltpu.SMEM)] + [whole] * 4,
        out_specs=whole,
        scratch_shapes=[pltpu.VMEM((rows, head_dim), BF16)],
        compiler_params=pltpu.CompilerParams(vmem_limit_bytes=40 * 1024 * 1024),
        cost_estimate=pl.CostEstimate(
            flops=2 * rows * head_dim * normed.shape[0], bytes_accessed=8 * 1024 * 1024, transcendentals=0
        ),
    )(core, normed, hidden, grads, context)


def per_device(tokens, attn_param, expert_ids, gate_score, w_in, w_out, cotangent):
    seq_len, features = tokens.shape
    head_dim = attn_param.shape[1]
    score_scale = head_dim ** (-0.5)
    devices = N_DP * EXPERTS
    slots = slot_matrix(expert_ids, seq_len)
    inner = jnp.transpose(w_in[0], (1, 2, 0))
    outer = w_out[0]

    cot_main, cot_extra = between_experts(contract(slots, cotangent, 1, 0).astype(BF16))
    cot_rows = jnp.concatenate([cot_main, cot_extra], axis=0)
    packed, cot_near = gather_params(attn_param, cot_rows)
    cot_far = spread_far(cot_near, ())

    normed_one, inverse_one = layer_norm(tokens)
    normed_one_b = normed_one.astype(BF16)
    normed_both = jnp.concatenate([normed_one_b, swap(normed_one_b, "c")], axis=0)
    blocks = packed.reshape(2 * HEADS + 2, features, head_dim)
    project = blocks[: HEADS + 2]
    out_blocks = blocks[HEADS + 2 :]
    projected = jnp.einsum(
        "td,jdc->tjc", normed_one_b, project, preferred_element_type=F32
    ).astype(BF16)
    queries = projected[:, :HEADS]
    key_rows = projected[:, HEADS]
    value_rows = projected[:, HEADS + 1]
    scores = jnp.einsum("qhc,kc->hqk", queries, key_rows, preferred_element_type=F32) * score_scale
    causal = lax.broadcasted_iota(jnp.int32, (seq_len, seq_len), 0) >= lax.broadcasted_iota(
        jnp.int32, (seq_len, seq_len), 1
    )
    scores = jnp.where(causal[None], scores, MASKED)
    row_max = jnp.max(scores, axis=2, keepdims=True)
    raised = jnp.exp(scores - row_max)
    attention = raised / jnp.sum(raised, axis=2, keepdims=True)
    attention_b = attention.astype(BF16)
    context = jnp.einsum(
        "hqk,kc->qhc", attention_b, value_rows, preferred_element_type=F32
    ).astype(BF16)
    context_flat = context.reshape(seq_len, HEADS * head_dim)
    context_both = jnp.concatenate([context_flat, swap(context_flat, "c")], axis=0)
    attn_out = jnp.einsum("thc,hdc->td", context, out_blocks, preferred_element_type=F32)
    residual = (tokens.astype(F32) + attn_out).astype(BF16)
    normed_two, inverse_two = layer_norm(residual)
    normed_two_b = after(normed_two.astype(BF16), cot_near[4], cot_far[0], cot_far[3], cot_far[4])
    main, extra = between_experts(contract(slots, normed_two_b, 1, 0).astype(BF16))
    own = after(jnp.concatenate([main, extra], axis=0), cot_far[1], cot_far[2], cot_far[5])
    near = spread_near(own)
    near[4], normed_both, context_both = lax.optimization_barrier((near[4], normed_both, context_both))
    h = HALF
    whole = EXPERTS * CAP
    rest = whole - h
    near_rows = experts(
        near,
        cot_near,
        inner,
        outer,
        [[(0, whole)], [(whole, h)], [(whole + h, rest)]] + [[(2 * whole + i * h, h)] for i in range(3)],
        2 * whole + 3 * h,
    )
    far = spread_far(near, (near_rows[0],))
    far_rows = experts(
        far,
        cot_far,
        inner,
        outer,
        [[(i * h, h)] for i in range(3)]
        + [[(3 * h + (2 * i + r) * rest, rest) for i in range(3)] for r in (0, 1)],
        (h + 2 * rest) * 3 // 2,
    )
    back_main, back_extra = between_experts(collect(near_rows, far_rows))
    cut = EXPERTS * MAIN
    back_rows = contract(slots[:cut], back_main, 0, 0) + contract(slots[cut:], back_extra, 0, 0)
    moe_grad = gate_score * back_rows
    grad_hidden = cotangent.astype(F32) + norm_back(normed_two, inverse_two, moe_grad)
    grad_hidden_b = grad_hidden.astype(BF16)
    hidden_both = jnp.concatenate([grad_hidden_b, swap(grad_hidden_b, "c")], axis=0)
    grad_context = jnp.einsum(
        "td,hdc->thc", grad_hidden_b, out_blocks, preferred_element_type=F32
    )
    grad_context_b = grad_context.astype(BF16)
    grad_attention = jnp.einsum(
        "qhc,kc->hqk", grad_context_b, value_rows, preferred_element_type=F32
    )
    grad_value = jnp.einsum("hqk,qhc->kc", attention_b, grad_context_b, preferred_element_type=F32)
    grad_scores = (
        attention
        * (grad_attention - jnp.sum(grad_attention * attention, axis=2, keepdims=True))
        * score_scale
    )
    grad_scores_b = grad_scores.astype(BF16)
    grad_query = jnp.einsum("hqk,kc->qhc", grad_scores_b, key_rows, preferred_element_type=F32)
    grad_key = jnp.einsum("hqk,qhc->kc", grad_scores_b, queries, preferred_element_type=F32)
    grad_qkv = jnp.concatenate([grad_query, grad_key[:, None], grad_value[:, None]], axis=1).astype(BF16)
    grads_flat = grad_qkv.reshape(seq_len, (HEADS + 2) * head_dim)
    grads_both = jnp.concatenate([grads_flat, swap(grads_flat, "c")], axis=0)
    core = lax.axis_index("c").astype(jnp.int32).reshape(1)
    terms = param_terms(
        core, normed_both, hidden_both, grads_both, context_both, (seq_len * devices) ** (-0.5), head_dim
    )
    attn_grad = jnp.sum(exchange(terms, CHIPS).astype(F32), axis=0)
    grad_normed = jnp.einsum("tjc,jdc->td", grad_qkv, project, preferred_element_type=F32)
    grad_tokens = (grad_hidden + norm_back(normed_one, inverse_one, grad_normed)).astype(BF16)
    return (grad_tokens, attn_grad)


def solution(mesh):
    fine = Mesh(mesh.devices.reshape(SIZES), AXES)
    rows = P(AXES, None)
    in_specs = (
        rows,
        P(DP, None),
        rows,
        rows,
        P(EX, None, None, DP),
        P(EX, DP, None),
        rows,
    )
    return jax.shard_map(
        per_device, mesh=fine, in_specs=in_specs, out_specs=(rows, rows), check_vma=False
    )
```

```python
import jax
import jax.numpy as jnp
from jax import lax
from jax.experimental import pallas as pl
from jax.experimental.pallas import tpu as pltpu
from jax.sharding import Mesh, PartitionSpec as P

EPSILON = 1e-05
MASKED = -1e30
AXES = ("z", "yh", "x", "yl", "c")
DP = ("z", "yh")
EX = ("x", "yl", "c")
CHIPS = ("z", "yh", "x", "yl")
SIZES = (4, 2, 4, 2, 2)
EXPERTS = 16
N_DP = 8
CAP = 10
MAIN = 8
HEADS = 2
HALF = 96
PADDED = 768
F32 = jnp.float32
BF16 = jnp.bfloat16


def layer_norm(values):
    widened = values.astype(F32)
    center = widened - jnp.mean(widened, axis=-1, keepdims=True)
    inverse = lax.rsqrt(jnp.mean(center * center, axis=-1, keepdims=True) + EPSILON)
    return (center * inverse, inverse)


def norm_back(normed, inverse, upstream):
    mean_grad = jnp.mean(upstream, axis=-1, keepdims=True)
    mean_proj = jnp.mean(upstream * normed, axis=-1, keepdims=True)
    return inverse * (upstream - mean_grad - normed * mean_proj)


def contract(first_op, second_op, first_dim, second_dim):
    return lax.dot_general(
        first_op,
        second_op,
        (((first_dim,), (second_dim,)), ((), ())),
        preferred_element_type=F32,
    )


def swap(values, axis):
    return lax.ppermute(values, axis, [(0, 1), (1, 0)])


def along_z(values, shift):
    return lax.ppermute(values, "z", [(i, (i + shift) % 4) for i in range(4)])


def exchange(blocks, axes):
    return lax.all_to_all(blocks, axes, split_axis=0, concat_axis=0, tiled=True)


def after(value, *earlier):
    return lax.optimization_barrier((value,) + earlier)[0]


def add_round(first, *others):
    total = first.astype(F32)
    for other in others:
        total = total + other.astype(F32)
    return total.astype(BF16)


def slot_matrix(expert_ids, seq_len):
    flat = expert_ids.reshape(-1)
    one_hot = (flat[:, None] == jnp.arange(EXPERTS, dtype=jnp.int32)[None, :]).astype(F32)
    rows = jnp.arange(seq_len)
    earlier = (rows[:, None] > rows[None, :]).astype(F32)
    before = jnp.dot(earlier, one_hot, preferred_element_type=F32)
    position = jnp.sum(before * one_hot, axis=1).astype(jnp.int32)
    rest = CAP - MAIN
    target = jnp.where(
        position < MAIN, flat * MAIN + position, EXPERTS * MAIN + flat * rest + position - MAIN
    )
    return (jnp.arange(EXPERTS * CAP, dtype=jnp.int32)[:, None] == target[None, :]).astype(BF16)


def place_kernel(places, piece, at_ref, *refs):
    block_refs, out_ref, sems = refs[: len(places)], refs[-2], refs[-1]
    copies = []
    number = 0
    for ref, parts in zip(block_refs, places):
        for i, (s, r, half) in enumerate(parts):
            z = lax.rem(at_ref[0] - s + 4, 4)
            yh = lax.rem(at_ref[1] + r, 2)
            copy = pltpu.make_async_copy(
                ref.at[pl.ds(i * piece, piece)], out_ref.at[z * 2 + yh, pl.ds(half * piece, piece)], sems.at[number]
            )
            copy.start()
            copies.append(copy)
            number += 1
    for copy in copies:
        copy.wait()


def gather_params(attn_param, earlier, normed):
    rows, head_dim = attn_param.shape
    half = rows // 2
    piece = half // 2
    core = lax.axis_index("c")
    own = lax.dynamic_slice_in_dim(attn_param, core * half, half, 0)
    first, second = own[:piece], own[piece:]
    around = [along_z(first, s) for s in (1, 3, 2)]
    own_y = swap(own, "yh")
    pair = after(jnp.concatenate([second, own_y[piece:]], axis=0), around[0], around[1])
    normed = swap(normed, "c")
    earlier = after(earlier, own_y, normed, *around)
    around_y = [swap(block, "yh") for block in around]
    pairs = [along_z(pair, s) for s in (1, 3, 2)]
    blocks = [own, own_y] + around + around_y + pairs
    places = (
        [[(0, 0, 0), (0, 0, 1)], [(0, 1, 0), (0, 1, 1)]]
        + [[(s, 0, 0)] for s in (1, 3, 2)]
        + [[(s, 1, 0)] for s in (1, 3, 2)]
        + [[(s, 0, 1), (s, 1, 1)] for s in (1, 3, 2)]
    )
    spread = spread_near(earlier)
    at = jnp.stack([lax.axis_index("z"), lax.axis_index("yh")]).astype(jnp.int32)
    at = after(at, *spread[1:4])
    anywhere = pl.BlockSpec(memory_space=pl.ANY)
    own = pl.pallas_call(
        lambda *refs: place_kernel(places, piece, *refs),
        out_shape=jax.ShapeDtypeStruct((N_DP, half, head_dim), BF16),
        in_specs=[pl.BlockSpec(memory_space=pltpu.SMEM)] + [anywhere] * len(blocks),
        out_specs=pl.BlockSpec(memory_space=pltpu.VMEM),
        scratch_shapes=[pltpu.SemaphoreType.DMA((16,))],
        compiler_params=pltpu.CompilerParams(vmem_limit_bytes=60 * 1024 * 1024),
    )(at, *blocks)
    other = swap(own, "c")
    first = jnp.where(core == 0, own, other)
    second = jnp.where(core == 0, other, own)
    return jnp.stack([first, second], axis=1).reshape(N_DP * rows, head_dim), spread, normed


def between_experts(rows):
    features = rows.shape[1]
    cut = EXPERTS * MAIN
    extra = rows[cut:].reshape(cut, -1)
    packed = jnp.concatenate([rows[:cut], extra], axis=1)
    width = packed.shape[1]
    packed = exchange(packed.reshape(EXPERTS, MAIN, width), EX).reshape(cut, width)
    extra = packed[:, features:].reshape(-1, features)
    return packed[:, :features], extra


def spread_near(own):
    one = own[:HALF]
    own_y = swap(own, "yh")
    return [own, own_y] + [along_z(one, s) for s in (1, 3, 2)]


def spread_far(near):
    own, own_y, near_z, far_z, across = near
    pair = after(jnp.concatenate([own[HALF:], own_y[HALF:]], axis=0), near_z, far_z)
    first = [swap(block, "yh") for block in (near_z, far_z, across)]
    return first + [along_z(pair, s) for s in (1, 3, 2)]


def collect(near, far):
    kept, one_y, two_y, *one_z = near
    early = [along_z(block, -s) for block, s in zip(one_z, (1, 3, 2))]
    early_y = swap(two_y, "yh")
    *one_yz, two_z, two_yz = far
    (*one_yz, two_yz), early, early_y = lax.optimization_barrier(([*one_yz, two_yz], early, early_y))
    late = [along_z(block, -s) for block, s in zip(one_yz, (1, 3, 2))]
    swapped = swap(two_yz, "yh")
    across = swap(add_round(one_y, *late), "yh")
    pairs = add_round(two_z, swapped)
    rest = kept.shape[0] - HALF
    back = [along_z(pairs[i * rest : (i + 1) * rest], -s) for i, s in enumerate((1, 3, 2))]
    one = add_round(kept[:HALF], across, *early)
    two = add_round(kept[HALF:], early_y, *back)
    return jnp.concatenate([one, two], axis=0)


def expert_kernel(counts, pieces_out, tall, *refs):
    count = len(counts)
    outs = len(pieces_out)
    normed_refs, cot_refs = refs[:count], refs[count : 2 * count]
    inner_ref, outer_ref = refs[2 * count : 2 * count + 2]
    out_refs = refs[2 * count + 2 : 2 * count + 2 + outs]
    (normed, cot, gate_map, up_map, outer_map, grad_gate, grad_up, result, row_sem, map_sem, out_sem) = refs[
        2 * count + 2 + outs :
    ]
    hidden, features = outer_ref.shape
    starts = [sum(counts[:i]) for i in range(count)]

    def load(source, target, sem):
        copy = pltpu.make_async_copy(source, target, sem)
        copy.start()
        return copy

    def load_rows(block_refs, target, side):
        return [
            load(ref, target.at[pl.ds(starts[i], counts[i])], row_sem.at[side, i])
            for i, ref in enumerate(block_refs)
        ]

    pieces = [(0, 256), (256, 256), (512, hidden - 512)]
    rows_in = load_rows(normed_refs, normed, 0)
    maps_in = []
    for i, (start, size) in enumerate(pieces):
        at = pl.ds(start, size)
        maps_in.append(
            [
                load(inner_ref.at[0, at], gate_map.at[at], map_sem.at[0, i]),
                load(inner_ref.at[1, at], up_map.at[at], map_sem.at[1, i]),
                load(outer_ref.at[at], outer_map.at[at], map_sem.at[2, i]),
            ]
        )
        if i == 0:
            rows_in += load_rows(cot_refs, cot, 1)
    blank = jnp.zeros((PADDED - hidden, features), BF16)
    for ref in (gate_map, up_map, outer_map):
        ref[pl.ds(hidden, PADDED - hidden)] = blank
    for copy in rows_in:
        copy.wait()
    steps = sum(counts) // tall

    for i in range(len(pieces)):
        for copy in maps_in[i]:
            copy.wait()
        at = pl.ds(i * 256, 256)

        @pl.loop(0, steps)
        def _(step):
            here = pl.ds(pl.multiple_of(step * tall, 16), tall)
            gate_part = contract(normed[here], gate_map[at], 1, 1)
            up_part = contract(normed[here], up_map[at], 1, 1)
            grad_act = contract(cot[here], outer_map[at], 1, 1)
            squash = 1.0 / (1.0 + jnp.exp(-gate_part))
            scaled = grad_act * squash
            grad_gate[here, at] = (scaled * up_part * (1.0 + gate_part * (1.0 - squash))).astype(BF16)
            grad_up[here, at] = (scaled * gate_part).astype(BF16)

    wide = 512
    copies = []
    for n in range(features // wide):
        lanes = pl.ds(n * wide, wide)

        @pl.loop(0, steps)
        def _(step):
            here = pl.ds(pl.multiple_of(step * tall, 16), tall)
            result[here, lanes] = (
                contract(grad_gate[here], gate_map[:, lanes], 1, 0)
                + contract(grad_up[here], up_map[:, lanes], 1, 0)
            ).astype(BF16)

        number = 0
        for ref, parts in zip(out_refs, pieces_out):
            at = 0
            for start, size in parts:
                copies.append(
                    load(
                        result.at[pl.ds(start, size), lanes],
                        ref.at[pl.ds(at, size), lanes],
                        out_sem.at[n, number],
                    )
                )
                at += size
                number += 1
    for copy in copies:
        copy.wait()


def experts(normed_blocks, cot_blocks, inner, outer, pieces_out, tall):
    counts = [block.shape[0] for block in normed_blocks]
    features = normed_blocks[0].shape[1]
    hidden = outer.shape[0]
    total = sum(counts)
    anywhere = pl.BlockSpec(memory_space=pl.ANY)
    return pl.pallas_call(
        lambda *refs: expert_kernel(counts, pieces_out, tall, *refs),
        out_shape=[
            jax.ShapeDtypeStruct((sum(size for _, size in parts), features), BF16) for parts in pieces_out
        ],
        in_specs=[anywhere] * (2 * len(counts) + 2),
        out_specs=[anywhere] * len(pieces_out),
        scratch_shapes=[
            pltpu.VMEM((total, features), BF16),
            pltpu.VMEM((total, features), BF16),
            pltpu.VMEM((PADDED, features), BF16),
            pltpu.VMEM((PADDED, features), BF16),
            pltpu.VMEM((PADDED, features), BF16),
            pltpu.VMEM((total, PADDED), BF16),
            pltpu.VMEM((total, PADDED), BF16),
            pltpu.VMEM((total, features), BF16),
            pltpu.SemaphoreType.DMA((2, len(counts))),
            pltpu.SemaphoreType.DMA((3, 3)),
            pltpu.SemaphoreType.DMA((features // 512, sum(len(parts) for parts in pieces_out))),
        ],
        compiler_params=pltpu.CompilerParams(vmem_limit_bytes=60 * 1024 * 1024),
        cost_estimate=pl.CostEstimate(
            flops=10 * total * features * hidden,
            bytes_accessed=6 * total * features + 6 * hidden * features,
            transcendentals=total * hidden,
        ),
    )(*normed_blocks, *cot_blocks, inner, outer)


def param_kernel(scale, head_dim, core_ref, normed_ref, hidden_ref, grads_ref, out_ref, terms):
    features = normed_ref.shape[1]
    tile = 1024
    for block in range(6):
        left_ref = normed_ref if block < 4 else hidden_ref
        right = grads_ref[:, block * head_dim : (block + 1) * head_dim]
        for start in range(0, features, tile):
            part = contract(left_ref[:, start : start + tile], right, 0, 0) * scale
            terms[pl.ds(block * features + start, tile)] = part.astype(BF16)
    core = core_ref[0]

    @pl.loop(0, out_ref.shape[0])
    def _(group):
        size = out_ref.shape[1]
        out_ref[group] = terms[pl.ds(pl.multiple_of((2 * group + core) * size, 16), size)]


def param_terms(core, normed, hidden, grads, scale, head_dim):
    features = normed.shape[1]
    rows = 6 * features
    whole = pl.BlockSpec(memory_space=pltpu.VMEM)
    return pl.pallas_call(
        lambda *refs: param_kernel(scale, head_dim, *refs),
        out_shape=jax.ShapeDtypeStruct((64, rows // 128, head_dim), BF16),
        in_specs=[pl.BlockSpec(memory_space=pltpu.SMEM)] + [whole] * 3,
        out_specs=whole,
        scratch_shapes=[pltpu.VMEM((rows, head_dim), BF16)],
        compiler_params=pltpu.CompilerParams(vmem_limit_bytes=40 * 1024 * 1024),
        cost_estimate=pl.CostEstimate(
            flops=2 * rows * head_dim * normed.shape[0], bytes_accessed=8 * 1024 * 1024, transcendentals=0
        ),
    )(core, normed, hidden, grads)


def per_device(tokens, attn_param, expert_ids, gate_score, w_in, w_out, cotangent):
    seq_len, features = tokens.shape
    head_dim = attn_param.shape[1]
    score_scale = head_dim ** (-0.5)
    devices = N_DP * EXPERTS
    slots = slot_matrix(expert_ids, seq_len)
    inner = jnp.transpose(w_in[0], (1, 2, 0))
    outer = w_out[0]

    cot_main, cot_extra = between_experts(contract(slots, cotangent, 1, 0).astype(BF16))
    cot_rows = jnp.concatenate([cot_main, cot_extra], axis=0)
    normed_one, inverse_one = layer_norm(tokens)
    normed_one_b = normed_one.astype(BF16)
    packed, cot_near, normed_other = gather_params(attn_param, cot_rows, normed_one_b)
    cot_far = spread_far(cot_near)

    normed_both = jnp.concatenate([normed_one_b, normed_other], axis=0)
    blocks = packed.reshape(2 * HEADS + 2, features, head_dim)
    project = blocks[: HEADS + 2]
    out_blocks = blocks[HEADS + 2 :]
    projected = jnp.einsum(
        "td,jdc->tjc", normed_one_b, project, preferred_element_type=F32
    ).astype(BF16)
    queries = projected[:, :HEADS]
    key_rows = projected[:, HEADS]
    value_rows = projected[:, HEADS + 1]
    scores = jnp.einsum("qhc,kc->hqk", queries, key_rows, preferred_element_type=F32) * score_scale
    causal = lax.broadcasted_iota(jnp.int32, (seq_len, seq_len), 0) >= lax.broadcasted_iota(
        jnp.int32, (seq_len, seq_len), 1
    )
    scores = jnp.where(causal[None], scores, MASKED)
    row_max = jnp.max(scores, axis=2, keepdims=True)
    raised = jnp.exp(scores - row_max)
    attention = raised / jnp.sum(raised, axis=2, keepdims=True)
    attention_b = attention.astype(BF16)
    context = jnp.einsum(
        "hqk,kc->qhc", attention_b, value_rows, preferred_element_type=F32
    ).astype(BF16)
    context_flat = context.reshape(seq_len, HEADS * head_dim)
    attn_out = jnp.einsum("thc,hdc->td", context, out_blocks, preferred_element_type=F32)
    residual = (tokens.astype(F32) + attn_out).astype(BF16)
    normed_two, inverse_two = layer_norm(residual)
    normed_two_b = after(normed_two.astype(BF16), cot_near[4], cot_far[0], cot_far[1], cot_far[3], cot_far[4])
    main, extra = between_experts(contract(slots, normed_two_b, 1, 0).astype(BF16))
    near = spread_near(jnp.concatenate([main, extra], axis=0))
    near[4] = after(near[4], cot_far[2], cot_far[5])
    h = HALF
    whole = EXPERTS * CAP
    rest = whole - h
    near_rows = experts(
        near,
        cot_near,
        inner,
        outer,
        [[(0, whole)], [(whole, h)], [(whole + h, rest)]] + [[(2 * whole + i * h, h)] for i in range(3)],
        2 * whole + 3 * h,
    )
    far = spread_far(near)
    far[0] = after(far[0], near_rows[0])
    far_rows = experts(
        far,
        cot_far,
        inner,
        outer,
        [[(i * h, h)] for i in range(3)]
        + [[(3 * h + (2 * i + r) * rest, rest) for i in range(3)] for r in (0, 1)],
        (h + 2 * rest) * 3 // 2,
    )
    back_main, back_extra = between_experts(collect(near_rows, far_rows))
    cut = EXPERTS * MAIN
    back_rows = contract(slots[:cut], back_main, 0, 0) + contract(slots[cut:], back_extra, 0, 0)
    moe_grad = gate_score * back_rows
    grad_hidden = cotangent.astype(F32) + norm_back(normed_two, inverse_two, moe_grad)
    grad_hidden_b = grad_hidden.astype(BF16)
    hidden_both = jnp.concatenate([grad_hidden_b, swap(grad_hidden_b, "c")], axis=0)
    grad_context = jnp.einsum(
        "td,hdc->thc", grad_hidden_b, out_blocks, preferred_element_type=F32
    )
    grad_context_b = grad_context.astype(BF16)
    grad_attention = jnp.einsum(
        "qhc,kc->hqk", grad_context_b, value_rows, preferred_element_type=F32
    )
    grad_value = jnp.einsum("hqk,qhc->kc", attention_b, grad_context_b, preferred_element_type=F32)
    grad_scores = (
        attention
        * (grad_attention - jnp.sum(grad_attention * attention, axis=2, keepdims=True))
        * score_scale
    )
    grad_scores_b = grad_scores.astype(BF16)
    grad_query = jnp.einsum("hqk,kc->qhc", grad_scores_b, key_rows, preferred_element_type=F32)
    grad_key = jnp.einsum("hqk,qhc->kc", grad_scores_b, queries, preferred_element_type=F32)
    grad_qkv = jnp.concatenate([grad_query, grad_key[:, None], grad_value[:, None]], axis=1).astype(BF16)
    grads_flat = jnp.concatenate([grad_qkv.reshape(seq_len, (HEADS + 2) * head_dim), context_flat], axis=1)
    grads_both = jnp.concatenate([grads_flat, swap(grads_flat, "c")], axis=0)
    core = lax.axis_index("c").astype(jnp.int32).reshape(1)
    terms = param_terms(
        core, normed_both, hidden_both, grads_both, (seq_len * devices) ** (-0.5), head_dim
    )
    attn_grad = jnp.sum(exchange(terms, CHIPS).astype(F32), axis=0)
    grad_normed = jnp.einsum("tjc,jdc->td", grad_qkv, project, preferred_element_type=F32)
    grad_tokens = (grad_hidden + norm_back(normed_one, inverse_one, grad_normed)).astype(BF16)
    return (grad_tokens, attn_grad)


def solution(mesh):
    fine = Mesh(mesh.devices.reshape(SIZES), AXES)
    rows = P(AXES, None)
    in_specs = (
        rows,
        P(DP, None),
        rows,
        rows,
        P(EX, None, None, DP),
        P(EX, DP, None),
        rows,
    )
    return jax.shard_map(
        per_device, mesh=fine, in_specs=in_specs, out_specs=(rows, rows), check_vma=False
    )
```

```python
import jax
import jax.numpy as jnp
from jax import lax
from jax.experimental import pallas as pl
from jax.experimental.pallas import tpu as pltpu
from jax.sharding import Mesh, PartitionSpec as P

EPSILON = 1e-05
MASKED = -1e30
AXES = ("z", "yh", "x", "yl", "c")
DP = ("z", "yh")
EX = ("x", "yl", "c")
CHIPS = ("z", "yh", "x", "yl")
SIZES = (4, 2, 4, 2, 2)
EXPERTS = 16
N_DP = 8
CAP = 10
MAIN = 8
HEADS = 2
HALF = 96
PADDED = 768
F32 = jnp.float32
BF16 = jnp.bfloat16


def layer_norm(values):
    widened = values.astype(F32)
    center = widened - jnp.mean(widened, axis=-1, keepdims=True)
    inverse = lax.rsqrt(jnp.mean(center * center, axis=-1, keepdims=True) + EPSILON)
    return (center * inverse, inverse)


def norm_back(normed, inverse, upstream):
    mean_grad = jnp.mean(upstream, axis=-1, keepdims=True)
    mean_proj = jnp.mean(upstream * normed, axis=-1, keepdims=True)
    return inverse * (upstream - mean_grad - normed * mean_proj)


def contract(first_op, second_op, first_dim, second_dim):
    return lax.dot_general(
        first_op,
        second_op,
        (((first_dim,), (second_dim,)), ((), ())),
        preferred_element_type=F32,
    )


def swap(values, axis):
    return lax.ppermute(values, axis, [(0, 1), (1, 0)])


def along_z(values, shift):
    return lax.ppermute(values, "z", [(i, (i + shift) % 4) for i in range(4)])


def exchange(blocks, axes):
    return lax.all_to_all(blocks, axes, split_axis=0, concat_axis=0, tiled=True)


def after(value, *earlier):
    return lax.optimization_barrier((value,) + earlier)[0]


def add_round(first, *others):
    total = first.astype(F32)
    for other in others:
        total = total + other.astype(F32)
    return total.astype(BF16)


def slot_matrix(expert_ids, seq_len):
    flat = expert_ids.reshape(-1)
    one_hot = (flat[:, None] == jnp.arange(EXPERTS, dtype=jnp.int32)[None, :]).astype(F32)
    rows = jnp.arange(seq_len)
    earlier = (rows[:, None] > rows[None, :]).astype(F32)
    before = jnp.dot(earlier, one_hot, preferred_element_type=F32)
    position = jnp.sum(before * one_hot, axis=1).astype(jnp.int32)
    rest = CAP - MAIN
    target = jnp.where(
        position < MAIN, flat * MAIN + position, EXPERTS * MAIN + flat * rest + position - MAIN
    )
    return (jnp.arange(EXPERTS * CAP, dtype=jnp.int32)[:, None] == target[None, :]).astype(BF16)


def place_kernel(places, piece, at_ref, *refs):
    block_refs, out_ref, sems = refs[: len(places)], refs[-2], refs[-1]
    copies = []
    number = 0
    for ref, parts in zip(block_refs, places):
        for i, (s, r, half) in enumerate(parts):
            z = lax.rem(at_ref[0] - s + 4, 4)
            yh = lax.rem(at_ref[1] + r, 2)
            copy = pltpu.make_async_copy(
                ref.at[pl.ds(i * piece, piece)], out_ref.at[z * 2 + yh, pl.ds(half * piece, piece)], sems.at[number]
            )
            copy.start()
            copies.append(copy)
            number += 1
    for copy in copies:
        copy.wait()


def gather_params(attn_param, earlier, normed):
    rows, head_dim = attn_param.shape
    half = rows // 2
    piece = half // 2
    core = lax.axis_index("c")
    own = lax.dynamic_slice_in_dim(attn_param, core * half, half, 0)
    first, second = own[:piece], own[piece:]
    around = [along_z(first, s) for s in (1, 3, 2)]
    own_y = swap(own, "yh")
    pair = after(jnp.concatenate([second, own_y[piece:]], axis=0), around[0], around[1])
    normed = swap(normed, "c")
    earlier = after(earlier, own_y, normed, *around)
    around_y = [swap(block, "yh") for block in around]
    pairs = [along_z(pair, s) for s in (1, 3, 2)]
    blocks = [own, own_y] + around + around_y + pairs
    places = (
        [[(0, 0, 0), (0, 0, 1)], [(0, 1, 0), (0, 1, 1)]]
        + [[(s, 0, 0)] for s in (1, 3, 2)]
        + [[(s, 1, 0)] for s in (1, 3, 2)]
        + [[(s, 0, 1), (s, 1, 1)] for s in (1, 3, 2)]
    )
    spread = spread_near(earlier)
    at = jnp.stack([lax.axis_index("z"), lax.axis_index("yh")]).astype(jnp.int32)
    at = after(at, *spread[2:4])
    anywhere = pl.BlockSpec(memory_space=pl.ANY)
    own = pl.pallas_call(
        lambda *refs: place_kernel(places, piece, *refs),
        out_shape=jax.ShapeDtypeStruct((N_DP, half, head_dim), BF16),
        in_specs=[pl.BlockSpec(memory_space=pltpu.SMEM)] + [anywhere] * len(blocks),
        out_specs=pl.BlockSpec(memory_space=pltpu.VMEM),
        scratch_shapes=[pltpu.SemaphoreType.DMA((16,))],
        compiler_params=pltpu.CompilerParams(vmem_limit_bytes=60 * 1024 * 1024),
    )(at, *blocks)
    other = swap(own, "c")
    first = jnp.where(core == 0, own, other)
    second = jnp.where(core == 0, other, own)
    return jnp.stack([first, second], axis=1).reshape(N_DP * rows, head_dim), spread, normed


def between_experts(rows):
    features = rows.shape[1]
    cut = EXPERTS * MAIN
    extra = rows[cut:].reshape(cut, -1)
    packed = jnp.concatenate([rows[:cut], extra], axis=1)
    width = packed.shape[1]
    packed = exchange(packed.reshape(EXPERTS, MAIN, width), EX).reshape(cut, width)
    extra = packed[:, features:].reshape(-1, features)
    return packed[:, :features], extra


def spread_near(own):
    one = own[:HALF]
    own_y = swap(own, "yh")
    return [own, own_y] + [along_z(one, s) for s in (1, 3, 2)]


def spread_far(near):
    own, own_y, near_z, far_z, across = near
    pair = after(jnp.concatenate([own[HALF:], own_y[HALF:]], axis=0), near_z, far_z)
    first = [swap(block, "yh") for block in (near_z, far_z, across)]
    return first + [along_z(pair, s) for s in (1, 3, 2)]


def collect(near, far):
    kept, one_y, two_y, *one_z = near
    early = [along_z(block, -s) for block, s in zip(one_z, (1, 3, 2))]
    early_y = swap(two_y, "yh")
    *one_yz, two_z, two_yz = far
    (*one_yz, two_yz), early, early_y = lax.optimization_barrier(([*one_yz, two_yz], early, early_y))
    late = [along_z(block, -s) for block, s in zip(one_yz, (1, 3, 2))]
    swapped = swap(two_yz, "yh")
    across = swap(add_round(one_y, *late), "yh")
    pairs = add_round(two_z, swapped)
    rest = kept.shape[0] - HALF
    back = [along_z(pairs[i * rest : (i + 1) * rest], -s) for i, s in enumerate((1, 3, 2))]
    one = add_round(kept[:HALF], across, *early)
    two = add_round(kept[HALF:], early_y, *back)
    return jnp.concatenate([one, two], axis=0)


def expert_kernel(counts, pieces_out, tall, *refs):
    count = len(counts)
    outs = len(pieces_out)
    normed_refs, cot_refs = refs[:count], refs[count : 2 * count]
    inner_ref, outer_ref = refs[2 * count : 2 * count + 2]
    out_refs = refs[2 * count + 2 : 2 * count + 2 + outs]
    (normed, cot, gate_map, up_map, outer_map, grad_gate, grad_up, result, row_sem, map_sem, out_sem) = refs[
        2 * count + 2 + outs :
    ]
    hidden, features = outer_ref.shape
    starts = [sum(counts[:i]) for i in range(count)]

    def load(source, target, sem):
        copy = pltpu.make_async_copy(source, target, sem)
        copy.start()
        return copy

    def load_rows(block_refs, target, side):
        return [
            load(ref, target.at[pl.ds(starts[i], counts[i])], row_sem.at[side, i])
            for i, ref in enumerate(block_refs)
        ]

    pieces = [(0, 256), (256, 256), (512, hidden - 512)]
    rows_in = load_rows(normed_refs, normed, 0)
    maps_in = []
    for i, (start, size) in enumerate(pieces):
        at = pl.ds(start, size)
        maps_in.append(
            [
                load(inner_ref.at[0, at], gate_map.at[at], map_sem.at[0, i]),
                load(inner_ref.at[1, at], up_map.at[at], map_sem.at[1, i]),
                load(outer_ref.at[at], outer_map.at[at], map_sem.at[2, i]),
            ]
        )
        if i == 0:
            rows_in += load_rows(cot_refs, cot, 1)
    blank = jnp.zeros((PADDED - hidden, features), BF16)
    for ref in (gate_map, up_map, outer_map):
        ref[pl.ds(hidden, PADDED - hidden)] = blank
    for copy in rows_in:
        copy.wait()
    steps = sum(counts) // tall

    for i in range(len(pieces)):
        for copy in maps_in[i]:
            copy.wait()
        at = pl.ds(i * 256, 256)

        @pl.loop(0, steps)
        def _(step):
            here = pl.ds(pl.multiple_of(step * tall, 16), tall)
            gate_part = contract(normed[here], gate_map[at], 1, 1)
            up_part = contract(normed[here], up_map[at], 1, 1)
            grad_act = contract(cot[here], outer_map[at], 1, 1)
            squash = 1.0 / (1.0 + jnp.exp(-gate_part))
            scaled = grad_act * squash
            grad_gate[here, at] = (scaled * up_part * (1.0 + gate_part * (1.0 - squash))).astype(BF16)
            grad_up[here, at] = (scaled * gate_part).astype(BF16)

    wide = 512
    copies = []
    for n in range(features // wide):
        lanes = pl.ds(n * wide, wide)

        @pl.loop(0, steps)
        def _(step):
            here = pl.ds(pl.multiple_of(step * tall, 16), tall)
            result[here, lanes] = (
                contract(grad_gate[here], gate_map[:, lanes], 1, 0)
                + contract(grad_up[here], up_map[:, lanes], 1, 0)
            ).astype(BF16)

        number = 0
        for ref, parts in zip(out_refs, pieces_out):
            at = 0
            for start, size in parts:
                copies.append(
                    load(
                        result.at[pl.ds(start, size), lanes],
                        ref.at[pl.ds(at, size), lanes],
                        out_sem.at[n, number],
                    )
                )
                at += size
                number += 1
    for copy in copies:
        copy.wait()


def experts(normed_blocks, cot_blocks, inner, outer, pieces_out, tall):
    counts = [block.shape[0] for block in normed_blocks]
    features = normed_blocks[0].shape[1]
    hidden = outer.shape[0]
    total = sum(counts)
    anywhere = pl.BlockSpec(memory_space=pl.ANY)
    return pl.pallas_call(
        lambda *refs: expert_kernel(counts, pieces_out, tall, *refs),
        out_shape=[
            jax.ShapeDtypeStruct((sum(size for _, size in parts), features), BF16) for parts in pieces_out
        ],
        in_specs=[anywhere] * (2 * len(counts) + 2),
        out_specs=[anywhere] * len(pieces_out),
        scratch_shapes=[
            pltpu.VMEM((total, features), BF16),
            pltpu.VMEM((total, features), BF16),
            pltpu.VMEM((PADDED, features), BF16),
            pltpu.VMEM((PADDED, features), BF16),
            pltpu.VMEM((PADDED, features), BF16),
            pltpu.VMEM((total, PADDED), BF16),
            pltpu.VMEM((total, PADDED), BF16),
            pltpu.VMEM((total, features), BF16),
            pltpu.SemaphoreType.DMA((2, len(counts))),
            pltpu.SemaphoreType.DMA((3, 3)),
            pltpu.SemaphoreType.DMA((features // 512, sum(len(parts) for parts in pieces_out))),
        ],
        compiler_params=pltpu.CompilerParams(vmem_limit_bytes=60 * 1024 * 1024),
        cost_estimate=pl.CostEstimate(
            flops=10 * total * features * hidden,
            bytes_accessed=6 * total * features + 6 * hidden * features,
            transcendentals=total * hidden,
        ),
    )(*normed_blocks, *cot_blocks, inner, outer)


def param_kernel(scale, head_dim, core_ref, normed_ref, hidden_ref, grads_ref, out_ref, terms):
    features = normed_ref.shape[1]
    tile = 1024
    for block in range(6):
        left_ref = normed_ref if block < 4 else hidden_ref
        right = grads_ref[:, block * head_dim : (block + 1) * head_dim]
        for start in range(0, features, tile):
            part = contract(left_ref[:, start : start + tile], right, 0, 0) * scale
            terms[pl.ds(block * features + start, tile)] = part.astype(BF16)
    core = core_ref[0]

    @pl.loop(0, out_ref.shape[0])
    def _(group):
        size = out_ref.shape[1]
        out_ref[group] = terms[pl.ds(pl.multiple_of((2 * group + core) * size, 16), size)]


def param_terms(core, normed, hidden, grads, scale, head_dim):
    features = normed.shape[1]
    rows = 6 * features
    whole = pl.BlockSpec(memory_space=pltpu.VMEM)
    return pl.pallas_call(
        lambda *refs: param_kernel(scale, head_dim, *refs),
        out_shape=jax.ShapeDtypeStruct((64, rows // 128, head_dim), BF16),
        in_specs=[pl.BlockSpec(memory_space=pltpu.SMEM)] + [whole] * 3,
        out_specs=whole,
        scratch_shapes=[pltpu.VMEM((rows, head_dim), BF16)],
        compiler_params=pltpu.CompilerParams(vmem_limit_bytes=40 * 1024 * 1024),
        cost_estimate=pl.CostEstimate(
            flops=2 * rows * head_dim * normed.shape[0], bytes_accessed=8 * 1024 * 1024, transcendentals=0
        ),
    )(core, normed, hidden, grads)


def per_device(tokens, attn_param, expert_ids, gate_score, w_in, w_out, cotangent):
    seq_len, features = tokens.shape
    head_dim = attn_param.shape[1]
    score_scale = head_dim ** (-0.5)
    devices = N_DP * EXPERTS
    slots = slot_matrix(expert_ids, seq_len)
    inner = jnp.transpose(w_in[0], (1, 2, 0))
    outer = w_out[0]

    cot_main, cot_extra = between_experts(contract(slots, cotangent, 1, 0).astype(BF16))
    cot_rows = jnp.concatenate([cot_main, cot_extra], axis=0)
    normed_one, inverse_one = layer_norm(tokens)
    normed_one_b = normed_one.astype(BF16)
    packed, cot_near, normed_other = gather_params(attn_param, cot_rows, normed_one_b)
    cot_far = spread_far(cot_near)

    normed_both = jnp.concatenate([normed_one_b, normed_other], axis=0)
    blocks = packed.reshape(2 * HEADS + 2, features, head_dim)
    project = blocks[: HEADS + 2]
    out_blocks = blocks[HEADS + 2 :]
    projected = jnp.einsum(
        "td,jdc->tjc", normed_one_b, project, preferred_element_type=F32
    ).astype(BF16)
    queries = projected[:, :HEADS]
    key_rows = projected[:, HEADS]
    value_rows = projected[:, HEADS + 1]
    scores = jnp.einsum("qhc,kc->hqk", queries, key_rows, preferred_element_type=F32) * score_scale
    causal = lax.broadcasted_iota(jnp.int32, (seq_len, seq_len), 0) >= lax.broadcasted_iota(
        jnp.int32, (seq_len, seq_len), 1
    )
    scores = jnp.where(causal[None], scores, MASKED)
    row_max = jnp.max(scores, axis=2, keepdims=True)
    raised = jnp.exp(scores - row_max)
    attention = raised / jnp.sum(raised, axis=2, keepdims=True)
    attention_b = attention.astype(BF16)
    context = jnp.einsum(
        "hqk,kc->qhc", attention_b, value_rows, preferred_element_type=F32
    ).astype(BF16)
    context_flat = context.reshape(seq_len, HEADS * head_dim)
    attn_out = jnp.einsum("thc,hdc->td", context, out_blocks, preferred_element_type=F32)
    residual = (tokens.astype(F32) + attn_out).astype(BF16)
    normed_two, inverse_two = layer_norm(residual)
    normed_two_b = after(normed_two.astype(BF16), cot_near[4], cot_far[0], cot_far[3], cot_far[4])
    main, extra = between_experts(contract(slots, normed_two_b, 1, 0).astype(BF16))
    near = spread_near(after(jnp.concatenate([main, extra], axis=0), cot_far[1], cot_far[2], cot_far[5]))
    h = HALF
    whole = EXPERTS * CAP
    rest = whole - h
    near_rows = experts(
        near,
        cot_near,
        inner,
        outer,
        [[(0, whole)], [(whole, h)], [(whole + h, rest)]] + [[(2 * whole + i * h, h)] for i in range(3)],
        2 * whole + 3 * h,
    )
    far = spread_far(near)
    far[0] = after(far[0], near_rows[0])
    far_rows = experts(
        far,
        cot_far,
        inner,
        outer,
        [[(i * h, h)] for i in range(3)]
        + [[(3 * h + (2 * i + r) * rest, rest) for i in range(3)] for r in (0, 1)],
        (h + 2 * rest) * 3 // 2,
    )
    back_main, back_extra = between_experts(collect(near_rows, far_rows))
    cut = EXPERTS * MAIN
    back_rows = contract(slots[:cut], back_main, 0, 0) + contract(slots[cut:], back_extra, 0, 0)
    moe_grad = gate_score * back_rows
    grad_hidden = cotangent.astype(F32) + norm_back(normed_two, inverse_two, moe_grad)
    grad_hidden_b = grad_hidden.astype(BF16)
    hidden_both = jnp.concatenate([grad_hidden_b, swap(grad_hidden_b, "c")], axis=0)
    grad_context = jnp.einsum(
        "td,hdc->thc", grad_hidden_b, out_blocks, preferred_element_type=F32
    )
    grad_context_b = grad_context.astype(BF16)
    grad_attention = jnp.einsum(
        "qhc,kc->hqk", grad_context_b, value_rows, preferred_element_type=F32
    )
    grad_value = jnp.einsum("hqk,qhc->kc", attention_b, grad_context_b, preferred_element_type=F32)
    grad_scores = (
        attention
        * (grad_attention - jnp.sum(grad_attention * attention, axis=2, keepdims=True))
        * score_scale
    )
    grad_scores_b = grad_scores.astype(BF16)
    grad_query = jnp.einsum("hqk,kc->qhc", grad_scores_b, key_rows, preferred_element_type=F32)
    grad_key = jnp.einsum("hqk,qhc->kc", grad_scores_b, queries, preferred_element_type=F32)
    grad_qkv = jnp.concatenate([grad_query, grad_key[:, None], grad_value[:, None]], axis=1).astype(BF16)
    grads_flat = jnp.concatenate([grad_qkv.reshape(seq_len, (HEADS + 2) * head_dim), context_flat], axis=1)
    grads_both = jnp.concatenate([grads_flat, swap(grads_flat, "c")], axis=0)
    core = lax.axis_index("c").astype(jnp.int32).reshape(1)
    terms = param_terms(
        core, normed_both, hidden_both, grads_both, (seq_len * devices) ** (-0.5), head_dim
    )
    attn_grad = jnp.sum(exchange(terms, CHIPS).astype(F32), axis=0)
    grad_normed = jnp.einsum("tjc,jdc->td", grad_qkv, project, preferred_element_type=F32)
    grad_tokens = (grad_hidden + norm_back(normed_one, inverse_one, grad_normed)).astype(BF16)
    return (grad_tokens, attn_grad)


def solution(mesh):
    fine = Mesh(mesh.devices.reshape(SIZES), AXES)
    rows = P(AXES, None)
    in_specs = (
        rows,
        P(DP, None),
        rows,
        rows,
        P(EX, None, None, DP),
        P(EX, DP, None),
        rows,
    )
    return jax.shard_map(
        per_device, mesh=fine, in_specs=in_specs, out_specs=(rows, rows), check_vma=False
    )
```

```python
import jax
import jax.numpy as jnp
from jax import lax
from jax.experimental import pallas as pl
from jax.experimental.pallas import tpu as pltpu
from jax.sharding import Mesh, PartitionSpec as P

EPSILON = 1e-05
MASKED = -1e30
AXES = ("z", "yh", "x", "yl", "c")
DP = ("z", "yh")
EX = ("x", "yl", "c")
CHIPS = ("z", "yh", "x", "yl")
SIZES = (4, 2, 4, 2, 2)
EXPERTS = 16
N_DP = 8
CAP = 10
MAIN = 8
HEADS = 2
HALF = 96
PADDED = 768
F32 = jnp.float32
BF16 = jnp.bfloat16


def layer_norm(values):
    widened = values.astype(F32)
    center = widened - jnp.mean(widened, axis=-1, keepdims=True)
    inverse = lax.rsqrt(jnp.mean(center * center, axis=-1, keepdims=True) + EPSILON)
    return (center * inverse, inverse)


def norm_back(normed, inverse, upstream):
    mean_grad = jnp.mean(upstream, axis=-1, keepdims=True)
    mean_proj = jnp.mean(upstream * normed, axis=-1, keepdims=True)
    return inverse * (upstream - mean_grad - normed * mean_proj)


def contract(first_op, second_op, first_dim, second_dim):
    return lax.dot_general(
        first_op,
        second_op,
        (((first_dim,), (second_dim,)), ((), ())),
        preferred_element_type=F32,
    )


def swap(values, axis):
    return lax.ppermute(values, axis, [(0, 1), (1, 0)])


def along_z(values, shift):
    return lax.ppermute(values, "z", [(i, (i + shift) % 4) for i in range(4)])


def exchange(blocks, axes):
    return lax.all_to_all(blocks, axes, split_axis=0, concat_axis=0, tiled=True)


def after(value, *earlier):
    return lax.optimization_barrier((value,) + earlier)[0]


def add_round(first, *others):
    total = first.astype(F32)
    for other in others:
        total = total + other.astype(F32)
    return total.astype(BF16)


def slot_matrix(expert_ids, seq_len):
    flat = expert_ids.reshape(-1)
    one_hot = (flat[:, None] == jnp.arange(EXPERTS, dtype=jnp.int32)[None, :]).astype(F32)
    rows = jnp.arange(seq_len)
    earlier = (rows[:, None] > rows[None, :]).astype(F32)
    before = jnp.dot(earlier, one_hot, preferred_element_type=F32)
    position = jnp.sum(before * one_hot, axis=1).astype(jnp.int32)
    rest = CAP - MAIN
    target = jnp.where(
        position < MAIN, flat * MAIN + position, EXPERTS * MAIN + flat * rest + position - MAIN
    )
    return (jnp.arange(EXPERTS * CAP, dtype=jnp.int32)[:, None] == target[None, :]).astype(BF16)


def place_kernel(places, piece, at_ref, *refs):
    block_refs, out_ref, sems = refs[: len(places)], refs[-2], refs[-1]
    copies = []
    number = 0
    for ref, parts in zip(block_refs, places):
        for i, (s, r, half) in enumerate(parts):
            z = lax.rem(at_ref[0] - s + 4, 4)
            yh = lax.rem(at_ref[1] + r, 2)
            copy = pltpu.make_async_copy(
                ref.at[pl.ds(i * piece, piece)], out_ref.at[z * 2 + yh, pl.ds(half * piece, piece)], sems.at[number]
            )
            copy.start()
            copies.append(copy)
            number += 1
    for copy in copies:
        copy.wait()


def gather_params(attn_param, earlier, normed):
    rows, head_dim = attn_param.shape
    half = rows // 2
    piece = half // 2
    core = lax.axis_index("c")
    own = lax.dynamic_slice_in_dim(attn_param, core * half, half, 0)
    first, second = own[:piece], own[piece:]
    around = [along_z(first, s) for s in (1, 3, 2)]
    own_y = swap(own, "yh")
    pair = after(jnp.concatenate([second, own_y[piece:]], axis=0), around[0], around[1])
    normed = swap(normed, "c")
    earlier = after(earlier, own_y, normed, *around)
    around_y = [swap(block, "yh") for block in around]
    pairs = [along_z(pair, s) for s in (1, 3, 2)]
    blocks = [own, own_y] + around + around_y + pairs
    places = (
        [[(0, 0, 0), (0, 0, 1)], [(0, 1, 0), (0, 1, 1)]]
        + [[(s, 0, 0)] for s in (1, 3, 2)]
        + [[(s, 1, 0)] for s in (1, 3, 2)]
        + [[(s, 0, 1), (s, 1, 1)] for s in (1, 3, 2)]
    )
    spread = spread_near(earlier)
    at = jnp.stack([lax.axis_index("z"), lax.axis_index("yh")]).astype(jnp.int32)
    at = after(at, *spread[1:4])
    anywhere = pl.BlockSpec(memory_space=pl.ANY)
    own = pl.pallas_call(
        lambda *refs: place_kernel(places, piece, *refs),
        out_shape=jax.ShapeDtypeStruct((N_DP, half, head_dim), BF16),
        in_specs=[pl.BlockSpec(memory_space=pltpu.SMEM)] + [anywhere] * len(blocks),
        out_specs=pl.BlockSpec(memory_space=pltpu.VMEM),
        scratch_shapes=[pltpu.SemaphoreType.DMA((16,))],
        compiler_params=pltpu.CompilerParams(vmem_limit_bytes=60 * 1024 * 1024),
    )(at, *blocks)
    other = swap(own, "c")
    first = jnp.where(core == 0, own, other)
    second = jnp.where(core == 0, other, own)
    return jnp.stack([first, second], axis=1).reshape(N_DP * rows, head_dim), spread, normed


def between_experts(rows):
    features = rows.shape[1]
    cut = EXPERTS * MAIN
    extra = rows[cut:].reshape(cut, -1)
    packed = jnp.concatenate([rows[:cut], extra], axis=1)
    width = packed.shape[1]
    packed = exchange(packed.reshape(EXPERTS, MAIN, width), EX).reshape(cut, width)
    extra = packed[:, features:].reshape(-1, features)
    return packed[:, :features], extra


def spread_near(own):
    one = own[:HALF]
    own_y = swap(own, "yh")
    return [own, own_y] + [along_z(one, s) for s in (1, 3, 2)]


def spread_far(near, *earlier):
    own, own_y, near_z, far_z, across = near
    pair = after(jnp.concatenate([own[HALF:], own_y[HALF:]], axis=0), near_z, far_z)
    near_z = after(near_z, *earlier) if earlier else near_z
    first = [swap(block, "yh") for block in (near_z, far_z, across)]
    return first + [along_z(pair, s) for s in (1, 3, 2)]


def collect(near, far):
    kept, one_y, two_y, *one_z = near
    early = [along_z(block, -s) for block, s in zip(one_z, (1, 3, 2))]
    early_y = swap(two_y, "yh")
    *one_yz, two_z, two_yz = far
    (*one_yz, two_yz), early, early_y = lax.optimization_barrier(([*one_yz, two_yz], early, early_y))
    late = [along_z(block, -s) for block, s in zip(one_yz, (1, 3, 2))]
    swapped = swap(two_yz, "yh")
    across = swap(add_round(one_y, *late), "yh")
    pairs = add_round(two_z, swapped)
    rest = kept.shape[0] - HALF
    back = [along_z(pairs[i * rest : (i + 1) * rest], -s) for i, s in enumerate((1, 3, 2))]
    one = add_round(kept[:HALF], across, *early)
    two = add_round(kept[HALF:], early_y, *back)
    return jnp.concatenate([one, two], axis=0)


def load(source, target, sem):
    copy = pltpu.make_async_copy(source, target, sem)
    copy.start()
    return copy


def act_kernel(counts, *refs):
    count = len(counts)
    cot_refs, outer_ref, out_ref = refs[:count], refs[count], refs[count + 1]
    cot, outer_map, row_sem, map_sem = refs[count + 2 :]
    hidden, features = outer_ref.shape
    copies = [load(outer_ref, outer_map.at[pl.ds(0, hidden)], map_sem.at[0])]
    for i, ref in enumerate(cot_refs):
        copies.append(load(ref, cot.at[pl.ds(sum(counts[:i]), counts[i])], row_sem.at[i]))
    outer_map[pl.ds(hidden, PADDED - hidden)] = jnp.zeros((PADDED - hidden, features), BF16)
    for copy in copies:
        copy.wait()
    tall = sum(counts) // 2

    @pl.loop(0, 2)
    def _(step):
        here = pl.ds(pl.multiple_of(step * tall, 16), tall)
        out_ref[here] = contract(cot[here], outer_map[...], 1, 1).astype(BF16)


def act_grads(cot_blocks, outer):
    counts = [block.shape[0] for block in cot_blocks]
    features = outer.shape[1]
    total = sum(counts)
    anywhere = pl.BlockSpec(memory_space=pl.ANY)
    return pl.pallas_call(
        lambda *refs: act_kernel(counts, *refs),
        out_shape=jax.ShapeDtypeStruct((total, PADDED), BF16),
        in_specs=[anywhere] * (len(counts) + 1),
        out_specs=pl.BlockSpec(memory_space=pltpu.VMEM),
        scratch_shapes=[
            pltpu.VMEM((total, features), BF16),
            pltpu.VMEM((PADDED, features), BF16),
            pltpu.SemaphoreType.DMA((len(counts),)),
            pltpu.SemaphoreType.DMA((1,)),
        ],
        compiler_params=pltpu.CompilerParams(vmem_limit_bytes=60 * 1024 * 1024),
        cost_estimate=pl.CostEstimate(
            flops=2 * total * features * PADDED,
            bytes_accessed=2 * (total + PADDED) * features,
            transcendentals=0,
        ),
    )(*cot_blocks, outer)


def expert_kernel(counts, pieces_out, tall, *refs):
    count = len(counts)
    outs = len(pieces_out)
    normed_refs = refs[:count]
    act_ref, inner_ref = refs[count : count + 2]
    out_refs = refs[count + 2 : count + 2 + outs]
    (normed, acts, gate_map, up_map, grad_gate, grad_up, result, row_sem, act_sem, map_sem, out_sem) = refs[
        count + 2 + outs :
    ]
    _, hidden, features = inner_ref.shape
    pieces = [(0, 256), (256, 256), (512, hidden - 512)]
    rows_in = [
        load(ref, normed.at[pl.ds(sum(counts[:i]), counts[i])], row_sem.at[i])
        for i, ref in enumerate(normed_refs)
    ]
    maps_in = []
    for i, (start, size) in enumerate(pieces):
        at = pl.ds(start, size)
        maps_in.append(
            [
                load(inner_ref.at[0, at], gate_map.at[at], map_sem.at[0, i]),
                load(inner_ref.at[1, at], up_map.at[at], map_sem.at[1, i]),
            ]
        )
        if i == 0:
            rows_in.append(load(act_ref, acts, act_sem.at[0]))
    blank = jnp.zeros((PADDED - hidden, features), BF16)
    for ref in (gate_map, up_map):
        ref[pl.ds(hidden, PADDED - hidden)] = blank
    for copy in rows_in:
        copy.wait()
    steps = sum(counts) // tall

    for i in range(len(pieces)):
        for copy in maps_in[i]:
            copy.wait()
        at = pl.ds(i * 256, 256)

        @pl.loop(0, steps)
        def _(step):
            here = pl.ds(pl.multiple_of(step * tall, 16), tall)
            gate_part = contract(normed[here], gate_map[at], 1, 1)
            up_part = contract(normed[here], up_map[at], 1, 1)
            squash = 1.0 / (1.0 + jnp.exp(-gate_part))
            scaled = acts[here, at].astype(F32) * squash
            grad_gate[here, at] = (scaled * up_part * (1.0 + gate_part * (1.0 - squash))).astype(BF16)
            grad_up[here, at] = (scaled * gate_part).astype(BF16)

    wide = 512
    copies = []
    for n in range(features // wide):
        lanes = pl.ds(n * wide, wide)

        @pl.loop(0, steps)
        def _(step):
            here = pl.ds(pl.multiple_of(step * tall, 16), tall)
            result[here, lanes] = (
                contract(grad_gate[here], gate_map[:, lanes], 1, 0)
                + contract(grad_up[here], up_map[:, lanes], 1, 0)
            ).astype(BF16)

        number = 0
        for ref, parts in zip(out_refs, pieces_out):
            at = 0
            for start, size in parts:
                copies.append(
                    load(
                        result.at[pl.ds(start, size), lanes],
                        ref.at[pl.ds(at, size), lanes],
                        out_sem.at[n, number],
                    )
                )
                at += size
                number += 1
    for copy in copies:
        copy.wait()


def experts(normed_blocks, acts, inner, pieces_out, tall):
    counts = [block.shape[0] for block in normed_blocks]
    features = normed_blocks[0].shape[1]
    total = sum(counts)
    anywhere = pl.BlockSpec(memory_space=pl.ANY)
    return pl.pallas_call(
        lambda *refs: expert_kernel(counts, pieces_out, tall, *refs),
        out_shape=[
            jax.ShapeDtypeStruct((sum(size for _, size in parts), features), BF16) for parts in pieces_out
        ],
        in_specs=[anywhere] * (len(counts) + 2),
        out_specs=[anywhere] * len(pieces_out),
        scratch_shapes=[
            pltpu.VMEM((total, features), BF16),
            pltpu.VMEM((total, PADDED), BF16),
            pltpu.VMEM((PADDED, features), BF16),
            pltpu.VMEM((PADDED, features), BF16),
            pltpu.VMEM((total, PADDED), BF16),
            pltpu.VMEM((total, PADDED), BF16),
            pltpu.VMEM((total, features), BF16),
            pltpu.SemaphoreType.DMA((len(counts),)),
            pltpu.SemaphoreType.DMA((1,)),
            pltpu.SemaphoreType.DMA((2, 3)),
            pltpu.SemaphoreType.DMA((features // 512, sum(len(parts) for parts in pieces_out))),
        ],
        compiler_params=pltpu.CompilerParams(vmem_limit_bytes=60 * 1024 * 1024),
        cost_estimate=pl.CostEstimate(
            flops=8 * total * features * PADDED,
            bytes_accessed=4 * total * features + 4 * PADDED * features,
            transcendentals=total * PADDED,
        ),
    )(*normed_blocks, acts, inner)


def param_kernel(scale, head_dim, core_ref, normed_ref, hidden_ref, grads_ref, out_ref, terms):
    features = normed_ref.shape[1]
    tile = 1024
    for block in range(6):
        left_ref = normed_ref if block < 4 else hidden_ref
        right = grads_ref[:, block * head_dim : (block + 1) * head_dim]
        for start in range(0, features, tile):
            part = contract(left_ref[:, start : start + tile], right, 0, 0) * scale
            terms[pl.ds(block * features + start, tile)] = part.astype(BF16)
    core = core_ref[0]

    @pl.loop(0, out_ref.shape[0])
    def _(group):
        size = out_ref.shape[1]
        out_ref[group] = terms[pl.ds(pl.multiple_of((2 * group + core) * size, 16), size)]


def param_terms(core, normed, hidden, grads, scale, head_dim):
    features = normed.shape[1]
    rows = 6 * features
    whole = pl.BlockSpec(memory_space=pltpu.VMEM)
    return pl.pallas_call(
        lambda *refs: param_kernel(scale, head_dim, *refs),
        out_shape=jax.ShapeDtypeStruct((64, rows // 128, head_dim), BF16),
        in_specs=[pl.BlockSpec(memory_space=pltpu.SMEM)] + [whole] * 3,
        out_specs=whole,
        scratch_shapes=[pltpu.VMEM((rows, head_dim), BF16)],
        compiler_params=pltpu.CompilerParams(vmem_limit_bytes=40 * 1024 * 1024),
        cost_estimate=pl.CostEstimate(
            flops=2 * rows * head_dim * normed.shape[0], bytes_accessed=8 * 1024 * 1024, transcendentals=0
        ),
    )(core, normed, hidden, grads)


def per_device(tokens, attn_param, expert_ids, gate_score, w_in, w_out, cotangent):
    seq_len, features = tokens.shape
    head_dim = attn_param.shape[1]
    score_scale = head_dim ** (-0.5)
    devices = N_DP * EXPERTS
    slots = slot_matrix(expert_ids, seq_len)
    inner = jnp.transpose(w_in[0], (1, 2, 0))
    outer = w_out[0]

    cot_main, cot_extra = between_experts(contract(slots, cotangent, 1, 0).astype(BF16))
    cot_rows = jnp.concatenate([cot_main, cot_extra], axis=0)
    normed_one, inverse_one = layer_norm(tokens)
    normed_one_b = normed_one.astype(BF16)
    packed, cot_near, normed_other = gather_params(attn_param, cot_rows, normed_one_b)
    cot_far = spread_far(cot_near)

    normed_both = jnp.concatenate([normed_one_b, normed_other], axis=0)
    blocks = packed.reshape(2 * HEADS + 2, features, head_dim)
    project = blocks[: HEADS + 2]
    out_blocks = blocks[HEADS + 2 :]
    projected = jnp.einsum(
        "td,jdc->tjc", normed_one_b, project, preferred_element_type=F32
    ).astype(BF16)
    queries = projected[:, :HEADS]
    key_rows = projected[:, HEADS]
    value_rows = projected[:, HEADS + 1]
    scores = jnp.einsum("qhc,kc->hqk", queries, key_rows, preferred_element_type=F32) * score_scale
    causal = lax.broadcasted_iota(jnp.int32, (seq_len, seq_len), 0) >= lax.broadcasted_iota(
        jnp.int32, (seq_len, seq_len), 1
    )
    scores = jnp.where(causal[None], scores, MASKED)
    row_max = jnp.max(scores, axis=2, keepdims=True)
    raised = jnp.exp(scores - row_max)
    attention = raised / jnp.sum(raised, axis=2, keepdims=True)
    attention_b = attention.astype(BF16)
    context = jnp.einsum(
        "hqk,kc->qhc", attention_b, value_rows, preferred_element_type=F32
    ).astype(BF16)
    context_flat = context.reshape(seq_len, HEADS * head_dim)
    attn_out = jnp.einsum("thc,hdc->td", context, out_blocks, preferred_element_type=F32)
    residual = (tokens.astype(F32) + attn_out).astype(BF16)
    normed_two, inverse_two = layer_norm(residual)
    normed_two_b = after(normed_two.astype(BF16), cot_near[4], cot_far[0], cot_far[1], cot_far[3], cot_far[4])
    main, extra = between_experts(contract(slots, normed_two_b, 1, 0).astype(BF16))
    near_acts = act_grads(cot_near, outer)
    far_acts = act_grads(cot_far, outer)
    near = spread_near(after(jnp.concatenate([main, extra], axis=0), near_acts, cot_far[2], cot_far[5]))
    h = HALF
    whole = EXPERTS * CAP
    rest = whole - h
    near_rows = experts(
        near,
        near_acts,
        inner,
        [[(0, whole)], [(whole, h)], [(whole + h, rest)]] + [[(2 * whole + i * h, h)] for i in range(3)],
        2 * whole + 3 * h,
    )
    far = spread_far(near, far_acts)
    far[0] = after(far[0], near_rows[0])
    far_rows = experts(
        far,
        far_acts,
        inner,
        [[(i * h, h)] for i in range(3)]
        + [[(3 * h + (2 * i + r) * rest, rest) for i in range(3)] for r in (0, 1)],
        (h + 2 * rest) * 3 // 2,
    )
    back_main, back_extra = between_experts(collect(near_rows, far_rows))
    cut = EXPERTS * MAIN
    back_rows = contract(slots[:cut], back_main, 0, 0) + contract(slots[cut:], back_extra, 0, 0)
    moe_grad = gate_score * back_rows
    grad_hidden = cotangent.astype(F32) + norm_back(normed_two, inverse_two, moe_grad)
    grad_hidden_b = grad_hidden.astype(BF16)
    hidden_both = jnp.concatenate([grad_hidden_b, swap(grad_hidden_b, "c")], axis=0)
    grad_context = jnp.einsum(
        "td,hdc->thc", grad_hidden_b, out_blocks, preferred_element_type=F32
    )
    grad_context_b = grad_context.astype(BF16)
    grad_attention = jnp.einsum(
        "qhc,kc->hqk", grad_context_b, value_rows, preferred_element_type=F32
    )
    grad_value = jnp.einsum("hqk,qhc->kc", attention_b, grad_context_b, preferred_element_type=F32)
    grad_scores = (
        attention
        * (grad_attention - jnp.sum(grad_attention * attention, axis=2, keepdims=True))
        * score_scale
    )
    grad_scores_b = grad_scores.astype(BF16)
    grad_query = jnp.einsum("hqk,kc->qhc", grad_scores_b, key_rows, preferred_element_type=F32)
    grad_key = jnp.einsum("hqk,qhc->kc", grad_scores_b, queries, preferred_element_type=F32)
    grad_qkv = jnp.concatenate([grad_query, grad_key[:, None], grad_value[:, None]], axis=1).astype(BF16)
    grads_flat = jnp.concatenate([grad_qkv.reshape(seq_len, (HEADS + 2) * head_dim), context_flat], axis=1)
    grads_both = jnp.concatenate([grads_flat, swap(grads_flat, "c")], axis=0)
    core = lax.axis_index("c").astype(jnp.int32).reshape(1)
    terms = param_terms(
        core, normed_both, hidden_both, grads_both, (seq_len * devices) ** (-0.5), head_dim
    )
    attn_grad = jnp.sum(exchange(terms, CHIPS).astype(F32), axis=0)
    grad_normed = jnp.einsum("tjc,jdc->td", grad_qkv, project, preferred_element_type=F32)
    grad_tokens = (grad_hidden + norm_back(normed_one, inverse_one, grad_normed)).astype(BF16)
    return (grad_tokens, attn_grad)


def solution(mesh):
    fine = Mesh(mesh.devices.reshape(SIZES), AXES)
    rows = P(AXES, None)
    in_specs = (
        rows,
        P(DP, None),
        rows,
        rows,
        P(EX, None, None, DP),
        P(EX, DP, None),
        rows,
    )
    return jax.shard_map(
        per_device, mesh=fine, in_specs=in_specs, out_specs=(rows, rows), check_vma=False
    )
```

```python
import jax
import jax.numpy as jnp
from jax import lax
from jax.experimental import pallas as pl
from jax.experimental.pallas import tpu as pltpu
from jax.sharding import Mesh, PartitionSpec as P

EPSILON = 1e-05
MASKED = -1e30
AXES = ("z", "yh", "x", "yl", "c")
DP = ("z", "yh")
EX = ("x", "yl", "c")
CHIPS = ("z", "yh", "x", "yl")
SIZES = (4, 2, 4, 2, 2)
EXPERTS = 16
N_DP = 8
CAP = 10
MAIN = 8
HEADS = 2
HALF = 96
PADDED = 768
F32 = jnp.float32
BF16 = jnp.bfloat16


def layer_norm(values):
    widened = values.astype(F32)
    center = widened - jnp.mean(widened, axis=-1, keepdims=True)
    inverse = lax.rsqrt(jnp.mean(center * center, axis=-1, keepdims=True) + EPSILON)
    return (center * inverse, inverse)


def norm_back(normed, inverse, upstream):
    mean_grad = jnp.mean(upstream, axis=-1, keepdims=True)
    mean_proj = jnp.mean(upstream * normed, axis=-1, keepdims=True)
    return inverse * (upstream - mean_grad - normed * mean_proj)


def contract(first_op, second_op, first_dim, second_dim):
    return lax.dot_general(
        first_op,
        second_op,
        (((first_dim,), (second_dim,)), ((), ())),
        preferred_element_type=F32,
    )


def swap(values, axis):
    return lax.ppermute(values, axis, [(0, 1), (1, 0)])


def along_z(values, shift):
    return lax.ppermute(values, "z", [(i, (i + shift) % 4) for i in range(4)])


def exchange(blocks, axes):
    return lax.all_to_all(blocks, axes, split_axis=0, concat_axis=0, tiled=True)


def after(value, *earlier):
    return lax.optimization_barrier((value,) + earlier)[0]


def add_round(first, *others):
    total = first.astype(F32)
    for other in others:
        total = total + other.astype(F32)
    return total.astype(BF16)


def slot_matrix(expert_ids, seq_len):
    flat = expert_ids.reshape(-1)
    one_hot = (flat[:, None] == jnp.arange(EXPERTS, dtype=jnp.int32)[None, :]).astype(F32)
    rows = jnp.arange(seq_len)
    earlier = (rows[:, None] > rows[None, :]).astype(F32)
    before = jnp.dot(earlier, one_hot, preferred_element_type=F32)
    position = jnp.sum(before * one_hot, axis=1).astype(jnp.int32)
    rest = CAP - MAIN
    target = jnp.where(
        position < MAIN, flat * MAIN + position, EXPERTS * MAIN + flat * rest + position - MAIN
    )
    return (jnp.arange(EXPERTS * CAP, dtype=jnp.int32)[:, None] == target[None, :]).astype(BF16)


def place_kernel(places, piece, at_ref, *refs):
    block_refs, out_ref, sems = refs[: len(places)], refs[-2], refs[-1]
    copies = []
    number = 0
    for ref, parts in zip(block_refs, places):
        for i, (s, r, half) in enumerate(parts):
            z = lax.rem(at_ref[0] - s + 4, 4)
            yh = lax.rem(at_ref[1] + r, 2)
            copy = pltpu.make_async_copy(
                ref.at[pl.ds(i * piece, piece)], out_ref.at[z * 2 + yh, pl.ds(half * piece, piece)], sems.at[number]
            )
            copy.start()
            copies.append(copy)
            number += 1
    for copy in copies:
        copy.wait()


def gather_params(attn_param, earlier, normed):
    rows, head_dim = attn_param.shape
    half = rows // 2
    piece = half // 2
    core = lax.axis_index("c")
    own = lax.dynamic_slice_in_dim(attn_param, core * half, half, 0)
    first, second = own[:piece], own[piece:]
    around = [along_z(first, s) for s in (1, 3, 2)]
    own_y = swap(own, "yh")
    pair = after(jnp.concatenate([second, own_y[piece:]], axis=0), around[0], around[1])
    normed = swap(normed, "c")
    earlier = after(earlier, own_y, normed, *around)
    around_y = [swap(block, "yh") for block in around]
    pairs = [along_z(pair, s) for s in (1, 3, 2)]
    blocks = [own, own_y] + around + around_y + pairs
    places = (
        [[(0, 0, 0), (0, 0, 1)], [(0, 1, 0), (0, 1, 1)]]
        + [[(s, 0, 0)] for s in (1, 3, 2)]
        + [[(s, 1, 0)] for s in (1, 3, 2)]
        + [[(s, 0, 1), (s, 1, 1)] for s in (1, 3, 2)]
    )
    spread = spread_near(earlier, *around_y)
    at = jnp.stack([lax.axis_index("z"), lax.axis_index("yh")]).astype(jnp.int32)
    at = after(at, *spread[1:4])
    anywhere = pl.BlockSpec(memory_space=pl.ANY)
    own = pl.pallas_call(
        lambda *refs: place_kernel(places, piece, *refs),
        out_shape=jax.ShapeDtypeStruct((N_DP, half, head_dim), BF16),
        in_specs=[pl.BlockSpec(memory_space=pltpu.SMEM)] + [anywhere] * len(blocks),
        out_specs=pl.BlockSpec(memory_space=pltpu.VMEM),
        scratch_shapes=[pltpu.SemaphoreType.DMA((16,))],
        compiler_params=pltpu.CompilerParams(vmem_limit_bytes=60 * 1024 * 1024),
    )(at, *blocks)
    other = swap(own, "c")
    first = jnp.where(core == 0, own, other)
    second = jnp.where(core == 0, other, own)
    return jnp.stack([first, second], axis=1).reshape(N_DP * rows, head_dim), spread, normed


def between_experts(rows):
    features = rows.shape[1]
    cut = EXPERTS * MAIN
    extra = rows[cut:].reshape(cut, -1)
    packed = jnp.concatenate([rows[:cut], extra], axis=1)
    width = packed.shape[1]
    packed = exchange(packed.reshape(EXPERTS, MAIN, width), EX).reshape(cut, width)
    extra = packed[:, features:].reshape(-1, features)
    return packed[:, :features], extra


def spread_near(own, *earlier):
    one = own[:HALF]
    own_y = swap(after(own, *earlier) if earlier else own, "yh")
    return [own, own_y] + [along_z(one, s) for s in (1, 3, 2)]


def spread_far(near, *earlier):
    own, own_y, near_z, far_z, across = near
    pair = after(jnp.concatenate([own[HALF:], own_y[HALF:]], axis=0), near_z, far_z)
    near_z = after(near_z, *earlier) if earlier else near_z
    first = [swap(block, "yh") for block in (near_z, far_z, across)]
    return first + [along_z(pair, s) for s in (1, 3, 2)]


def collect(near, far):
    kept, one_y, two_y, *one_z = near
    early = [along_z(block, -s) for block, s in zip(one_z, (1, 3, 2))]
    early_y = swap(two_y, "yh")
    *one_yz, two_z, two_yz = far
    (*one_yz, two_yz), early, early_y = lax.optimization_barrier(([*one_yz, two_yz], early, early_y))
    late = [along_z(block, -s) for block, s in zip(one_yz, (1, 3, 2))]
    swapped = swap(two_yz, "yh")
    across = swap(add_round(one_y, *late), "yh")
    pairs = add_round(two_z, swapped)
    rest = kept.shape[0] - HALF
    back = [along_z(pairs[i * rest : (i + 1) * rest], -s) for i, s in enumerate((1, 3, 2))]
    one = add_round(kept[:HALF], across, *early)
    two = add_round(kept[HALF:], early_y, *back)
    return jnp.concatenate([one, two], axis=0)


def load(source, target, sem):
    copy = pltpu.make_async_copy(source, target, sem)
    copy.start()
    return copy


def act_kernel(counts, *refs):
    count = len(counts)
    cot_refs, outer_ref, out_ref = refs[:count], refs[count], refs[count + 1]
    cot, outer_map, row_sem, map_sem = refs[count + 2 :]
    hidden, features = outer_ref.shape
    copies = [load(outer_ref, outer_map.at[pl.ds(0, hidden)], map_sem.at[0])]
    for i, ref in enumerate(cot_refs):
        copies.append(load(ref, cot.at[pl.ds(sum(counts[:i]), counts[i])], row_sem.at[i]))
    outer_map[pl.ds(hidden, PADDED - hidden)] = jnp.zeros((PADDED - hidden, features), BF16)
    for copy in copies:
        copy.wait()
    tall = sum(counts) // 2

    @pl.loop(0, 2)
    def _(step):
        here = pl.ds(pl.multiple_of(step * tall, 16), tall)
        out_ref[here] = contract(cot[here], outer_map[...], 1, 1).astype(BF16)


def act_grads(cot_blocks, outer):
    counts = [block.shape[0] for block in cot_blocks]
    features = outer.shape[1]
    total = sum(counts)
    anywhere = pl.BlockSpec(memory_space=pl.ANY)
    return pl.pallas_call(
        lambda *refs: act_kernel(counts, *refs),
        out_shape=jax.ShapeDtypeStruct((total, PADDED), BF16),
        in_specs=[anywhere] * (len(counts) + 1),
        out_specs=pl.BlockSpec(memory_space=pltpu.VMEM),
        scratch_shapes=[
            pltpu.VMEM((total, features), BF16),
            pltpu.VMEM((PADDED, features), BF16),
            pltpu.SemaphoreType.DMA((len(counts),)),
            pltpu.SemaphoreType.DMA((1,)),
        ],
        compiler_params=pltpu.CompilerParams(vmem_limit_bytes=60 * 1024 * 1024),
        cost_estimate=pl.CostEstimate(
            flops=2 * total * features * PADDED,
            bytes_accessed=2 * (total + PADDED) * features,
            transcendentals=0,
        ),
    )(*cot_blocks, outer)


def expert_kernel(counts, pieces_out, tall, *refs):
    count = len(counts)
    outs = len(pieces_out)
    normed_refs = refs[:count]
    act_ref, inner_ref = refs[count : count + 2]
    out_refs = refs[count + 2 : count + 2 + outs]
    (normed, acts, gate_map, up_map, grad_gate, grad_up, result, row_sem, act_sem, map_sem, out_sem) = refs[
        count + 2 + outs :
    ]
    _, hidden, features = inner_ref.shape
    pieces = [(0, 256), (256, 256), (512, hidden - 512)]
    rows_in = [
        load(ref, normed.at[pl.ds(sum(counts[:i]), counts[i])], row_sem.at[i])
        for i, ref in enumerate(normed_refs)
    ]
    maps_in = []
    for i, (start, size) in enumerate(pieces):
        at = pl.ds(start, size)
        maps_in.append(
            [
                load(inner_ref.at[0, at], gate_map.at[at], map_sem.at[0, i]),
                load(inner_ref.at[1, at], up_map.at[at], map_sem.at[1, i]),
            ]
        )
        if i == 0:
            rows_in.append(load(act_ref, acts, act_sem.at[0]))
    blank = jnp.zeros((PADDED - hidden, features), BF16)
    for ref in (gate_map, up_map):
        ref[pl.ds(hidden, PADDED - hidden)] = blank
    for copy in rows_in:
        copy.wait()
    steps = sum(counts) // tall

    for i in range(len(pieces)):
        for copy in maps_in[i]:
            copy.wait()
        at = pl.ds(i * 256, 256)

        @pl.loop(0, steps)
        def _(step):
            here = pl.ds(pl.multiple_of(step * tall, 16), tall)
            gate_part = contract(normed[here], gate_map[at], 1, 1)
            up_part = contract(normed[here], up_map[at], 1, 1)
            squash = 1.0 / (1.0 + jnp.exp(-gate_part))
            scaled = acts[here, at].astype(F32) * squash
            grad_gate[here, at] = (scaled * up_part * (1.0 + gate_part * (1.0 - squash))).astype(BF16)
            grad_up[here, at] = (scaled * gate_part).astype(BF16)

    wide = 512
    copies = []
    for n in range(features // wide):
        lanes = pl.ds(n * wide, wide)

        @pl.loop(0, steps)
        def _(step):
            here = pl.ds(pl.multiple_of(step * tall, 16), tall)
            result[here, lanes] = (
                contract(grad_gate[here], gate_map[:, lanes], 1, 0)
                + contract(grad_up[here], up_map[:, lanes], 1, 0)
            ).astype(BF16)

        number = 0
        for ref, parts in zip(out_refs, pieces_out):
            at = 0
            for start, size in parts:
                copies.append(
                    load(
                        result.at[pl.ds(start, size), lanes],
                        ref.at[pl.ds(at, size), lanes],
                        out_sem.at[n, number],
                    )
                )
                at += size
                number += 1
    for copy in copies:
        copy.wait()


def experts(normed_blocks, acts, inner, pieces_out, tall):
    counts = [block.shape[0] for block in normed_blocks]
    features = normed_blocks[0].shape[1]
    total = sum(counts)
    anywhere = pl.BlockSpec(memory_space=pl.ANY)
    return pl.pallas_call(
        lambda *refs: expert_kernel(counts, pieces_out, tall, *refs),
        out_shape=[
            jax.ShapeDtypeStruct((sum(size for _, size in parts), features), BF16) for parts in pieces_out
        ],
        in_specs=[anywhere] * (len(counts) + 2),
        out_specs=[anywhere] * len(pieces_out),
        scratch_shapes=[
            pltpu.VMEM((total, features), BF16),
            pltpu.VMEM((total, PADDED), BF16),
            pltpu.VMEM((PADDED, features), BF16),
            pltpu.VMEM((PADDED, features), BF16),
            pltpu.VMEM((total, PADDED), BF16),
            pltpu.VMEM((total, PADDED), BF16),
            pltpu.VMEM((total, features), BF16),
            pltpu.SemaphoreType.DMA((len(counts),)),
            pltpu.SemaphoreType.DMA((1,)),
            pltpu.SemaphoreType.DMA((2, 3)),
            pltpu.SemaphoreType.DMA((features // 512, sum(len(parts) for parts in pieces_out))),
        ],
        compiler_params=pltpu.CompilerParams(vmem_limit_bytes=60 * 1024 * 1024),
        cost_estimate=pl.CostEstimate(
            flops=8 * total * features * PADDED,
            bytes_accessed=4 * total * features + 4 * PADDED * features,
            transcendentals=total * PADDED,
        ),
    )(*normed_blocks, acts, inner)


def param_kernel(scale, head_dim, core_ref, normed_ref, hidden_ref, grads_ref, out_ref, terms):
    features = normed_ref.shape[1]
    tile = 1024
    for block in range(6):
        left_ref = normed_ref if block < 4 else hidden_ref
        right = grads_ref[:, block * head_dim : (block + 1) * head_dim]
        for start in range(0, features, tile):
            part = contract(left_ref[:, start : start + tile], right, 0, 0) * scale
            terms[pl.ds(block * features + start, tile)] = part.astype(BF16)
    core = core_ref[0]

    @pl.loop(0, out_ref.shape[0])
    def _(group):
        size = out_ref.shape[1]
        out_ref[group] = terms[pl.ds(pl.multiple_of((2 * group + core) * size, 16), size)]


def param_terms(core, normed, hidden, grads, scale, head_dim):
    features = normed.shape[1]
    rows = 6 * features
    whole = pl.BlockSpec(memory_space=pltpu.VMEM)
    return pl.pallas_call(
        lambda *refs: param_kernel(scale, head_dim, *refs),
        out_shape=jax.ShapeDtypeStruct((64, rows // 128, head_dim), BF16),
        in_specs=[pl.BlockSpec(memory_space=pltpu.SMEM)] + [whole] * 3,
        out_specs=whole,
        scratch_shapes=[pltpu.VMEM((rows, head_dim), BF16)],
        compiler_params=pltpu.CompilerParams(vmem_limit_bytes=40 * 1024 * 1024),
        cost_estimate=pl.CostEstimate(
            flops=2 * rows * head_dim * normed.shape[0], bytes_accessed=8 * 1024 * 1024, transcendentals=0
        ),
    )(core, normed, hidden, grads)


def per_device(tokens, attn_param, expert_ids, gate_score, w_in, w_out, cotangent):
    seq_len, features = tokens.shape
    head_dim = attn_param.shape[1]
    score_scale = head_dim ** (-0.5)
    devices = N_DP * EXPERTS
    slots = slot_matrix(expert_ids, seq_len)
    inner = jnp.transpose(w_in[0], (1, 2, 0))
    outer = w_out[0]

    cot_main, cot_extra = between_experts(contract(slots, cotangent, 1, 0).astype(BF16))
    cot_rows = jnp.concatenate([cot_main, cot_extra], axis=0)
    normed_one, inverse_one = layer_norm(tokens)
    normed_one_b = normed_one.astype(BF16)
    packed, cot_near, normed_other = gather_params(attn_param, cot_rows, normed_one_b)
    cot_far = spread_far(cot_near)

    normed_both = jnp.concatenate([normed_one_b, normed_other], axis=0)
    blocks = packed.reshape(2 * HEADS + 2, features, head_dim)
    project = blocks[: HEADS + 2]
    out_blocks = blocks[HEADS + 2 :]
    projected = jnp.einsum(
        "td,jdc->tjc", normed_one_b, project, preferred_element_type=F32
    ).astype(BF16)
    queries = projected[:, :HEADS]
    key_rows = projected[:, HEADS]
    value_rows = projected[:, HEADS + 1]
    scores = jnp.einsum("qhc,kc->hqk", queries, key_rows, preferred_element_type=F32) * score_scale
    causal = lax.broadcasted_iota(jnp.int32, (seq_len, seq_len), 0) >= lax.broadcasted_iota(
        jnp.int32, (seq_len, seq_len), 1
    )
    scores = jnp.where(causal[None], scores, MASKED)
    row_max = jnp.max(scores, axis=2, keepdims=True)
    raised = jnp.exp(scores - row_max)
    attention = raised / jnp.sum(raised, axis=2, keepdims=True)
    attention_b = attention.astype(BF16)
    context = jnp.einsum(
        "hqk,kc->qhc", attention_b, value_rows, preferred_element_type=F32
    ).astype(BF16)
    context_flat = context.reshape(seq_len, HEADS * head_dim)
    attn_out = jnp.einsum("thc,hdc->td", context, out_blocks, preferred_element_type=F32)
    residual = (tokens.astype(F32) + attn_out).astype(BF16)
    normed_two, inverse_two = layer_norm(residual)
    normed_two_b = after(normed_two.astype(BF16), cot_near[4], cot_far[0], cot_far[1], cot_far[3], cot_far[4])
    main, extra = between_experts(contract(slots, normed_two_b, 1, 0).astype(BF16))
    near_acts = act_grads(cot_near, outer)
    far_acts = act_grads(cot_far, outer)
    near = spread_near(after(jnp.concatenate([main, extra], axis=0), near_acts, cot_far[2], cot_far[5]))
    h = HALF
    whole = EXPERTS * CAP
    rest = whole - h
    near_rows = experts(
        near,
        near_acts,
        inner,
        [[(0, whole)], [(whole, h)], [(whole + h, rest)]] + [[(2 * whole + i * h, h)] for i in range(3)],
        2 * whole + 3 * h,
    )
    far = spread_far(near, far_acts)
    far[0] = after(far[0], near_rows[0])
    far_rows = experts(
        far,
        far_acts,
        inner,
        [[(i * h, h)] for i in range(3)]
        + [[(3 * h + (2 * i + r) * rest, rest) for i in range(3)] for r in (0, 1)],
        (h + 2 * rest) * 3,
    )
    back_main, back_extra = between_experts(collect(near_rows, far_rows))
    cut = EXPERTS * MAIN
    back_rows = contract(slots[:cut], back_main, 0, 0) + contract(slots[cut:], back_extra, 0, 0)
    moe_grad = gate_score * back_rows
    grad_hidden = cotangent.astype(F32) + norm_back(normed_two, inverse_two, moe_grad)
    grad_hidden_b = grad_hidden.astype(BF16)
    hidden_both = jnp.concatenate([grad_hidden_b, swap(grad_hidden_b, "c")], axis=0)
    grad_context = jnp.einsum(
        "td,hdc->thc", grad_hidden_b, out_blocks, preferred_element_type=F32
    )
    grad_context_b = grad_context.astype(BF16)
    grad_attention = jnp.einsum(
        "qhc,kc->hqk", grad_context_b, value_rows, preferred_element_type=F32
    )
    grad_value = jnp.einsum("hqk,qhc->kc", attention_b, grad_context_b, preferred_element_type=F32)
    grad_scores = (
        attention
        * (grad_attention - jnp.sum(grad_attention * attention, axis=2, keepdims=True))
        * score_scale
    )
    grad_scores_b = grad_scores.astype(BF16)
    grad_query = jnp.einsum("hqk,kc->qhc", grad_scores_b, key_rows, preferred_element_type=F32)
    grad_key = jnp.einsum("hqk,qhc->kc", grad_scores_b, queries, preferred_element_type=F32)
    grad_qkv = jnp.concatenate([grad_query, grad_key[:, None], grad_value[:, None]], axis=1).astype(BF16)
    grads_flat = jnp.concatenate([grad_qkv.reshape(seq_len, (HEADS + 2) * head_dim), context_flat], axis=1)
    grads_both = jnp.concatenate([grads_flat, swap(grads_flat, "c")], axis=0)
    core = lax.axis_index("c").astype(jnp.int32).reshape(1)
    terms = param_terms(
        core, normed_both, hidden_both, grads_both, (seq_len * devices) ** (-0.5), head_dim
    )
    attn_grad = jnp.sum(exchange(terms, CHIPS).astype(F32), axis=0)
    grad_normed = jnp.einsum("tjc,jdc->td", grad_qkv, project, preferred_element_type=F32)
    grad_tokens = (grad_hidden + norm_back(normed_one, inverse_one, grad_normed)).astype(BF16)
    return (grad_tokens, attn_grad)


def solution(mesh):
    fine = Mesh(mesh.devices.reshape(SIZES), AXES)
    rows = P(AXES, None)
    in_specs = (
        rows,
        P(DP, None),
        rows,
        rows,
        P(EX, None, None, DP),
        P(EX, DP, None),
        rows,
    )
    return jax.shard_map(
        per_device, mesh=fine, in_specs=in_specs, out_specs=(rows, rows), check_vma=False
    )
```

```python
import jax
import jax.numpy as jnp
from jax import lax
from jax.experimental import pallas as pl
from jax.experimental.pallas import tpu as pltpu
from jax.sharding import Mesh, PartitionSpec as P

EPSILON = 1e-05
MASKED = -1e30
AXES = ("z", "yh", "x", "yl", "c")
DP = ("z", "yh")
EX = ("x", "yl", "c")
CHIPS = ("z", "yh", "x", "yl")
SIZES = (4, 2, 4, 2, 2)
EXPERTS = 16
N_DP = 8
CAP = 10
MAIN = 8
HEADS = 2
HALF = 96
PADDED = 768
F32 = jnp.float32
BF16 = jnp.bfloat16


def layer_norm(values):
    widened = values.astype(F32)
    center = widened - jnp.mean(widened, axis=-1, keepdims=True)
    inverse = lax.rsqrt(jnp.mean(center * center, axis=-1, keepdims=True) + EPSILON)
    return (center * inverse, inverse)


def norm_back(normed, inverse, upstream):
    mean_grad = jnp.mean(upstream, axis=-1, keepdims=True)
    mean_proj = jnp.mean(upstream * normed, axis=-1, keepdims=True)
    return inverse * (upstream - mean_grad - normed * mean_proj)


def contract(first_op, second_op, first_dim, second_dim):
    return lax.dot_general(
        first_op,
        second_op,
        (((first_dim,), (second_dim,)), ((), ())),
        preferred_element_type=F32,
    )


def swap(values, axis):
    return lax.ppermute(values, axis, [(0, 1), (1, 0)])


def along_z(values, shift):
    return lax.ppermute(values, "z", [(i, (i + shift) % 4) for i in range(4)])


def exchange(blocks, axes):
    return lax.all_to_all(blocks, axes, split_axis=0, concat_axis=0, tiled=True)


def after(value, *earlier):
    return lax.optimization_barrier((value,) + earlier)[0]


def add_round(first, *others):
    total = first.astype(F32)
    for other in others:
        total = total + other.astype(F32)
    return total.astype(BF16)


def slot_matrix(expert_ids, seq_len):
    flat = expert_ids.reshape(-1)
    one_hot = (flat[:, None] == jnp.arange(EXPERTS, dtype=jnp.int32)[None, :]).astype(F32)
    rows = jnp.arange(seq_len)
    earlier = (rows[:, None] > rows[None, :]).astype(F32)
    before = jnp.dot(earlier, one_hot, preferred_element_type=F32)
    position = jnp.sum(before * one_hot, axis=1).astype(jnp.int32)
    rest = CAP - MAIN
    target = jnp.where(
        position < MAIN, flat * MAIN + position, EXPERTS * MAIN + flat * rest + position - MAIN
    )
    return (jnp.arange(EXPERTS * CAP, dtype=jnp.int32)[:, None] == target[None, :]).astype(BF16)


def place_kernel(places, piece, at_ref, *refs):
    block_refs, out_ref, sems = refs[: len(places)], refs[-2], refs[-1]
    copies = []
    number = 0
    for ref, parts in zip(block_refs, places):
        for i, (s, r, half) in enumerate(parts):
            z = lax.rem(at_ref[0] - s + 4, 4)
            yh = lax.rem(at_ref[1] + r, 2)
            copy = pltpu.make_async_copy(
                ref.at[pl.ds(i * piece, piece)], out_ref.at[z * 2 + yh, pl.ds(half * piece, piece)], sems.at[number]
            )
            copy.start()
            copies.append(copy)
            number += 1
    for copy in copies:
        copy.wait()


def gather_params(attn_param, earlier, normed):
    rows, head_dim = attn_param.shape
    half = rows // 2
    piece = half // 2
    core = lax.axis_index("c")
    own = lax.dynamic_slice_in_dim(attn_param, core * half, half, 0)
    first, second = own[:piece], own[piece:]
    around = [along_z(first, s) for s in (1, 3, 2)]
    own_y = swap(own, "yh")
    pair = after(jnp.concatenate([second, own_y[piece:]], axis=0), around[0], around[1])
    normed = swap(normed, "c")
    earlier = after(earlier, own_y, normed, *around)
    around_y = [swap(block, "yh") for block in around]
    pairs = [along_z(pair, s) for s in (1, 3, 2)]
    blocks = [own, own_y] + around + around_y + pairs
    places = (
        [[(0, 0, 0), (0, 0, 1)], [(0, 1, 0), (0, 1, 1)]]
        + [[(s, 0, 0)] for s in (1, 3, 2)]
        + [[(s, 1, 0)] for s in (1, 3, 2)]
        + [[(s, 0, 1), (s, 1, 1)] for s in (1, 3, 2)]
    )
    spread = spread_near(earlier, *around_y)
    at = jnp.stack([lax.axis_index("z"), lax.axis_index("yh")]).astype(jnp.int32)
    at = after(at, *spread[1:4])
    anywhere = pl.BlockSpec(memory_space=pl.ANY)
    own = pl.pallas_call(
        lambda *refs: place_kernel(places, piece, *refs),
        out_shape=jax.ShapeDtypeStruct((N_DP, half, head_dim), BF16),
        in_specs=[pl.BlockSpec(memory_space=pltpu.SMEM)] + [anywhere] * len(blocks),
        out_specs=pl.BlockSpec(memory_space=pltpu.VMEM),
        scratch_shapes=[pltpu.SemaphoreType.DMA((16,))],
        compiler_params=pltpu.CompilerParams(vmem_limit_bytes=60 * 1024 * 1024),
    )(at, *blocks)
    other = swap(own, "c")
    first = jnp.where(core == 0, own, other)
    second = jnp.where(core == 0, other, own)
    return jnp.stack([first, second], axis=1).reshape(N_DP * rows, head_dim), spread, normed


def between_experts(rows):
    features = rows.shape[1]
    cut = EXPERTS * MAIN
    extra = rows[cut:].reshape(cut, -1)
    packed = jnp.concatenate([rows[:cut], extra], axis=1)
    width = packed.shape[1]
    packed = exchange(packed.reshape(EXPERTS, MAIN, width), EX).reshape(cut, width)
    extra = packed[:, features:].reshape(-1, features)
    return packed[:, :features], extra


def spread_near(own, *earlier):
    one = own[:HALF]
    own_y = swap(after(own, *earlier) if earlier else own, "yh")
    return [own, own_y] + [along_z(one, s) for s in (1, 3, 2)]


def spread_far(near, *earlier):
    own, own_y, near_z, far_z, across = near
    pair = after(jnp.concatenate([own[HALF:], own_y[HALF:]], axis=0), near_z, far_z)
    near_z = after(near_z, *earlier) if earlier else near_z
    first = [swap(block, "yh") for block in (near_z, far_z, across)]
    return first + [along_z(pair, s) for s in (1, 3, 2)]


def collect(near, far):
    kept, one_y, two_y, *one_z = near
    early = [along_z(block, -s) for block, s in zip(one_z, (1, 3, 2))]
    early_y = swap(two_y, "yh")
    one_yz, two_z, two_yz = far[:3], far[3:6], far[6:]
    one_yz, two_yz, early, early_y = lax.optimization_barrier((one_yz, two_yz, early, early_y))
    swapped = [swap(block, "yh") for block in two_yz]
    late = [along_z(block, -s) for block, s in zip(one_yz, (1, 3, 2))]
    back = [along_z(add_round(two_z[i], swapped[i]), -s) for i, s in enumerate((1, 3, 2))]
    across = swap(add_round(one_y, *late), "yh")
    one = add_round(kept[:HALF], across, *early)
    two = add_round(kept[HALF:], early_y, *back)
    return jnp.concatenate([one, two], axis=0)


def load(source, target, sem):
    copy = pltpu.make_async_copy(source, target, sem)
    copy.start()
    return copy


def act_kernel(counts, *refs):
    count = len(counts)
    cot_refs, outer_ref, out_ref = refs[:count], refs[count], refs[count + 1]
    cot, outer_map, row_sem, map_sem = refs[count + 2 :]
    hidden, features = outer_ref.shape
    copies = [load(outer_ref, outer_map.at[pl.ds(0, hidden)], map_sem.at[0])]
    for i, ref in enumerate(cot_refs):
        copies.append(load(ref, cot.at[pl.ds(sum(counts[:i]), counts[i])], row_sem.at[i]))
    outer_map[pl.ds(hidden, PADDED - hidden)] = jnp.zeros((PADDED - hidden, features), BF16)
    for copy in copies:
        copy.wait()
    tall = sum(counts) // 2

    @pl.loop(0, 2)
    def _(step):
        here = pl.ds(pl.multiple_of(step * tall, 16), tall)
        out_ref[here] = contract(cot[here], outer_map[...], 1, 1).astype(BF16)


def act_grads(cot_blocks, outer):
    counts = [block.shape[0] for block in cot_blocks]
    features = outer.shape[1]
    total = sum(counts)
    anywhere = pl.BlockSpec(memory_space=pl.ANY)
    return pl.pallas_call(
        lambda *refs: act_kernel(counts, *refs),
        out_shape=jax.ShapeDtypeStruct((total, PADDED), BF16),
        in_specs=[anywhere] * (len(counts) + 1),
        out_specs=pl.BlockSpec(memory_space=pltpu.VMEM),
        scratch_shapes=[
            pltpu.VMEM((total, features), BF16),
            pltpu.VMEM((PADDED, features), BF16),
            pltpu.SemaphoreType.DMA((len(counts),)),
            pltpu.SemaphoreType.DMA((1,)),
        ],
        compiler_params=pltpu.CompilerParams(vmem_limit_bytes=60 * 1024 * 1024),
        cost_estimate=pl.CostEstimate(
            flops=2 * total * features * PADDED,
            bytes_accessed=2 * (total + PADDED) * features,
            transcendentals=0,
        ),
    )(*cot_blocks, outer)


def expert_kernel(counts, pieces_out, tall, *refs):
    count = len(counts)
    outs = len(pieces_out)
    normed_refs = refs[:count]
    act_ref, inner_ref = refs[count : count + 2]
    out_refs = refs[count + 2 : count + 2 + outs]
    (normed, acts, gate_map, up_map, grad_gate, grad_up, result, row_sem, act_sem, map_sem, out_sem) = refs[
        count + 2 + outs :
    ]
    _, hidden, features = inner_ref.shape
    pieces = [(0, 256), (256, 256), (512, hidden - 512)]
    rows_in = [
        load(ref, normed.at[pl.ds(sum(counts[:i]), counts[i])], row_sem.at[i])
        for i, ref in enumerate(normed_refs)
    ]
    maps_in = []
    for i, (start, size) in enumerate(pieces):
        at = pl.ds(start, size)
        maps_in.append(
            [
                load(inner_ref.at[0, at], gate_map.at[at], map_sem.at[0, i]),
                load(inner_ref.at[1, at], up_map.at[at], map_sem.at[1, i]),
            ]
        )
        if i == 0:
            rows_in.append(load(act_ref, acts, act_sem.at[0]))
    blank = jnp.zeros((PADDED - hidden, features), BF16)
    for ref in (gate_map, up_map):
        ref[pl.ds(hidden, PADDED - hidden)] = blank
    for copy in rows_in:
        copy.wait()
    steps = sum(counts) // tall

    for i in range(len(pieces)):
        for copy in maps_in[i]:
            copy.wait()
        at = pl.ds(i * 256, 256)

        @pl.loop(0, steps)
        def _(step):
            here = pl.ds(pl.multiple_of(step * tall, 16), tall)
            gate_part = contract(normed[here], gate_map[at], 1, 1)
            up_part = contract(normed[here], up_map[at], 1, 1)
            squash = 1.0 / (1.0 + jnp.exp(-gate_part))
            scaled = acts[here, at].astype(F32) * squash
            grad_gate[here, at] = (scaled * up_part * (1.0 + gate_part * (1.0 - squash))).astype(BF16)
            grad_up[here, at] = (scaled * gate_part).astype(BF16)

    wide = 512
    copies = []
    for n in range(features // wide):
        lanes = pl.ds(n * wide, wide)

        @pl.loop(0, steps)
        def _(step):
            here = pl.ds(pl.multiple_of(step * tall, 16), tall)
            result[here, lanes] = (
                contract(grad_gate[here], gate_map[:, lanes], 1, 0)
                + contract(grad_up[here], up_map[:, lanes], 1, 0)
            ).astype(BF16)

        number = 0
        for ref, parts in zip(out_refs, pieces_out):
            at = 0
            for start, size in parts:
                copies.append(
                    load(
                        result.at[pl.ds(start, size), lanes],
                        ref.at[pl.ds(at, size), lanes],
                        out_sem.at[n, number],
                    )
                )
                at += size
                number += 1
    for copy in copies:
        copy.wait()


def experts(normed_blocks, acts, inner, pieces_out, tall):
    counts = [block.shape[0] for block in normed_blocks]
    features = normed_blocks[0].shape[1]
    total = sum(counts)
    anywhere = pl.BlockSpec(memory_space=pl.ANY)
    return pl.pallas_call(
        lambda *refs: expert_kernel(counts, pieces_out, tall, *refs),
        out_shape=[
            jax.ShapeDtypeStruct((sum(size for _, size in parts), features), BF16) for parts in pieces_out
        ],
        in_specs=[anywhere] * (len(counts) + 2),
        out_specs=[anywhere] * len(pieces_out),
        scratch_shapes=[
            pltpu.VMEM((total, features), BF16),
            pltpu.VMEM((total, PADDED), BF16),
            pltpu.VMEM((PADDED, features), BF16),
            pltpu.VMEM((PADDED, features), BF16),
            pltpu.VMEM((total, PADDED), BF16),
            pltpu.VMEM((total, PADDED), BF16),
            pltpu.VMEM((total, features), BF16),
            pltpu.SemaphoreType.DMA((len(counts),)),
            pltpu.SemaphoreType.DMA((1,)),
            pltpu.SemaphoreType.DMA((2, 3)),
            pltpu.SemaphoreType.DMA((features // 512, sum(len(parts) for parts in pieces_out))),
        ],
        compiler_params=pltpu.CompilerParams(vmem_limit_bytes=60 * 1024 * 1024),
        cost_estimate=pl.CostEstimate(
            flops=8 * total * features * PADDED,
            bytes_accessed=4 * total * features + 4 * PADDED * features,
            transcendentals=total * PADDED,
        ),
    )(*normed_blocks, acts, inner)


def param_kernel(scale, head_dim, core_ref, normed_ref, hidden_ref, grads_ref, out_ref, terms):
    features = normed_ref.shape[1]
    tile = 1024
    for block in range(6):
        left_ref = normed_ref if block < 4 else hidden_ref
        right = grads_ref[:, block * head_dim : (block + 1) * head_dim]
        for start in range(0, features, tile):
            part = contract(left_ref[:, start : start + tile], right, 0, 0) * scale
            terms[pl.ds(block * features + start, tile)] = part.astype(BF16)
    core = core_ref[0]

    @pl.loop(0, out_ref.shape[0])
    def _(group):
        size = out_ref.shape[1]
        out_ref[group] = terms[pl.ds(pl.multiple_of((2 * group + core) * size, 16), size)]


def param_terms(core, normed, hidden, grads, scale, head_dim):
    features = normed.shape[1]
    rows = 6 * features
    whole = pl.BlockSpec(memory_space=pltpu.VMEM)
    return pl.pallas_call(
        lambda *refs: param_kernel(scale, head_dim, *refs),
        out_shape=jax.ShapeDtypeStruct((64, rows // 128, head_dim), BF16),
        in_specs=[pl.BlockSpec(memory_space=pltpu.SMEM)] + [whole] * 3,
        out_specs=whole,
        scratch_shapes=[pltpu.VMEM((rows, head_dim), BF16)],
        compiler_params=pltpu.CompilerParams(vmem_limit_bytes=40 * 1024 * 1024),
        cost_estimate=pl.CostEstimate(
            flops=2 * rows * head_dim * normed.shape[0], bytes_accessed=8 * 1024 * 1024, transcendentals=0
        ),
    )(core, normed, hidden, grads)


def per_device(tokens, attn_param, expert_ids, gate_score, w_in, w_out, cotangent):
    seq_len, features = tokens.shape
    head_dim = attn_param.shape[1]
    score_scale = head_dim ** (-0.5)
    devices = N_DP * EXPERTS
    slots = slot_matrix(expert_ids, seq_len)
    inner = jnp.transpose(w_in[0], (1, 2, 0))
    outer = w_out[0]

    cot_main, cot_extra = between_experts(contract(slots, cotangent, 1, 0).astype(BF16))
    cot_rows = jnp.concatenate([cot_main, cot_extra], axis=0)
    normed_one, inverse_one = layer_norm(tokens)
    normed_one_b = normed_one.astype(BF16)
    packed, cot_near, normed_other = gather_params(attn_param, cot_rows, normed_one_b)
    cot_far = spread_far(cot_near)

    normed_both = jnp.concatenate([normed_one_b, normed_other], axis=0)
    blocks = packed.reshape(2 * HEADS + 2, features, head_dim)
    project = blocks[: HEADS + 2]
    out_blocks = blocks[HEADS + 2 :]
    projected = jnp.einsum(
        "td,jdc->tjc", normed_one_b, project, preferred_element_type=F32
    ).astype(BF16)
    queries = projected[:, :HEADS]
    key_rows = projected[:, HEADS]
    value_rows = projected[:, HEADS + 1]
    scores = jnp.einsum("qhc,kc->hqk", queries, key_rows, preferred_element_type=F32) * score_scale
    causal = lax.broadcasted_iota(jnp.int32, (seq_len, seq_len), 0) >= lax.broadcasted_iota(
        jnp.int32, (seq_len, seq_len), 1
    )
    scores = jnp.where(causal[None], scores, MASKED)
    row_max = jnp.max(scores, axis=2, keepdims=True)
    raised = jnp.exp(scores - row_max)
    attention = raised / jnp.sum(raised, axis=2, keepdims=True)
    attention_b = attention.astype(BF16)
    context = jnp.einsum(
        "hqk,kc->qhc", attention_b, value_rows, preferred_element_type=F32
    ).astype(BF16)
    context_flat = context.reshape(seq_len, HEADS * head_dim)
    attn_out = jnp.einsum("thc,hdc->td", context, out_blocks, preferred_element_type=F32)
    residual = (tokens.astype(F32) + attn_out).astype(BF16)
    normed_two, inverse_two = layer_norm(residual)
    normed_two_b = after(normed_two.astype(BF16), cot_near[4], cot_far[0], cot_far[1], cot_far[3], cot_far[4])
    main, extra = between_experts(contract(slots, normed_two_b, 1, 0).astype(BF16))
    near_acts = act_grads(cot_near, outer)
    far_acts = act_grads(cot_far, outer)
    near = spread_near(after(jnp.concatenate([main, extra], axis=0), near_acts, cot_far[2], cot_far[5]))
    h = HALF
    whole = EXPERTS * CAP
    rest = whole - h
    near_rows = experts(
        near,
        near_acts,
        inner,
        [[(0, whole)], [(whole, h)], [(whole + h, rest)]] + [[(2 * whole + i * h, h)] for i in range(3)],
        2 * whole + 3 * h,
    )
    far = spread_far(near, far_acts)
    far[0] = after(far[0], near_rows[0])
    far_rows = experts(
        far,
        far_acts,
        inner,
        [[(i * h, h)] for i in range(3)]
        + [[(3 * h + (2 * i + r) * rest, rest)] for r in (0, 1) for i in range(3)],
        (h + 2 * rest) * 3,
    )
    back_main, back_extra = between_experts(collect(near_rows, far_rows))
    cut = EXPERTS * MAIN
    back_rows = contract(slots[:cut], back_main, 0, 0) + contract(slots[cut:], back_extra, 0, 0)
    moe_grad = gate_score * back_rows
    grad_hidden = cotangent.astype(F32) + norm_back(normed_two, inverse_two, moe_grad)
    grad_hidden_b = grad_hidden.astype(BF16)
    hidden_both = jnp.concatenate([grad_hidden_b, swap(grad_hidden_b, "c")], axis=0)
    grad_context = jnp.einsum(
        "td,hdc->thc", grad_hidden_b, out_blocks, preferred_element_type=F32
    )
    grad_context_b = grad_context.astype(BF16)
    grad_attention = jnp.einsum(
        "qhc,kc->hqk", grad_context_b, value_rows, preferred_element_type=F32
    )
    grad_value = jnp.einsum("hqk,qhc->kc", attention_b, grad_context_b, preferred_element_type=F32)
    grad_scores = (
        attention
        * (grad_attention - jnp.sum(grad_attention * attention, axis=2, keepdims=True))
        * score_scale
    )
    grad_scores_b = grad_scores.astype(BF16)
    grad_query = jnp.einsum("hqk,kc->qhc", grad_scores_b, key_rows, preferred_element_type=F32)
    grad_key = jnp.einsum("hqk,qhc->kc", grad_scores_b, queries, preferred_element_type=F32)
    grad_qkv = jnp.concatenate([grad_query, grad_key[:, None], grad_value[:, None]], axis=1).astype(BF16)
    grads_flat = jnp.concatenate([grad_qkv.reshape(seq_len, (HEADS + 2) * head_dim), context_flat], axis=1)
    grads_both = jnp.concatenate([grads_flat, swap(grads_flat, "c")], axis=0)
    core = lax.axis_index("c").astype(jnp.int32).reshape(1)
    terms = param_terms(
        core, normed_both, hidden_both, grads_both, (seq_len * devices) ** (-0.5), head_dim
    )
    attn_grad = jnp.sum(exchange(terms, CHIPS).astype(F32), axis=0)
    grad_normed = jnp.einsum("tjc,jdc->td", grad_qkv, project, preferred_element_type=F32)
    grad_tokens = (grad_hidden + norm_back(normed_one, inverse_one, grad_normed)).astype(BF16)
    return (grad_tokens, attn_grad)


def solution(mesh):
    fine = Mesh(mesh.devices.reshape(SIZES), AXES)
    rows = P(AXES, None)
    in_specs = (
        rows,
        P(DP, None),
        rows,
        rows,
        P(EX, None, None, DP),
        P(EX, DP, None),
        rows,
    )
    return jax.shard_map(
        per_device, mesh=fine, in_specs=in_specs, out_specs=(rows, rows), check_vma=False
    )
```

```python
import jax
import jax.numpy as jnp
from jax import lax
from jax.experimental import pallas as pl
from jax.experimental.pallas import tpu as pltpu
from jax.sharding import Mesh, PartitionSpec as P

EPSILON = 1e-05
MASKED = -1e30
AXES = ("z", "yh", "x", "yl", "c")
DP = ("z", "yh")
EX = ("x", "yl", "c")
CHIPS = ("z", "yh", "x", "yl")
SIZES = (4, 2, 4, 2, 2)
EXPERTS = 16
N_DP = 8
CAP = 10
MAIN = 8
HEADS = 2
HALF = 96
PADDED = 768
F32 = jnp.float32
BF16 = jnp.bfloat16


def layer_norm(values):
    widened = values.astype(F32)
    center = widened - jnp.mean(widened, axis=-1, keepdims=True)
    inverse = lax.rsqrt(jnp.mean(center * center, axis=-1, keepdims=True) + EPSILON)
    return (center * inverse, inverse)


def norm_back(normed, inverse, upstream):
    mean_grad = jnp.mean(upstream, axis=-1, keepdims=True)
    mean_proj = jnp.mean(upstream * normed, axis=-1, keepdims=True)
    return inverse * (upstream - mean_grad - normed * mean_proj)


def contract(first_op, second_op, first_dim, second_dim):
    return lax.dot_general(
        first_op,
        second_op,
        (((first_dim,), (second_dim,)), ((), ())),
        preferred_element_type=F32,
    )


def swap(values, axis):
    return lax.ppermute(values, axis, [(0, 1), (1, 0)])


def along_z(values, shift):
    return lax.ppermute(values, "z", [(i, (i + shift) % 4) for i in range(4)])


def exchange(blocks, axes):
    return lax.all_to_all(blocks, axes, split_axis=0, concat_axis=0, tiled=True)


def after(value, *earlier):
    return lax.optimization_barrier((value,) + earlier)[0]


def add_round(first, *others):
    total = first.astype(F32)
    for other in others:
        total = total + other.astype(F32)
    return total.astype(BF16)


def slot_matrix(expert_ids, seq_len):
    flat = expert_ids.reshape(-1)
    one_hot = (flat[:, None] == jnp.arange(EXPERTS, dtype=jnp.int32)[None, :]).astype(F32)
    rows = jnp.arange(seq_len)
    earlier = (rows[:, None] > rows[None, :]).astype(F32)
    before = jnp.dot(earlier, one_hot, preferred_element_type=F32)
    position = jnp.sum(before * one_hot, axis=1).astype(jnp.int32)
    rest = CAP - MAIN
    target = jnp.where(
        position < MAIN, flat * MAIN + position, EXPERTS * MAIN + flat * rest + position - MAIN
    )
    return (jnp.arange(EXPERTS * CAP, dtype=jnp.int32)[:, None] == target[None, :]).astype(BF16)


def place_kernel(places, piece, at_ref, *refs):
    block_refs, out_ref, sems = refs[: len(places)], refs[-2], refs[-1]
    copies = []
    number = 0
    for ref, parts in zip(block_refs, places):
        for i, (s, r, half) in enumerate(parts):
            z = lax.rem(at_ref[0] - s + 4, 4)
            yh = lax.rem(at_ref[1] + r, 2)
            copy = pltpu.make_async_copy(
                ref.at[pl.ds(i * piece, piece)], out_ref.at[z * 2 + yh, pl.ds(half * piece, piece)], sems.at[number]
            )
            copy.start()
            copies.append(copy)
            number += 1
    for copy in copies:
        copy.wait()


def gather_params(attn_param, earlier, normed):
    rows, head_dim = attn_param.shape
    half = rows // 2
    piece = half // 2
    core = lax.axis_index("c")
    own = lax.dynamic_slice_in_dim(attn_param, core * half, half, 0)
    first, second = own[:piece], own[piece:]
    around = [along_z(first, s) for s in (1, 3, 2)]
    own_y = swap(own, "yh")
    pair = after(jnp.concatenate([second, own_y[piece:]], axis=0), around[0], around[1])
    normed = swap(normed, "c")
    earlier = after(earlier, own_y, normed, *around)
    around_y = [swap(block, "yh") for block in around]
    pairs = [along_z(pair, s) for s in (1, 3, 2)]
    blocks = [own, own_y] + around + around_y + pairs
    places = (
        [[(0, 0, 0), (0, 0, 1)], [(0, 1, 0), (0, 1, 1)]]
        + [[(s, 0, 0)] for s in (1, 3, 2)]
        + [[(s, 1, 0)] for s in (1, 3, 2)]
        + [[(s, 0, 1), (s, 1, 1)] for s in (1, 3, 2)]
    )
    spread = spread_near(earlier, *around_y)
    at = jnp.stack([lax.axis_index("z"), lax.axis_index("yh")]).astype(jnp.int32)
    at = after(at, *spread[1:4])
    anywhere = pl.BlockSpec(memory_space=pl.ANY)
    own = pl.pallas_call(
        lambda *refs: place_kernel(places, piece, *refs),
        out_shape=jax.ShapeDtypeStruct((N_DP, half, head_dim), BF16),
        in_specs=[pl.BlockSpec(memory_space=pltpu.SMEM)] + [anywhere] * len(blocks),
        out_specs=pl.BlockSpec(memory_space=pltpu.VMEM),
        scratch_shapes=[pltpu.SemaphoreType.DMA((16,))],
        compiler_params=pltpu.CompilerParams(vmem_limit_bytes=60 * 1024 * 1024),
    )(at, *blocks)
    other = swap(own, "c")
    first = jnp.where(core == 0, own, other)
    second = jnp.where(core == 0, other, own)
    return jnp.stack([first, second], axis=1).reshape(N_DP * rows, head_dim), spread, normed


def between_experts(rows):
    features = rows.shape[1]
    cut = EXPERTS * MAIN
    extra = rows[cut:].reshape(cut, -1)
    packed = jnp.concatenate([rows[:cut], extra], axis=1)
    width = packed.shape[1]
    packed = exchange(packed.reshape(EXPERTS, MAIN, width), EX).reshape(cut, width)
    extra = packed[:, features:].reshape(-1, features)
    return packed[:, :features], extra


def spread_near(own, *earlier):
    one = own[:HALF]
    own_y = swap(after(own, *earlier) if earlier else own, "yh")
    return [own, own_y] + [along_z(one, s) for s in (1, 3, 2)]


def spread_far(near, *earlier):
    own, own_y, near_z, far_z, across = near
    pair = after(jnp.concatenate([own[HALF:], own_y[HALF:]], axis=0), near_z, far_z)
    near_z = after(near_z, *earlier) if earlier else near_z
    first = [swap(block, "yh") for block in (near_z, far_z, across)]
    return first + [along_z(pair, s) for s in (1, 3, 2)]


def collect(near, far):
    kept, one_y, two_y, *one_z = near
    early = [along_z(block, -s) for block, s in zip(one_z, (1, 3, 2))]
    early_y = swap(two_y, "yh")
    *one_yz, two_z, two_yz = far
    (*one_yz, two_yz), early, early_y = lax.optimization_barrier(([*one_yz, two_yz], early, early_y))
    late = [along_z(block, -s) for block, s in zip(one_yz, (1, 3, 2))]
    swapped = swap(two_yz, "yh")
    across = swap(add_round(one_y, *late), "yh")
    pairs = add_round(two_z, swapped)
    rest = kept.shape[0] - HALF
    back = [along_z(pairs[i * rest : (i + 1) * rest], -s) for i, s in enumerate((1, 3, 2))]
    one = add_round(kept[:HALF], across, *early)
    two = add_round(kept[HALF:], early_y, *back)
    return jnp.concatenate([one, two], axis=0)


def load(source, target, sem):
    copy = pltpu.make_async_copy(source, target, sem)
    copy.start()
    return copy


def act_kernel(counts, *refs):
    count = len(counts)
    cot_refs, outer_ref, out_ref = refs[:count], refs[count], refs[count + 1]
    cot, outer_map, row_sem, map_sem = refs[count + 2 :]
    hidden, features = outer_ref.shape
    copies = [load(outer_ref, outer_map.at[pl.ds(0, hidden)], map_sem.at[0])]
    for i, ref in enumerate(cot_refs):
        copies.append(load(ref, cot.at[pl.ds(sum(counts[:i]), counts[i])], row_sem.at[i]))
    outer_map[pl.ds(hidden, PADDED - hidden)] = jnp.zeros((PADDED - hidden, features), BF16)
    for copy in copies:
        copy.wait()
    tall = sum(counts) // 2

    @pl.loop(0, 2)
    def _(step):
        here = pl.ds(pl.multiple_of(step * tall, 16), tall)
        out_ref[here] = contract(cot[here], outer_map[...], 1, 1).astype(BF16)


def act_grads(cot_blocks, outer):
    counts = [block.shape[0] for block in cot_blocks]
    features = outer.shape[1]
    total = sum(counts)
    anywhere = pl.BlockSpec(memory_space=pl.ANY)
    return pl.pallas_call(
        lambda *refs: act_kernel(counts, *refs),
        out_shape=jax.ShapeDtypeStruct((total, PADDED), BF16),
        in_specs=[anywhere] * (len(counts) + 1),
        out_specs=pl.BlockSpec(memory_space=pltpu.VMEM),
        scratch_shapes=[
            pltpu.VMEM((total, features), BF16),
            pltpu.VMEM((PADDED, features), BF16),
            pltpu.SemaphoreType.DMA((len(counts),)),
            pltpu.SemaphoreType.DMA((1,)),
        ],
        compiler_params=pltpu.CompilerParams(vmem_limit_bytes=60 * 1024 * 1024),
        cost_estimate=pl.CostEstimate(
            flops=2 * total * features * PADDED,
            bytes_accessed=2 * (total + PADDED) * features,
            transcendentals=0,
        ),
    )(*cot_blocks, outer)


def expert_kernel(counts, pieces_out, tall, *refs):
    count = len(counts)
    outs = len(pieces_out)
    normed_refs = refs[:count]
    act_ref, inner_ref = refs[count : count + 2]
    out_refs = refs[count + 2 : count + 2 + outs]
    (normed, acts, gate_map, up_map, grad_gate, grad_up, result, row_sem, act_sem, map_sem, out_sem) = refs[
        count + 2 + outs :
    ]
    _, hidden, features = inner_ref.shape
    pieces = [(0, 256), (256, 256), (512, hidden - 512)]
    rows_in = [
        load(ref, normed.at[pl.ds(sum(counts[:i]), counts[i])], row_sem.at[i])
        for i, ref in enumerate(normed_refs)
    ]
    maps_in = []
    for i, (start, size) in enumerate(pieces):
        at = pl.ds(start, size)
        maps_in.append(
            [
                load(inner_ref.at[0, at], gate_map.at[at], map_sem.at[0, i]),
                load(inner_ref.at[1, at], up_map.at[at], map_sem.at[1, i]),
            ]
        )
        if i == 0:
            rows_in.append(load(act_ref, acts, act_sem.at[0]))
    blank = jnp.zeros((PADDED - hidden, features), BF16)
    for ref in (gate_map, up_map):
        ref[pl.ds(hidden, PADDED - hidden)] = blank
    for copy in rows_in:
        copy.wait()
    steps = sum(counts) // tall

    for i in range(len(pieces)):
        for copy in maps_in[i]:
            copy.wait()
        at = pl.ds(i * 256, 256)

        @pl.loop(0, steps)
        def _(step):
            here = pl.ds(pl.multiple_of(step * tall, 16), tall)
            gate_part = contract(normed[here], gate_map[at], 1, 1)
            up_part = contract(normed[here], up_map[at], 1, 1)
            squash = 1.0 / (1.0 + jnp.exp(-gate_part))
            scaled = acts[here, at].astype(F32) * squash
            grad_gate[here, at] = (scaled * up_part * (1.0 + gate_part * (1.0 - squash))).astype(BF16)
            grad_up[here, at] = (scaled * gate_part).astype(BF16)

    wide = 512
    copies = []
    for n in range(features // wide):
        lanes = pl.ds(n * wide, wide)

        @pl.loop(0, steps)
        def _(step):
            here = pl.ds(pl.multiple_of(step * tall, 16), tall)
            result[here, lanes] = (
                contract(grad_gate[here], gate_map[:, lanes], 1, 0)
                + contract(grad_up[here], up_map[:, lanes], 1, 0)
            ).astype(BF16)

        number = 0
        for ref, parts in zip(out_refs, pieces_out):
            at = 0
            for start, size in parts:
                copies.append(
                    load(
                        result.at[pl.ds(start, size), lanes],
                        ref.at[pl.ds(at, size), lanes],
                        out_sem.at[n, number],
                    )
                )
                at += size
                number += 1
    for copy in copies:
        copy.wait()


def experts(normed_blocks, acts, inner, pieces_out, tall):
    counts = [block.shape[0] for block in normed_blocks]
    features = normed_blocks[0].shape[1]
    total = sum(counts)
    anywhere = pl.BlockSpec(memory_space=pl.ANY)
    return pl.pallas_call(
        lambda *refs: expert_kernel(counts, pieces_out, tall, *refs),
        out_shape=[
            jax.ShapeDtypeStruct((sum(size for _, size in parts), features), BF16) for parts in pieces_out
        ],
        in_specs=[anywhere] * (len(counts) + 2),
        out_specs=[anywhere] * len(pieces_out),
        scratch_shapes=[
            pltpu.VMEM((total, features), BF16),
            pltpu.VMEM((total, PADDED), BF16),
            pltpu.VMEM((PADDED, features), BF16),
            pltpu.VMEM((PADDED, features), BF16),
            pltpu.VMEM((total, PADDED), BF16),
            pltpu.VMEM((total, PADDED), BF16),
            pltpu.VMEM((total, features), BF16),
            pltpu.SemaphoreType.DMA((len(counts),)),
            pltpu.SemaphoreType.DMA((1,)),
            pltpu.SemaphoreType.DMA((2, 3)),
            pltpu.SemaphoreType.DMA((features // 512, sum(len(parts) for parts in pieces_out))),
        ],
        compiler_params=pltpu.CompilerParams(vmem_limit_bytes=60 * 1024 * 1024),
        cost_estimate=pl.CostEstimate(
            flops=8 * total * features * PADDED,
            bytes_accessed=4 * total * features + 4 * PADDED * features,
            transcendentals=total * PADDED,
        ),
    )(*normed_blocks, acts, inner)


def param_kernel(scale, head_dim, core_ref, normed_ref, hidden_ref, grads_ref, out_ref, terms):
    features = normed_ref.shape[1]
    tile = 1024
    for block in range(6):
        left_ref = normed_ref if block < 4 else hidden_ref
        right = grads_ref[:, block * head_dim : (block + 1) * head_dim]
        for start in range(0, features, tile):
            part = contract(left_ref[:, start : start + tile], right, 0, 0) * scale
            terms[pl.ds(block * features + start, tile)] = part.astype(BF16)
    core = core_ref[0]

    @pl.loop(0, out_ref.shape[0])
    def _(group):
        size = out_ref.shape[1]
        out_ref[group] = terms[pl.ds(pl.multiple_of((2 * group + core) * size, 16), size)]


def param_terms(core, normed, hidden, grads, scale, head_dim):
    features = normed.shape[1]
    rows = 6 * features
    whole = pl.BlockSpec(memory_space=pltpu.VMEM)
    return pl.pallas_call(
        lambda *refs: param_kernel(scale, head_dim, *refs),
        out_shape=jax.ShapeDtypeStruct((64, rows // 128, head_dim), BF16),
        in_specs=[pl.BlockSpec(memory_space=pltpu.SMEM)] + [whole] * 3,
        out_specs=whole,
        scratch_shapes=[pltpu.VMEM((rows, head_dim), BF16)],
        compiler_params=pltpu.CompilerParams(vmem_limit_bytes=40 * 1024 * 1024),
        cost_estimate=pl.CostEstimate(
            flops=2 * rows * head_dim * normed.shape[0], bytes_accessed=8 * 1024 * 1024, transcendentals=0
        ),
    )(core, normed, hidden, grads)


def per_device(tokens, attn_param, expert_ids, gate_score, w_in, w_out, cotangent):
    seq_len, features = tokens.shape
    head_dim = attn_param.shape[1]
    score_scale = head_dim ** (-0.5)
    devices = N_DP * EXPERTS
    slots = slot_matrix(expert_ids, seq_len)
    inner = jnp.transpose(w_in[0], (1, 2, 0))
    outer = w_out[0]

    cot_main, cot_extra = between_experts(contract(slots, cotangent, 1, 0).astype(BF16))
    cot_rows = jnp.concatenate([cot_main, cot_extra], axis=0)
    normed_one, inverse_one = layer_norm(tokens)
    normed_one_b = normed_one.astype(BF16)
    packed, cot_near, normed_other = gather_params(attn_param, cot_rows, normed_one_b)
    cot_far = spread_far(cot_near)

    normed_both = jnp.concatenate([normed_one_b, normed_other], axis=0)
    blocks = packed.reshape(2 * HEADS + 2, features, head_dim)
    project = blocks[: HEADS + 2]
    out_blocks = blocks[HEADS + 2 :]
    projected = jnp.einsum(
        "td,jdc->tjc", normed_one_b, project, preferred_element_type=F32
    ).astype(BF16)
    queries = projected[:, :HEADS]
    key_rows = projected[:, HEADS]
    value_rows = projected[:, HEADS + 1]
    scores = jnp.einsum("qhc,kc->hqk", queries, key_rows, preferred_element_type=F32) * score_scale
    causal = lax.broadcasted_iota(jnp.int32, (seq_len, seq_len), 0) >= lax.broadcasted_iota(
        jnp.int32, (seq_len, seq_len), 1
    )
    scores = jnp.where(causal[None], scores, MASKED)
    row_max = jnp.max(scores, axis=2, keepdims=True)
    raised = jnp.exp(scores - row_max)
    attention = raised / jnp.sum(raised, axis=2, keepdims=True)
    attention_b = attention.astype(BF16)
    context = jnp.einsum(
        "hqk,kc->qhc", attention_b, value_rows, preferred_element_type=F32
    ).astype(BF16)
    context_flat = context.reshape(seq_len, HEADS * head_dim)
    attn_out = jnp.einsum("thc,hdc->td", context, out_blocks, preferred_element_type=F32)
    residual = (tokens.astype(F32) + attn_out).astype(BF16)
    normed_two, inverse_two = layer_norm(residual)
    normed_two_b = after(normed_two.astype(BF16), cot_near[4], cot_far[0], cot_far[1], cot_far[3], cot_far[4])
    main, extra = between_experts(contract(slots, normed_two_b, 1, 0).astype(BF16))
    near_acts = act_grads(cot_near, outer)
    far_acts = act_grads(cot_far, outer)
    near = spread_near(after(jnp.concatenate([main, extra], axis=0), near_acts, cot_far[5]))
    h = HALF
    whole = EXPERTS * CAP
    rest = whole - h
    near_rows = experts(
        near,
        near_acts,
        inner,
        [[(0, whole)], [(whole, h)], [(whole + h, rest)]] + [[(2 * whole + i * h, h)] for i in range(3)],
        2 * whole + 3 * h,
    )
    far = spread_far(near, far_acts)
    far[0] = after(far[0], near_rows[0])
    far_rows = experts(
        far,
        far_acts,
        inner,
        [[(i * h, h)] for i in range(3)]
        + [[(3 * h + (2 * i + r) * rest, rest) for i in range(3)] for r in (0, 1)],
        (h + 2 * rest) * 3,
    )
    back_main, back_extra = between_experts(collect(near_rows, far_rows))
    cut = EXPERTS * MAIN
    back_rows = contract(slots[:cut], back_main, 0, 0) + contract(slots[cut:], back_extra, 0, 0)
    moe_grad = gate_score * back_rows
    grad_hidden = cotangent.astype(F32) + norm_back(normed_two, inverse_two, moe_grad)
    grad_hidden_b = grad_hidden.astype(BF16)
    hidden_both = jnp.concatenate([grad_hidden_b, swap(grad_hidden_b, "c")], axis=0)
    grad_context = jnp.einsum(
        "td,hdc->thc", grad_hidden_b, out_blocks, preferred_element_type=F32
    )
    grad_context_b = grad_context.astype(BF16)
    grad_attention = jnp.einsum(
        "qhc,kc->hqk", grad_context_b, value_rows, preferred_element_type=F32
    )
    grad_value = jnp.einsum("hqk,qhc->kc", attention_b, grad_context_b, preferred_element_type=F32)
    grad_scores = (
        attention
        * (grad_attention - jnp.sum(grad_attention * attention, axis=2, keepdims=True))
        * score_scale
    )
    grad_scores_b = grad_scores.astype(BF16)
    grad_query = jnp.einsum("hqk,kc->qhc", grad_scores_b, key_rows, preferred_element_type=F32)
    grad_key = jnp.einsum("hqk,qhc->kc", grad_scores_b, queries, preferred_element_type=F32)
    grad_qkv = jnp.concatenate([grad_query, grad_key[:, None], grad_value[:, None]], axis=1).astype(BF16)
    grads_flat = jnp.concatenate([grad_qkv.reshape(seq_len, (HEADS + 2) * head_dim), context_flat], axis=1)
    grads_both = jnp.concatenate([grads_flat, swap(grads_flat, "c")], axis=0)
    core = lax.axis_index("c").astype(jnp.int32).reshape(1)
    terms = param_terms(
        core, normed_both, hidden_both, grads_both, (seq_len * devices) ** (-0.5), head_dim
    )
    attn_grad = jnp.sum(exchange(terms, CHIPS).astype(F32), axis=0)
    grad_normed = jnp.einsum("tjc,jdc->td", grad_qkv, project, preferred_element_type=F32)
    grad_tokens = (grad_hidden + norm_back(normed_one, inverse_one, grad_normed)).astype(BF16)
    return (grad_tokens, attn_grad)


def solution(mesh):
    fine = Mesh(mesh.devices.reshape(SIZES), AXES)
    rows = P(AXES, None)
    in_specs = (
        rows,
        P(DP, None),
        rows,
        rows,
        P(EX, None, None, DP),
        P(EX, DP, None),
        rows,
    )
    return jax.shard_map(
        per_device, mesh=fine, in_specs=in_specs, out_specs=(rows, rows), check_vma=False
    )
```
